32 devices in a mesh: seq: 16 (over z, y, core), rows: 2 (over x).
Axes of the slice: x: 2, y: 2, z: 4, core: 2. Of those that a mesh axis runs over, the one named last changes fastest.
Arguments:
- patches: bfloat16 [16, 1536, 768], P('seq', 'rows'), may hold values from -6 to 6
- lengths: int32 [16, 4], P('seq'), may hold values from 0 to 576, as said below
- w_qkv: bfloat16 [768, 2304], P('seq'), may hold values from -0.21875 to 0.21875
- qkv_bias: bfloat16 [2304], replicated, may hold values from -3 to 3
- w_out: bfloat16 [768, 768], P('seq'), may hold values from -2 to 2
- out_bias: bfloat16 [768], replicated, may hold values from -3 to 3
- w_up: bfloat16 [768, 3072], P('seq'), may hold values from -0.21875 to 0.21875
- up_bias: bfloat16 [3072], replicated, may hold values from -3 to 3
- w_down: bfloat16 [3072, 768], P('seq'), may hold values from -0.109375 to 0.109375
- down_bias: bfloat16 [768], replicated, may hold values from -3 to 3
- gain_one: bfloat16 [768], replicated, may hold values from 0.3 to 2.8
- shift_one: bfloat16 [768], replicated, may hold values from -3 to 3
- gain_two: bfloat16 [768], replicated, may hold values from 0.3 to 2.8
- shift_two: bfloat16 [768], replicated, may hold values from -3 to 3
- rope_freqs: float32 [2, 12, 32], replicated, may hold values from -0.5 to 0.5
- cotangent: bfloat16 [16, 1536, 768], P('seq', 'rows'), may hold values from -6 to 6
Outputs:
- hidden_out: bfloat16 [16, 1536, 768], P('seq', 'rows')
- patch_grad: float32 [16, 1536, 768], P('seq', 'rows')
- grad_w_qkv: float32 [768, 2304], P('seq')
- grad_qkv_bias: float32 [2304], replicated
- grad_w_out: float32 [768, 768], P('seq')
- grad_out_bias: float32 [768], replicated
- grad_w_up: float32 [768, 3072], P('seq')
- grad_up_bias: float32 [3072], replicated
- grad_w_down: float32 [3072, 768], P('seq')
- grad_down_bias: float32 [768], replicated
- grad_gain_one: float32 [768], replicated
- grad_shift_one: float32 [768], replicated
- grad_gain_two: float32 [768], replicated
- grad_shift_two: float32 [768], replicated
- grad_freqs: float32 [2, 12, 32], replicated
- norm_main: float32 [], replicated
- norm_freqs: float32 [], replicated
The draws below stay inside these ranges and needn't reach their ends.
Inputs may be any that keep to these rules, and one draw needn't show every extreme that they name: `lengths`: each entry is 0 or the patch count of a square image of side 14, 20 or 24; in each row the nonzero entries come first and add up to at most 1536; positions past their sum are padding.
All inputs are finite; a program needn't handle non-finite values.
Results may differ from the reference program's by a relative error of at most 0.012.
The reference program's roundings to bfloat16 on the way count: a program that leaves them out, or rounds other values in their place, can miss the bound.
Values may be sent and summed in bfloat16 or wider, within the bound.
No kernel may reach another device: no remote copies, remote signals or barrier semaphores. Data moves between devices by JAX's collectives and lax.ppermute only.
A program may use at most 192 MiB of HBM per device.

```python
import jax
import jax.numpy as jnp
from jax import lax

D = 768
H = 12
DH = 64
FF = 3072
SEQ_LEN = 1536
IMGS = 4
SIDE_S = 14
SIDE_M = 20
SIDE_L = 24
SEQS = 16


def draw_lengths(key, part):
    key = jax.random.fold_in(key, 5)
    picked = jax.random.randint(key, (SEQS, IMGS), 0, 3)
    image_areas = jnp.where(picked == 0, SIDE_S * SIDE_S, jnp.where(picked == 1, SIDE_M * SIDE_M, SIDE_L * SIDE_L)).astype(jnp.int32)
    first_row = jnp.arange(SEQS, dtype=jnp.int32)[:, None] == 0
    image_areas = jnp.where(first_row, SIDE_L * SIDE_L, image_areas).astype(jnp.int32)
    filled = jnp.cumsum(image_areas, axis=1)
    return jnp.where(filled <= SEQ_LEN, image_areas, 0).astype(jnp.int32)


def ramp_gain(key, start, finish):
    place = jnp.arange(D, dtype=jnp.float32) / (D - 1)
    trend = start * jnp.exp(place * jnp.log(finish / start))
    rough = jax.random.uniform(key, (D,), jnp.float32, 0.85, 1.15)
    return trend * rough


def draw_gain_one(key, part):
    key = jax.random.fold_in(key, 11)
    return ramp_gain(key, 0.5, 2.0).astype(jnp.bfloat16)


def draw_gain_two(key, part):
    key = jax.random.fold_in(key, 13)
    return ramp_gain(key, 0.5, 2.0).astype(jnp.bfloat16)


def block_scale(own_key, extent, pieces, low, high):
    def one(dim, shards_of):
        draws = jax.random.uniform(jax.random.fold_in(jax.random.fold_in(own_key, 6), dim), (shards_of,), jnp.float32, low / len(pieces), high / len(pieces))
        return jnp.repeat(jnp.exp(draws), extent[dim] // shards_of).reshape((-1,) + (1,) * (len(extent) - dim - 1))

    level = one(*pieces[0])
    for cut in pieces[1:]:
        level = level * one(*cut)
    return level


def gaussian(stream_key, shape, scale, limit, cuts=(), kind=jnp.bfloat16):
    array = scale * jax.random.normal(stream_key, shape, jnp.float32)
    if cuts:
        array = array * block_scale(stream_key, shape, cuts, -0.22, 0.18)
    return jnp.clip(array, -limit, limit).astype(kind)


def setup_inputs(seed: int = 0) -> dict:
    streams_of = jax.random.split(jax.random.key(seed), 17)
    patches = gaussian(streams_of[0], (SEQS, SEQ_LEN, D), 1.0, 6.0, ((0, 16), (1, 2)))
    lengths = draw_lengths(jax.random.fold_in(streams_of[16], 71), 0)
    w_qkv = gaussian(streams_of[2], (D, 3 * D), D ** -0.5, 0.21875, ((0, 16),))
    qkv_bias = gaussian(streams_of[3], (3 * D,), 0.5, 3.0)
    w_out = gaussian(streams_of[4], (D, D), (D * 4 // (SIDE_M * SIDE_M)) ** -0.5, 2.0, ((0, 16),))
    out_bias = gaussian(streams_of[5], (D,), 0.5, 3.0)
    w_up = gaussian(streams_of[6], (D, FF), D ** -0.5, 0.21875, ((0, 16),))
    up_bias = gaussian(streams_of[7], (FF,), 0.5, 3.0)
    w_down = gaussian(streams_of[8], (FF, D), FF ** -0.5, 0.109375, ((0, 16),))
    down_bias = gaussian(streams_of[9], (D,), 0.5, 3.0)
    gain_one = draw_gain_one(jax.random.fold_in(streams_of[16], 71), 0)
    shift_one = gaussian(streams_of[11], (D,), 0.5, 3.0)
    gain_two = draw_gain_two(jax.random.fold_in(streams_of[16], 71), 0)
    shift_two = gaussian(streams_of[13], (D,), 0.5, 3.0)
    rope_freqs = jnp.clip(jax.random.uniform(streams_of[14], (2, H, DH // 2), jnp.float32, -0.5, 0.5), -0.5, 0.5)
    cotangent = gaussian(streams_of[15], (SEQS, SEQ_LEN, D), 1.0, 6.0, ((0, 16), (1, 2)))
    return {"patches": patches, "lengths": lengths, "w_qkv": w_qkv, "qkv_bias": qkv_bias, "w_out": w_out, "out_bias": out_bias, "w_up": w_up, "up_bias": up_bias, "w_down": w_down, "down_bias": down_bias, "gain_one": gain_one, "shift_one": shift_one, "gain_two": gain_two, "shift_two": shift_two, "rope_freqs": rope_freqs, "cotangent": cotangent}


epsilon = 1e-06
precise = lax.Precision.HIGHEST

@jax.custom_vjp
def low(v):
    return lax.optimization_barrier(v.astype(jnp.bfloat16)).astype(jnp.float32)

@jax.custom_vjp
def low_back(v):
    return v

def low_keep(v):
    return (low(v), None)

def low_pass(kept, grad):
    return (grad,)

def back_keep(v):
    return (v, None)

def back_low(kept, grad):
    return (low(grad),)
low.defvjp(low_keep, low_pass)
low_back.defvjp(back_keep, back_low)

def image_layout(lengths, positions):
    slot_count = lengths.shape[0]
    image_ends = jnp.cumsum(lengths).astype(jnp.int32)
    image_starts = (image_ends - lengths).astype(jnp.int32)
    inside = (positions[:, None] >= image_starts[None, :]) & (positions[:, None] < image_ends[None, :])
    slot_ids = jnp.arange(slot_count, dtype=jnp.int32)
    present = jnp.any(inside, axis=1)
    block_ids = lax.optimization_barrier(jnp.sum(jnp.where(inside, slot_ids[None, :], 0), axis=1)).astype(jnp.int32) + jnp.where(present, 0, slot_count).astype(jnp.int32)
    image_side = jnp.where(lengths == SIDE_S * SIDE_S, SIDE_S, jnp.where(lengths == SIDE_M * SIDE_M, SIDE_M, SIDE_L)).astype(jnp.int32)
    offset = (positions - lax.optimization_barrier(jnp.sum(jnp.where(inside, image_starts[None, :], 0), axis=1))).astype(jnp.int32)
    image_width = jnp.maximum(lax.optimization_barrier(jnp.sum(jnp.where(inside, image_side[None, :], 0), axis=1)), 1).astype(jnp.int32)
    row_pos = jnp.where(present, offset // image_width, 0).astype(jnp.int32)
    col_pos = jnp.where(present, offset % image_width, 0).astype(jnp.int32)
    return (block_ids, row_pos, col_pos)

def layer_norm(features, gain_in, shift_in):
    average = lax.optimization_barrier(jnp.mean(features, axis=-1, keepdims=True))
    centered = features - average
    variance = lax.optimization_barrier(jnp.mean(centered * centered, axis=-1, keepdims=True))
    return centered * lax.rsqrt(variance + epsilon) * gain_in + shift_in

def rotate(vectors, angles):
    half_dim = vectors.shape[-1] // 2
    leading = vectors[..., :half_dim]
    trailing = vectors[..., half_dim:]
    cosines = jnp.cos(angles)
    sines = jnp.sin(angles)
    return jnp.concatenate([leading * cosines - trailing * sines, leading * sines + trailing * cosines], axis=-1)

def rotate_pair(queries, keys_in, rope_freqs, row_pos, col_pos):
    angles = row_pos[:, None, None] * rope_freqs[0] + col_pos[:, None, None] * rope_freqs[1]
    return (rotate(queries, angles), rotate(keys_in, angles))

def layer_forward(features, w_qkv, qkv_bias, w_out, out_bias, w_up, up_bias, w_down, down_bias, gain_one, shift_one, gain_two, shift_two, rope_freqs, block_ids, row_pos, col_pos):
    length = features.shape[0]
    normed_one = low(layer_norm(features, gain_one, shift_one))
    projected = low_back(jnp.dot(normed_one, w_qkv, precision=precise) + qkv_bias)
    query_pre = projected[:, :D].reshape(length, H, DH)
    key_pre = projected[:, D:2 * D].reshape(length, H, DH)
    query_rot, key_rot = rotate_pair(query_pre, key_pre, rope_freqs, row_pos, col_pos)
    queries = low(query_rot)
    keys_low = low(key_rot)
    values_low = low(projected[:, 2 * D:]).reshape(length, H, DH)
    allowed = block_ids[:, None] == block_ids[None, :]

    def one_head(operands):
        head_query, head_key, head_value = operands
        scores = low_back(jnp.dot(head_query, head_key.T, precision=precise) * 0.125)
        scores = jnp.where(allowed, scores, -1e+30)
        attention = jax.nn.softmax(scores, axis=-1)
        return jnp.dot(low(attention), head_value, precision=precise)
    per_head = lax.map(jax.checkpoint(one_head), (queries.transpose(1, 0, 2), keys_low.transpose(1, 0, 2), values_low.transpose(1, 0, 2)))
    attended = low(low_back(per_head.transpose(1, 0, 2).reshape(length, D)))
    branch = low_back(jnp.dot(attended, w_out, precision=precise) + out_bias)
    residual_one = features + branch
    normed_two = low(layer_norm(residual_one, gain_two, shift_two))
    up_pre = low_back(jnp.dot(normed_two, w_up, precision=precise) + up_bias)
    activated = low(jax.nn.gelu(up_pre, approximate=False))
    return residual_one + jnp.dot(activated, w_down, precision=precise) + down_bias

def reference(patches, lengths, w_qkv, qkv_bias, w_out, out_bias, w_up, up_bias, w_down, down_bias, gain_one, shift_one, gain_two, shift_two, rope_freqs, cotangent):
    params = tuple((param_in.astype(jnp.float32) for param_in in (w_qkv, qkv_bias, w_out, out_bias, w_up, up_bias, w_down, down_bias, gain_one, shift_one, gain_two, shift_two, rope_freqs)))
    positions = jnp.arange(SEQ_LEN, dtype=jnp.int32)

    def one_sequence(carry, seq_item):
        seq_patches, seq_lengths, seq_cot = seq_item
        block_ids, row_pos, col_pos = image_layout(seq_lengths, positions)
        row_float = row_pos.astype(jnp.float32)
        col_float = col_pos.astype(jnp.float32)

        def forward_fn(features, *weights):
            return layer_forward(features, *weights, block_ids, row_float, col_float)
        result, pullback = jax.vjp(forward_fn, seq_patches.astype(jnp.float32), *params)
        gradients = pullback(seq_cot.astype(jnp.float32))
        summed = tuple((running + piece_grad for running, piece_grad in zip(carry, gradients[1:])))
        return (summed, (result.astype(jnp.bfloat16), gradients[0]))
    zeros_init = tuple((jnp.zeros(param_in.shape, jnp.float32) for param_in in params))
    grad_sums, (hidden_out, patch_grad) = lax.scan(one_sequence, zeros_init, (patches, lengths, cotangent))
    main_squares = sum((jnp.sum(grad_piece * grad_piece) for grad_piece in grad_sums[:-1]))
    norm_main = jnp.sqrt(main_squares)
    norm_freqs = jnp.sqrt(jnp.sum(grad_sums[-1] * grad_sums[-1]))
    return (hidden_out, patch_grad, grad_sums[0], grad_sums[1], grad_sums[2], grad_sums[3], grad_sums[4], grad_sums[5], grad_sums[6], grad_sums[7], grad_sums[8], grad_sums[9], grad_sums[10], grad_sums[11], grad_sums[12], norm_main, norm_freqs)
```

```python
import jax
import jax.numpy as jnp
from jax import lax
from jax.experimental import pallas as pl
from jax.experimental.pallas import tpu as pltpu
from jax.sharding import PartitionSpec as P

SIDE_S = 14
SIDE_M = 20
SIDE_L = 24
EPS = 1e-06
NEG = -1e30
HEAD = 64
PAIR = 128
TILE = 256
F32 = jnp.float32
BF16 = jnp.bfloat16
VMEM_LIMIT = 60 * 1024 * 1024


def params(**kw):
    return pltpu.CompilerParams(vmem_limit_bytes=VMEM_LIMIT, **kw)


def nn(a, b):
    return lax.dot_general(a, b, (((1,), (0,)), ((), ())), preferred_element_type=F32)


def nt(a, b):
    return lax.dot_general(a, b, (((1,), (1,)), ((), ())), preferred_element_type=F32)


def tn(a, b):
    return lax.dot_general(a, b, (((0,), (0,)), ((), ())), preferred_element_type=F32)


def layout(lengths, total, tile):
    slots = lengths.shape[0]
    ends = []
    running = jnp.int32(0)
    for s in range(slots):
        running = running + lengths[s]
        ends.append(running)
    starts = [e - lengths[s] for s, e in enumerate(ends)]
    pos = jnp.arange(total, dtype=jnp.int32)

    def place(at):
        block = jnp.full(at.shape, slots, jnp.int32)
        first = jnp.broadcast_to(running, at.shape)
        last = jnp.full(at.shape, total, jnp.int32)
        side = jnp.ones(at.shape, jnp.int32)
        for s in range(slots):
            inside = (at >= starts[s]) & (at < ends[s])
            width = jnp.where(
                lengths[s] == SIDE_S * SIDE_S,
                SIDE_S,
                jnp.where(lengths[s] == SIDE_M * SIDE_M, SIDE_M, SIDE_L),
            ).astype(jnp.int32)
            block = jnp.where(inside, s, block)
            first = jnp.where(inside, starts[s], first)
            last = jnp.where(inside, ends[s], last)
            side = jnp.where(inside, width, side)
        return block, first, last, side

    block, first, last, side = place(pos)
    present = block < slots
    offset = pos - first
    row_pos = jnp.where(present, offset // side, 0)
    col_pos = jnp.where(present, offset % side, 0)
    tiles = jnp.arange(total // tile, dtype=jnp.int32) * tile
    lo = place(tiles)[1] // tile
    hi = (place(tiles + tile - 1)[2] + tile - 1) // tile
    return block, row_pos, col_pos, lo, hi


def swap_halves(u):
    width = u.shape[-1]
    lane = lax.broadcasted_iota(jnp.int32, u.shape, 1) % HEAD
    return jnp.where(
        lane < HEAD // 2,
        pltpu.roll(u, width - HEAD // 2, 1),
        pltpu.roll(u, HEAD // 2, 1),
    )


def qkv_kernel(side_ref, own_ref, other_ref, w_ref, bias_ref, gain_ref, shift_ref, cos_ref, sin_ref, normed_ref, out_ref):
    step = pl.program_id(0)
    half = pl.num_programs(0) // 2
    width = cos_ref.shape[1]
    mine = (step // half) == side_ref[0]
    x = jnp.where(mine, own_ref[...].astype(F32), other_ref[...].astype(F32))
    mean = jnp.mean(x, axis=1, keepdims=True)
    cen = x - mean
    var = jnp.mean(cen * cen, axis=1, keepdims=True)
    normed = (cen * lax.rsqrt(var + EPS) * gain_ref[...] + shift_ref[...]).astype(BF16)
    normed_ref[...] = normed
    proj = nn(normed, w_ref[...]) + bias_ref[...]
    c = cos_ref[...]
    s = sin_ref[...]
    q = proj[:, :width]
    k = proj[:, width : 2 * width]
    q = (q * c + swap_halves(q) * s).astype(BF16)
    k = (k * c + swap_halves(k) * s).astype(BF16)
    out_ref[:, :width] = (q.astype(F32) * 0.125).astype(BF16)
    out_ref[:, width : 2 * width] = k
    out_ref[:, 2 * width :] = proj[:, 2 * width :].astype(BF16)


def qkv_call(side, own, other, w, bias, gain, shift, cos, sin):
    rows, width = own.shape
    total = 2 * rows
    cols = w.shape[1]
    per = rows // TILE
    last = per - 1
    whole = lambda i, s: (0, 0)
    return pl.pallas_call(
        qkv_kernel,
        grid_spec=pltpu.PrefetchScalarGridSpec(
            num_scalar_prefetch=1,
            grid=(total // TILE,),
            in_specs=[
                pl.BlockSpec((TILE, width), lambda i, s: (jnp.clip(i - per * s[0], 0, last), 0)),
                pl.BlockSpec((TILE, width), lambda i, s: (jnp.clip(i - per * (1 - s[0]), 0, last), 0)),
                pl.BlockSpec((width, cols), whole),
                pl.BlockSpec((1, cols), whole),
                pl.BlockSpec((1, width), whole),
                pl.BlockSpec((1, width), whole),
                pl.BlockSpec((TILE, cols // 3), lambda i, s: (i, 0)),
                pl.BlockSpec((TILE, cols // 3), lambda i, s: (i, 0)),
            ],
            out_specs=[
                pl.BlockSpec((TILE, width), lambda i, s: (i, 0)),
                pl.BlockSpec((TILE, cols), lambda i, s: (i, 0)),
            ],
        ),
        out_shape=[
            jax.ShapeDtypeStruct((total, width), BF16),
            jax.ShapeDtypeStruct((total, cols), BF16),
        ],
        compiler_params=params(),
        cost_estimate=pl.CostEstimate(flops=2 * total * width * cols, bytes_accessed=12 * 10**6, transcendentals=0),
    )(side, own, other, w, bias, gain, shift, cos, sin)


def head_lanes(shape, odd):
    lane = lax.broadcasted_iota(jnp.int32, shape, 1)
    return (lane >= HEAD) if odd else (lane < HEAD)


def attend_kernel(lo_ref, hi_ref, qkv_ref, mq_ref, mk_ref, out_ref, lse_ref, kaug, qaug, vt, scores, acc):
    step = pl.program_id(0)
    width = out_ref.shape[1]
    heads = width // HEAD
    total = qkv_ref.shape[0]

    @pl.when(step == 0)
    def _():
        mk = mk_ref[...]
        for h in range(heads):
            pair = h // 2
            k = qkv_ref[:, width + pair * PAIR : width + (pair + 1) * PAIR]
            kaug[h] = jnp.where(head_lanes(k.shape, h % 2), k, mk)
        vt[...] = qkv_ref[:, 2 * width :].T

    rows = pl.ds(pl.multiple_of(step * TILE, TILE), TILE)
    mq = mq_ref[rows, :]
    for h in range(heads):
        pair = h // 2
        q = qkv_ref[rows, pair * PAIR : (pair + 1) * PAIR]
        qaug[h] = jnp.where(head_lanes(q.shape, h % 2), q, mq)
    lo = lo_ref[step]
    hi = hi_ref[step]

    def first(kt, best):
        keys = pl.ds(pl.multiple_of(kt * TILE, TILE), TILE)
        out = []
        for h in range(heads):
            s = nt(kaug[h, keys, :], qaug[h])
            scores[h, keys, :] = s
            out.append(jnp.maximum(best[h], jnp.max(s.reshape(TILE // 8, 8, TILE), axis=0)))
        return tuple(out)

    best = lax.fori_loop(lo, hi, first, tuple(jnp.full((8, TILE), -jnp.inf, F32) for _ in range(heads)))
    best = [jnp.max(b, axis=0, keepdims=True) for b in best]
    acc[...] = jnp.zeros_like(acc)

    def second(kt, sums):
        keys = pl.ds(pl.multiple_of(kt * TILE, TILE), TILE)
        out = []
        for h in range(heads):
            p = jnp.exp(scores[h, keys, :] - best[h])
            out.append(sums[h] + jnp.sum(p.reshape(TILE // 8, 8, TILE), axis=0))
            own = slice(h * HEAD, (h + 1) * HEAD)
            acc[own, :] += nn(vt[own, keys], p.astype(BF16))
        return tuple(out)

    sums = lax.fori_loop(lo, hi, second, tuple(jnp.zeros((8, TILE), F32) for _ in range(heads)))
    lses = []
    outs = []
    for h in range(heads):
        tot = jnp.sum(sums[h], axis=0, keepdims=True)
        outs.append(acc[h * HEAD : (h + 1) * HEAD, :] / tot)
        lses.append(best[h] + jnp.log(tot))
    lses += [jnp.zeros_like(lses[0])] * (8 - heads)
    lse_ref[...] = jnp.concatenate(lses, axis=0)
    out_ref[...] = jnp.concatenate(outs, axis=0).T.astype(BF16)


def attend_call(lo, hi, qkv, mq, mk):
    total, cols = qkv.shape
    width = cols // 3
    heads = width // HEAD
    whole = lambda i, a, b: (0, 0)
    return pl.pallas_call(
        attend_kernel,
        grid_spec=pltpu.PrefetchScalarGridSpec(
            num_scalar_prefetch=2,
            grid=(total // TILE,),
            in_specs=[
                pl.BlockSpec((total, cols), whole),
                pl.BlockSpec((total, PAIR), whole),
                pl.BlockSpec((total, PAIR), whole),
            ],
            out_specs=[
                pl.BlockSpec((TILE, width), lambda i, a, b: (i, 0)),
                pl.BlockSpec((8, TILE), lambda i, a, b: (0, i)),
            ],
            scratch_shapes=[
                pltpu.VMEM((heads, total, PAIR), BF16),
                pltpu.VMEM((heads, TILE, PAIR), BF16),
                pltpu.VMEM((width, total), BF16),
                pltpu.VMEM((heads, total, TILE), F32),
                pltpu.VMEM((width, TILE), F32),
            ],
        ),
        out_shape=[
            jax.ShapeDtypeStruct((total, width), BF16),
            jax.ShapeDtypeStruct((8, total), F32),
        ],
        compiler_params=params(),
        cost_estimate=pl.CostEstimate(flops=8 * total * total * width, bytes_accessed=6 * 10**6, transcendentals=0),
    )(lo, hi, qkv, mq, mk)


def phi_parts(x):
    cdf = 0.5 * (1.0 + lax.erf(x * 0.7071067811865476))
    pdf = jnp.exp(-0.5 * x * x) * 0.3989422804014327
    return cdf, pdf


def ffn_kernel(
    att_ref, x_ref, cot_ref, wo_ref, wu_ref, wd_ref, ob_ref, ub_ref, db_ref, gain_ref, shift_ref,
    hid_ref, gres_ref, gatt_ref, gwo_ref, gwu_ref, gwd_ref, gub_ref, sums_ref,
    res, normed, acc, gacc, act, gup,
):
    step = pl.program_id(0)
    rows = x_ref.shape[0]
    chunks = [pl.ds(r, TILE) for r in range(0, rows, TILE)]

    @pl.when(step == 0)
    def _():
        for ch in chunks:
            r = x_ref[ch, :].astype(F32) + (nn(att_ref[ch, :], wo_ref[...]) + ob_ref[...])
            res[ch, :] = r
            cen = r - jnp.mean(r, axis=1, keepdims=True)
            var = jnp.mean(cen * cen, axis=1, keepdims=True)
            normed[ch, :] = (cen * lax.rsqrt(var + EPS) * gain_ref[...] + shift_ref[...]).astype(BF16)
        acc[...] = jnp.zeros_like(acc)
        gacc[...] = jnp.zeros_like(gacc)

    bias_sum = jnp.zeros((1, ub_ref.shape[1]), F32)
    for ch in chunks:
        up = nn(normed[ch, :], wu_ref[...]) + ub_ref[...]
        cdf, pdf = phi_parts(up)
        a = (up * cdf).astype(BF16)
        act[ch, :] = a
        g = (nt(cot_ref[ch, :], wd_ref[...]) * (cdf + up * pdf)).astype(BF16)
        gup[ch, :] = g
        bias_sum += jnp.sum(g.astype(F32), axis=0, keepdims=True)
        acc[ch, :] += nn(a, wd_ref[...])
        gacc[ch, :] += nt(g, wu_ref[...])
    gub_ref[...] = bias_sum
    gwd_ref[...] = tn(act[...], cot_ref[...]).astype(BF16)
    gwu_ref[...] = tn(normed[...], gup[...]).astype(BF16)

    @pl.when(step == pl.num_programs(0) - 1)
    def _():
        width = x_ref.shape[1]
        zero = jnp.zeros((1, width), F32)
        s_out, s_down, s_gain, s_shift = zero, zero, zero, zero
        gain = gain_ref[...]
        for ch in chunks:
            r = res[ch, :]
            hid_ref[ch, :] = (r + acc[ch, :] + db_ref[...]).astype(BF16)
            cen = r - jnp.mean(r, axis=1, keepdims=True)
            rs = lax.rsqrt(jnp.mean(cen * cen, axis=1, keepdims=True) + EPS)
            xh = cen * rs
            e = gacc[ch, :]
            eg = e * gain
            cot = cot_ref[ch, :].astype(F32)
            g = cot + rs * (
                eg - jnp.mean(eg, axis=1, keepdims=True) - xh * jnp.mean(eg * xh, axis=1, keepdims=True)
            )
            gres_ref[ch, :] = g
            gb = g.astype(BF16)
            act[ch, :width] = gb
            gatt_ref[ch, :] = nt(gb, wo_ref[...]).astype(BF16)
            s_out += jnp.sum(gb.astype(F32), axis=0, keepdims=True)
            s_down += jnp.sum(cot, axis=0, keepdims=True)
            s_gain += jnp.sum(e * xh, axis=0, keepdims=True)
            s_shift += jnp.sum(e, axis=0, keepdims=True)
        gwo_ref[...] = tn(att_ref[...], act[:, :width]).astype(BF16)
        sums_ref[...] = jnp.concatenate([s_out, s_down, s_gain, s_shift] + [zero] * 4, axis=0)


def ffn_call(att, x, cot, wo, wu, wd, ob, ub, db, gain, shift):
    rows, width = x.shape
    hidden = wu.shape[1]
    block = width
    whole = lambda j: (0, 0)
    one = lambda r, c: pl.BlockSpec((r, c), whole)
    return pl.pallas_call(
        ffn_kernel,
        grid=(hidden // block,),
        in_specs=[
            one(rows, width),
            one(rows, width),
            one(rows, width),
            one(width, width),
            pl.BlockSpec((width, block), lambda j: (0, j)),
            pl.BlockSpec((block, width), lambda j: (j, 0)),
            one(1, width),
            pl.BlockSpec((1, block), lambda j: (0, j)),
            one(1, width),
            one(1, width),
            one(1, width),
        ],
        out_specs=[
            one(rows, width),
            one(rows, width),
            one(rows, width),
            one(width, width),
            pl.BlockSpec((width, block), lambda j: (0, j)),
            pl.BlockSpec((block, width), lambda j: (j, 0)),
            pl.BlockSpec((1, block), lambda j: (0, j)),
            one(8, width),
        ],
        out_shape=[
            jax.ShapeDtypeStruct((rows, width), BF16),
            jax.ShapeDtypeStruct((rows, width), F32),
            jax.ShapeDtypeStruct((rows, width), BF16),
            jax.ShapeDtypeStruct((width, width), BF16),
            jax.ShapeDtypeStruct((width, hidden), BF16),
            jax.ShapeDtypeStruct((hidden, width), BF16),
            jax.ShapeDtypeStruct((1, hidden), F32),
            jax.ShapeDtypeStruct((8, width), F32),
        ],
        scratch_shapes=[
            pltpu.VMEM((rows, width), F32),
            pltpu.VMEM((rows, width), BF16),
            pltpu.VMEM((rows, width), F32),
            pltpu.VMEM((rows, width), F32),
            pltpu.VMEM((rows, block), BF16),
            pltpu.VMEM((rows, block), BF16),
        ],
        compiler_params=params(),
        cost_estimate=pl.CostEstimate(
            flops=12 * rows * width * hidden + 6 * rows * width * width,
            bytes_accessed=30 * 10**6,
            transcendentals=rows * hidden,
        ),
    )(att, x, cot, wo, wu, wd, ob, ub, db, gain, shift)


def attend_back_kernel(
    lo_ref, hi_ref, qkv_ref, do_ref, o_ref, lse_ref, mq_ref, mk_ref, cos_ref, sin_ref, pos_ref,
    gproj_ref, sums_ref, tsum_ref,
    kaug, kt_ref, qaug, qm, dom, dk, dv, dqt, delta,
):
    step = pl.program_id(0)
    width = do_ref.shape[1]
    heads = width // HEAD
    pairs = heads // 2
    total = qkv_ref.shape[0]

    @pl.when(step == 0)
    def _():
        mk = mk_ref[...]
        for h in range(heads):
            pair = h // 2
            k = qkv_ref[:, width + pair * PAIR : width + (pair + 1) * PAIR]
            kaug[h] = jnp.where(head_lanes(k.shape, h % 2), k, mk)
        kt_ref[...] = qkv_ref[:, width : 2 * width].T
        dk[...] = jnp.zeros_like(dk)
        dv[...] = jnp.zeros_like(dv)
        sums_ref[...] = jnp.zeros_like(sums_ref)
        tsum_ref[...] = jnp.zeros_like(tsum_ref)

    rows = pl.ds(pl.multiple_of(step * TILE, TILE), TILE)
    mq = mq_ref[rows, :]
    for h in range(heads):
        pair = slice((h // 2) * PAIR, (h // 2 + 1) * PAIR)
        q = qkv_ref[rows, pair]
        lanes = head_lanes(q.shape, h % 2)
        qaug[h] = jnp.where(lanes, q, mq)
        qm[h] = jnp.where(lanes, q, jnp.zeros_like(q))
        dom[h] = jnp.where(lanes, do_ref[rows, pair], jnp.zeros_like(q))
    inner = do_ref[rows, :].astype(F32) * o_ref[rows, :].astype(F32)
    pick = (
        lax.broadcasted_iota(jnp.int32, (8, width), 1) // HEAD == lax.broadcasted_iota(jnp.int32, (8, width), 0)
    ).astype(F32)
    delta[...] = lax.dot_general(
        pick, inner, (((1,), (1,)), ((), ())), precision=lax.Precision.HIGHEST, preferred_element_type=F32
    )
    dqt[...] = jnp.zeros_like(dqt)

    def body(kt, carry):
        keys = pl.ds(pl.multiple_of(kt * TILE, TILE), TILE)
        for pr in range(pairs):
            pair = slice(pr * PAIR, (pr + 1) * PAIR)
            v = qkv_ref[keys, 2 * width + pr * PAIR : 2 * width + (pr + 1) * PAIR]
            dv_new = dv[keys, pair]
            dk_new = dk[keys, pair]
            for h in (2 * pr, 2 * pr + 1):
                own = slice(h * HEAD, (h + 1) * HEAD)
                s = nt(kaug[h, keys, :], qaug[h])
                p = jnp.exp(s - lse_ref[h : h + 1, rows])
                dp = nt(v, dom[h])
                ds = (p * (dp - delta[h : h + 1, :])).astype(BF16)
                dv_new += nn(p.astype(BF16), dom[h])
                dk_new += nn(ds, qm[h])
                dqt[own, :] += nn(kt_ref[own, keys], ds)
            dv[keys, pair] = dv_new
            dk[keys, pair] = dk_new
        return carry

    lax.fori_loop(lo_ref[step], hi_ref[step], body, 0)

    def unrotate(u, c, s):
        return (u * c - swap_halves(u) * s).astype(BF16)

    def freq_sum(u, rot, at):
        w = u * swap_halves(rot)
        pos = pos_ref[at, :]
        tsum_ref[0:1, :] += jnp.sum(w * pos[:, 0:1], axis=0, keepdims=True)
        tsum_ref[1:2, :] += jnp.sum(w * pos[:, 1:2], axis=0, keepdims=True)

    dq = dqt[...].T * 0.125
    freq_sum(dq, qkv_ref[rows, :width].astype(F32) * 8.0, rows)
    gq = unrotate(dq, cos_ref[rows, :], sin_ref[rows, :])
    gproj_ref[rows, :width] = gq
    sums_ref[0:1, :width] += jnp.sum(gq.astype(F32), axis=0, keepdims=True)

    @pl.when(step == pl.num_programs(0) - 1)
    def _():
        for t in range(total // TILE):
            at = pl.ds(t * TILE, TILE)
            u = dk[at, :]
            freq_sum(u, qkv_ref[at, width : 2 * width].astype(F32), at)
            gk = unrotate(u, cos_ref[at, :], sin_ref[at, :])
            gv = dv[at, :].astype(BF16)
            gproj_ref[at, width : 2 * width] = gk
            gproj_ref[at, 2 * width :] = gv
            sums_ref[0:1, width : 2 * width] += jnp.sum(gk.astype(F32), axis=0, keepdims=True)
            sums_ref[0:1, 2 * width :] += jnp.sum(gv.astype(F32), axis=0, keepdims=True)


def attend_back_call(lo, hi, qkv, do, o, lse, mq, mk, cos, sin, pos):
    total, cols = qkv.shape
    width = cols // 3
    heads = width // HEAD
    arrays = (qkv, do, o, lse, mq, mk, cos, sin, pos)
    whole = lambda i, a, b: (0, 0)
    return pl.pallas_call(
        attend_back_kernel,
        grid_spec=pltpu.PrefetchScalarGridSpec(
            num_scalar_prefetch=2,
            grid=(total // TILE,),
            in_specs=[pl.BlockSpec(a.shape, whole) for a in arrays],
            out_specs=[
                pl.BlockSpec((total, cols), whole),
                pl.BlockSpec((8, cols), whole),
                pl.BlockSpec((8, width), whole),
            ],
            scratch_shapes=[
                pltpu.VMEM((heads, total, PAIR), BF16),
                pltpu.VMEM((width, total), BF16),
                pltpu.VMEM((heads, TILE, PAIR), BF16),
                pltpu.VMEM((heads, TILE, PAIR), BF16),
                pltpu.VMEM((heads, TILE, PAIR), BF16),
                pltpu.VMEM((total, width), F32),
                pltpu.VMEM((total, width), F32),
                pltpu.VMEM((width, TILE), F32),
                pltpu.VMEM((8, TILE), F32),
            ],
        ),
        out_shape=[
            jax.ShapeDtypeStruct((total, cols), BF16),
            jax.ShapeDtypeStruct((8, cols), F32),
            jax.ShapeDtypeStruct((8, width), F32),
        ],
        compiler_params=params(),
        cost_estimate=pl.CostEstimate(flops=20 * total * total * width, bytes_accessed=20 * 10**6, transcendentals=0),
    )(lo, hi, *arrays)


def norm_back_kernel(x_ref, own_ref, got_ref, gres_ref, gain_ref, out_ref, sums_ref):
    @pl.when(pl.program_id(0) == 0)
    def _():
        sums_ref[...] = jnp.zeros_like(sums_ref)

    x = x_ref[...].astype(F32)
    cen = x - jnp.mean(x, axis=1, keepdims=True)
    rs = lax.rsqrt(jnp.mean(cen * cen, axis=1, keepdims=True) + EPS)
    xh = cen * rs
    e = own_ref[...] + got_ref[...].astype(F32)
    eg = e * gain_ref[...]
    out_ref[...] = gres_ref[...] + rs * (
        eg - jnp.mean(eg, axis=1, keepdims=True) - xh * jnp.mean(eg * xh, axis=1, keepdims=True)
    )
    sums_ref[0:1, :] += jnp.sum(e * xh, axis=0, keepdims=True)
    sums_ref[1:2, :] += jnp.sum(e, axis=0, keepdims=True)


def norm_back_call(x, own, got, gres, gain):
    rows, width = x.shape
    tile = pl.BlockSpec((TILE, width), lambda i: (i, 0))
    return pl.pallas_call(
        norm_back_kernel,
        grid=(rows // TILE,),
        in_specs=[tile, tile, tile, tile, pl.BlockSpec((1, width), lambda i: (0, 0))],
        out_specs=[tile, pl.BlockSpec((8, width), lambda i: (0, 0))],
        out_shape=[jax.ShapeDtypeStruct((rows, width), F32), jax.ShapeDtypeStruct((8, width), F32)],
        compiler_params=params(),
        cost_estimate=pl.CostEstimate(flops=20 * rows * width, bytes_accessed=12 * rows * width, transcendentals=0),
    )(x, own, got, gres, gain)


def bit_groups(count):
    bits = count.bit_length() - 1
    groups = []
    at = bits
    while at > 1:
        low = max(1, at - 3)
        groups.append((low, at - low))
        at = low
    if bits:
        groups.append((0, 1))
    return groups


def partners(count, mask):
    return [(i, i ^ mask) for i in range(count)]


def reorder(pieces, me):
    out = list(pieces)
    bit = 1
    while bit < len(out):
        flip = (me & bit) != 0
        out = [jnp.where(flip, out[t ^ bit], out[t]) for t in range(len(out))]
        bit *= 2
    return out


def gather_rows(shard, axis, count):
    index = lax.axis_index(axis)
    held = shard[None]
    for low, size in bit_groups(count):
        pieces = [held] + [
            lax.ppermute(held, axis, partners(count, m << low)) for m in range(1, 1 << size)
        ]
        me = (index >> low) & ((1 << size) - 1)
        held = jnp.stack(reorder(pieces, me), axis=1)
        held = held.reshape((-1,) + shard.shape)
    return held.reshape((-1,) + shard.shape[1:])


def scatter_rows(full, axis, count):
    index = lax.axis_index(axis)
    rows = full.shape[0] // count
    held = full
    left = count
    groups = bit_groups(count)[::-1]
    for low, size in groups:
        span = 1 << size
        blocks = held.reshape((left // span, span, rows, full.shape[1]))
        me = (index >> low) & (span - 1)
        sums = lax.dynamic_index_in_dim(blocks, me, 1, False).astype(F32)
        for m in range(1, span):
            send = lax.dynamic_index_in_dim(blocks, me ^ m, 1, False)
            sums = sums + lax.ppermute(send, axis, partners(count, m << low)).astype(F32)
        left //= span
        held = sums if left == 1 else sums.astype(BF16)
    return held.reshape(rows, full.shape[1])


def butterfly(value, axis, count):
    mask = 1
    while mask < count:
        value = value + lax.ppermute(value, axis, partners(count, mask))
        mask *= 2
    return value


def body(
    patches, lengths, w_qkv, qkv_bias, w_out, out_bias, w_up, up_bias, w_down, down_bias,
    gain_one, shift_one, gain_two, shift_two, rope_freqs, cotangent,
):
    _, rows, width = patches.shape
    count = lax.axis_size("seq")
    side = lax.axis_index("rows")
    flip = [(0, 1), (1, 0)]
    total = 2 * rows
    heads = rope_freqs.shape[1]
    half = width // 2
    hidden = up_bias.shape[0]
    depth = w_out.shape[0]
    deep = w_down.shape[0]
    wide = lambda v: v.astype(F32)[None, :]

    x = patches[0]
    cot = cotangent[0]
    x_other = lax.ppermute(x, "rows", flip)

    own_cols = lax.dynamic_index_in_dim(w_qkv.reshape(depth, 3, 2, half), side, 2, False)
    qkv_full = gather_rows(own_cols.reshape(depth, 3 * half), "seq", count)

    bulk = jnp.concatenate(
        [w_out, w_down] + [w_up[:, c : c + width] for c in range(0, hidden, width)], axis=0
    )
    bulk = lax.all_gather(bulk, "seq", axis=0, tiled=False)
    out_full = bulk[:, :depth].reshape(width, width)
    down_full = bulk[:, depth : depth + deep].reshape(hidden, width)
    up_full = jnp.concatenate(
        [
            bulk[:, depth + deep + c * depth : depth + deep + (c + 1) * depth].reshape(width, width)
            for c in range(hidden // width)
        ],
        axis=1,
    )

    block, row_pos, col_pos, lo, hi = layout(lengths[0], total, TILE)
    row_f = row_pos.astype(F32)
    col_f = col_pos.astype(F32)
    own_freqs = lax.dynamic_slice_in_dim(rope_freqs, side * (heads // 2), heads // 2, 1)
    lane_freqs = jnp.concatenate([own_freqs, own_freqs], axis=-1).reshape(2, half)
    angles = row_f[:, None] * lane_freqs[0] + col_f[:, None] * lane_freqs[1]
    lane = jnp.arange(half) % HEAD
    cos = jnp.cos(angles)
    sin = jnp.sin(angles) * jnp.where(lane < HEAD // 2, -1.0, 1.0)
    slot = jnp.arange(PAIR, dtype=jnp.int32)[None, :] % HEAD
    same = slot == block[:, None]
    mk = same.astype(BF16)
    mq = jnp.where(same | (slot > lengths.shape[1]), 0.0, NEG).astype(BF16)
    pos = jnp.pad(jnp.stack([row_f, col_f], axis=1), ((0, 0), (0, 6)))
    own_bias = lax.dynamic_index_in_dim(qkv_bias.reshape(3, 2, half), side, 1, False).reshape(3 * half)

    normed, qkv = qkv_call(
        side[None].astype(jnp.int32), x, x_other, qkv_full, wide(own_bias), wide(gain_one), wide(shift_one), cos, sin
    )
    att, lse = attend_call(lo, hi, qkv, mq, mk)

    mine = lax.dynamic_slice_in_dim(att, side * rows, rows, 0)
    theirs = lax.dynamic_slice_in_dim(att, (1 - side) * rows, rows, 0)
    got = lax.ppermute(theirs, "rows", flip)
    att_rows = jnp.where(side == 0, jnp.concatenate([mine, got], 1), jnp.concatenate([got, mine], 1))

    hid, gres, gatt, gwo, gwu, gwd, gub, sums_two = ffn_call(
        att_rows, x, cot, out_full, up_full, down_full,
        wide(out_bias), wide(up_bias), wide(down_bias), wide(gain_two), wide(shift_two),
    )

    grads = jnp.concatenate(
        [gwo.reshape(count, depth, width), gwd.reshape(count, deep, width)]
        + [gwu[:, c : c + width].reshape(count, depth, width) for c in range(0, hidden, width)],
        axis=1,
    )

    g_mine = lax.dynamic_slice_in_dim(gatt, side * half, half, 1)
    g_theirs = lax.dynamic_slice_in_dim(gatt, (1 - side) * half, half, 1)
    g_got = lax.ppermute(g_theirs, "rows", flip)
    do = jnp.where(side == 0, jnp.concatenate([g_mine, g_got], 0), jnp.concatenate([g_got, g_mine], 0))

    gproj, sums_qkv, tsum = attend_back_call(lo, hi, qkv, do, att, lse, mq, mk, cos, sin, pos)

    part = nt(gproj, qkv_full)
    part_mine = lax.dynamic_slice_in_dim(part, side * rows, rows, 0)
    part_theirs = lax.dynamic_slice_in_dim(part, (1 - side) * rows, rows, 0).astype(BF16)
    part_got = lax.ppermute(part_theirs, "rows", flip)
    gw_qkv = tn(normed, gproj).astype(BF16)
    shard_own = scatter_rows(gw_qkv, "seq", count)
    shard_other = lax.ppermute(shard_own, "rows", flip)
    first = jnp.where(side == 0, shard_own, shard_other).reshape(depth, 3, 1, half)
    other = jnp.where(side == 0, shard_other, shard_own).reshape(depth, 3, 1, half)
    shard_qkv = jnp.concatenate([first, other], axis=2).reshape(depth, 6 * half)

    patch_grad, sums_one = norm_back_call(x, part_mine, part_got, gres, wide(gain_one))

    shard = lax.psum_scatter(grads.reshape(-1, width), "seq", scatter_dimension=0, tiled=True)
    shard = shard.astype(F32) + lax.ppermute(shard, "rows", flip).astype(F32)
    shard_out = shard[:depth]
    shard_down = shard[depth : depth + deep]
    shard_up = jnp.concatenate(
        [shard[depth + deep + c * depth : depth + deep + (c + 1) * depth] for c in range(hidden // width)], axis=1
    )
    squares = 0.5 * (jnp.sum(shard * shard) + jnp.sum(shard_qkv * shard_qkv))

    own_sums = jnp.zeros((3, 2, half), F32)
    own_sums = lax.dynamic_update_index_in_dim(own_sums, sums_qkv[0].reshape(3, half), side, 1)
    t_own = tsum[:2].reshape(2, heads // 2, 2, HEAD // 2)
    t_own = t_own[:, :, 1] - t_own[:, :, 0]
    t_all = lax.dynamic_update_slice_in_dim(jnp.zeros((2, heads, HEAD // 2), F32), t_own, side * (heads // 2), 1)
    small = jnp.concatenate(
        [
            own_sums.reshape(-1),
            gub[0],
            sums_two[:4].reshape(-1),
            sums_one[:2].reshape(-1),
            t_all.reshape(-1),
            squares[None],
        ]
    )
    pad = -small.shape[0] % 1024
    small = jnp.pad(small, (0, pad)).reshape(-1, 128)
    small = small + lax.ppermute(small, "rows", flip)
    small = butterfly(small, "seq", count).reshape(-1)
    at = 0

    def take(n):
        nonlocal at
        at += n
        return small[at - n : at]

    s_qkv = take(3 * width)
    s_up = take(hidden)
    s_out, s_down, s_gain2, s_shift2, s_gain1, s_shift1 = (take(width) for _ in range(6))
    s_freqs = take(width)
    main = take(1)[0]
    for piece in (s_qkv, s_up, s_out, s_down, s_gain2, s_shift2, s_gain1, s_shift1):
        main = main + jnp.sum(piece * piece)
    return (
        hid[None],
        patch_grad[None],
        shard_qkv,
        s_qkv,
        shard_out,
        s_out,
        shard_up,
        s_up,
        shard_down,
        s_down,
        s_gain1,
        s_shift1,
        s_gain2,
        s_shift2,
        s_freqs.reshape(rope_freqs.shape),
        jnp.sqrt(main),
        jnp.sqrt(jnp.sum(s_freqs * s_freqs)),
    )


def solution(mesh):
    in_specs = (
        P("seq", "rows", None),
        P("seq", None),
        P("seq", None),
        P(),
        P("seq", None),
        P(),
        P("seq", None),
        P(),
        P("seq", None),
        P(),
        P(),
        P(),
        P(),
        P(),
        P(),
        P("seq", "rows", None),
    )
    out_specs = (
        P("seq", "rows", None),
        P("seq", "rows", None),
        P("seq", None),
        P(),
        P("seq", None),
        P(),
        P("seq", None),
        P(),
        P("seq", None),
        P(),
        P(),
        P(),
        P(),
        P(),
        P(),
        P(),
        P(),
    )
    return jax.shard_map(body, mesh=mesh, in_specs=in_specs, out_specs=out_specs, check_vma=False)
```

```python
import jax
import jax.numpy as jnp
from jax import lax
from jax.experimental import pallas as pl
from jax.experimental.pallas import tpu as pltpu
from jax.sharding import PartitionSpec as P

SIDE_S = 14
SIDE_M = 20
SIDE_L = 24
EPS = 1e-06
NEG = -1e30
HEAD = 64
PAIR = 128
TILE = 256
F32 = jnp.float32
BF16 = jnp.bfloat16
VMEM_LIMIT = 60 * 1024 * 1024
OUT_BIAS, DOWN_BIAS, GAIN_ONE, SHIFT_ONE, GAIN_TWO, SHIFT_TWO = (slice(r, r + 1) for r in range(3, 9))


def cost(us):
    return pl.CostEstimate(flops=int(us * 1150000000), bytes_accessed=10**5, transcendentals=0)


def params(**kw):
    return pltpu.CompilerParams(vmem_limit_bytes=VMEM_LIMIT, **kw)


def nn(a, b):
    return lax.dot_general(a, b, (((1,), (0,)), ((), ())), preferred_element_type=F32)


def nt(a, b):
    return lax.dot_general(a, b, (((1,), (1,)), ((), ())), preferred_element_type=F32)


def tn(a, b):
    return lax.dot_general(a, b, (((0,), (0,)), ((), ())), preferred_element_type=F32)


def swap_halves(u):
    width = u.shape[-1]
    lane = lax.broadcasted_iota(jnp.int32, u.shape, 1) % HEAD
    return jnp.where(
        lane < HEAD // 2,
        pltpu.roll(u, width - HEAD // 2, 1),
        pltpu.roll(u, HEAD // 2, 1),
    )


def head_lanes(shape, odd):
    lane = lax.broadcasted_iota(jnp.int32, shape, 1)
    return (lane >= HEAD) if odd else (lane < HEAD)


def tile_bounds(info_ref, tile, total):
    first = tile * TILE
    last = first + TILE - 1
    run = jnp.int32(0)
    low = jnp.int32(-1)
    high = jnp.int32(total)
    for s in range(3, info_ref.shape[0]):
        end = run + info_ref[s]
        low = jnp.where((first >= run) & (first < end), run, low)
        high = jnp.where((last >= run) & (last < end), end, high)
        run = end
    low = jnp.where(low < 0, run, low)
    return lax.div(low, TILE), lax.div(high + (TILE - 1), TILE)


def pack_kernel(info_ref, out_ref, up_ref, qkv_ref, packed_ref, cols_ref):
    depth, width = out_ref.shape
    half = width // 2
    packed_ref[:depth, :] = out_ref[...]
    for c in range(up_ref.shape[1] // width):
        packed_ref[(c + 1) * depth : (c + 2) * depth, :] = up_ref[:, c * width : (c + 1) * width]
    for i in range(3):
        at = pl.multiple_of(i * width + info_ref[0] * half, PAIR)
        cols_ref[:, i * half : (i + 1) * half] = qkv_ref[:, pl.ds(at, half)]


def pack_call(info, w_out, w_up, w_qkv):
    depth, width = w_out.shape
    whole = lambda r, c: pl.BlockSpec((r, c), lambda i, s: (0, 0))
    blocks = w_up.shape[1] // width + 1
    return pl.pallas_call(
        pack_kernel,
        grid_spec=pltpu.PrefetchScalarGridSpec(
            num_scalar_prefetch=1,
            grid=(1,),
            in_specs=[whole(*w_out.shape), whole(*w_up.shape), whole(*w_qkv.shape)],
            out_specs=[whole(blocks * depth, width), whole(depth, 3 * width // 2)],
        ),
        out_shape=[
            jax.ShapeDtypeStruct((blocks * depth, width), BF16),
            jax.ShapeDtypeStruct((depth, 3 * width // 2), BF16),
        ],
        compiler_params=params(),
        cost_estimate=cost(2.5),
    )(info, w_out, w_up, w_qkv)


def table_kernel(info_ref, freq_ref, cos_ref, sin_ref, mq_ref, mk_ref, pos_ref):
    step = pl.program_id(0)
    slots = info_ref.shape[0] - 3

    def place(shape):
        at = lax.broadcasted_iota(jnp.int32, shape, 0) + step * TILE
        block = jnp.full(shape, slots, jnp.int32)
        offset = jnp.zeros(shape, jnp.int32)
        side = jnp.ones(shape, F32)
        run = jnp.int32(0)
        for s in range(slots):
            count = info_ref[3 + s]
            inside = (at >= run) & (at < run + count)
            width = jnp.where(count == SIDE_S * SIDE_S, SIDE_S, jnp.where(count == SIDE_M * SIDE_M, SIDE_M, SIDE_L))
            block = jnp.where(inside, s, block)
            offset = jnp.where(inside, at - run, offset)
            side = jnp.where(inside, width.astype(F32), side)
            run = run + count
        offset = offset.astype(F32)
        row = jnp.floor((offset + 0.5) / side)
        return block, row, offset - row * side

    block, row, col = place((TILE, PAIR))
    lane = lax.broadcasted_iota(jnp.int32, (TILE, PAIR), 1)
    slot = lane % HEAD
    same = slot == block
    mk_ref[...] = same.astype(F32).astype(BF16)
    mq_ref[...] = jnp.where(same | (slot > slots), 0.0, NEG).astype(BF16)
    pos_ref[...] = jnp.where(lane == 0, row, jnp.where(lane == 1, col, 0.0))
    half = TILE // 2
    width = cos_ref.shape[1]
    front = lax.broadcasted_iota(jnp.int32, (half, width), 1) % HEAD < HEAD // 2
    both = lambda u: (u[:half, 0:1], u[half:, 0:1])
    row_a, row_b = both(row)
    col_a, col_b = both(col)
    angle = jnp.where(front, row_a, row_b) * freq_ref[0:1, :] + jnp.where(front, col_a, col_b) * freq_ref[1:2, :]
    for ref, value in ((cos_ref, jnp.cos(angle)), (sin_ref, jnp.sin(angle))):
        up = pltpu.roll(value, HEAD // 2, 1)
        down = pltpu.roll(value, width - HEAD // 2, 1)
        sign = -1.0 if ref is sin_ref else 1.0
        ref[:half, :] = jnp.where(front, sign * value, up)
        ref[half:, :] = jnp.where(front, sign * down, value)


def table_call(info, freqs, total):
    width = freqs.shape[1]
    tile = lambda c: pl.BlockSpec((TILE, c), lambda i, s: (i, 0))
    return pl.pallas_call(
        table_kernel,
        grid_spec=pltpu.PrefetchScalarGridSpec(
            num_scalar_prefetch=1,
            grid=(total // TILE,),
            in_specs=[pl.BlockSpec(freqs.shape, lambda i, s: (0, 0))],
            out_specs=[tile(width), tile(width), tile(PAIR), tile(PAIR), tile(PAIR)],
        ),
        out_shape=[
            jax.ShapeDtypeStruct((total, width), F32),
            jax.ShapeDtypeStruct((total, width), F32),
            jax.ShapeDtypeStruct((total, PAIR), BF16),
            jax.ShapeDtypeStruct((total, PAIR), BF16),
            jax.ShapeDtypeStruct((total, PAIR), F32),
        ],
        compiler_params=params(),
        cost_estimate=cost(9),
    )(info, freqs)


def qkv_kernel(
    place_ref, own_ref, other_ref, wa_ref, wb_ref, vec_ref, cos_ref, sin_ref, mk_ref,
    xh_ref, q_ref, k_ref, v_ref, kaug_ref, kt_ref, vt_ref, w_ref, wt_ref, *, depth,
):
    step = pl.program_id(0)
    half = pl.num_programs(0) // 2
    width = cos_ref.shape[1]

    @pl.when(step == 0)
    def _():
        if depth is None:
            w_ref[...] = wa_ref[...]
        else:
            core = place_ref[1]
            pieces = wa_ref.shape[0] // depth
            for m in range(pieces):
                at = (place_ref[2] ^ m) * (2 * depth)
                held = spot(m, 2 * pieces)
                rows = slice(held * depth, (held + 1) * depth)
                w_ref[pl.ds(pl.multiple_of(at + core * depth, 16), depth), :] = wa_ref[rows, :]
                w_ref[pl.ds(pl.multiple_of(at + (1 - core) * depth, 16), depth), :] = wb_ref[rows, :]
        wt_ref[...] = w_ref[...].T

    mine = (step // half) == place_ref[0]
    x = jnp.where(mine, own_ref[...].astype(F32), other_ref[...].astype(F32))
    mean = jnp.mean(x, axis=1, keepdims=True)
    cen = x - mean
    var = jnp.mean(cen * cen, axis=1, keepdims=True)
    xh = cen * lax.rsqrt(var + EPS)
    xh_ref[...] = xh.astype(BF16).T
    normed = (xh * vec_ref[GAIN_ONE] + vec_ref[SHIFT_ONE]).astype(BF16)
    mid = pl.ds(pl.multiple_of(place_ref[0] * width, PAIR), width)
    bias = jnp.concatenate([vec_ref[i : i + 1, mid] for i in range(3)], axis=1)
    proj = nn(normed, w_ref[...]) + bias
    c = cos_ref[...]
    s = sin_ref[...]
    q = proj[:, :width]
    k = proj[:, width : 2 * width]
    q = (q * c + swap_halves(q) * s).astype(BF16)
    k = (k * c + swap_halves(k) * s).astype(BF16)
    v = proj[:, 2 * width :].astype(BF16)
    q_ref[...] = (q.astype(F32) * 0.125).astype(BF16)
    k_ref[...] = k
    v_ref[...] = v
    kt_ref[...] = k.T
    vt_ref[...] = v.T
    mk = mk_ref[...]
    for h in range(width // HEAD):
        pair = h // 2
        kp = k[:, pair * PAIR : (pair + 1) * PAIR]
        kaug_ref[h] = jnp.where(head_lanes(kp.shape, h % 2), kp, mk)


def qkv_call(place, own, other, wa, wb, depth, vec, cos, sin, mk):
    rows, width = own.shape
    total = 2 * rows
    cols = wa.shape[1]
    third = cols // 3
    heads = third // HEAD
    per = rows // TILE
    last = per - 1
    whole = lambda i, s: (0, 0)
    tile = lambda c: pl.BlockSpec((TILE, c), lambda i, s: (i, 0))
    return pl.pallas_call(
        lambda *refs: qkv_kernel(*refs, depth=depth),
        grid_spec=pltpu.PrefetchScalarGridSpec(
            num_scalar_prefetch=1,
            grid=(total // TILE,),
            in_specs=[
                pl.BlockSpec((TILE, width), lambda i, s: (jnp.clip(i - per * s[0], 0, last), 0)),
                pl.BlockSpec((TILE, width), lambda i, s: (jnp.clip(i - per * (1 - s[0]), 0, last), 0)),
                pl.BlockSpec(wa.shape, whole),
                pl.BlockSpec(wb.shape, whole),
                pl.BlockSpec(vec.shape, whole),
                tile(third),
                tile(third),
                tile(PAIR),
            ],
            out_specs=[
                pl.BlockSpec((width, TILE), lambda i, s: (0, i)),
                tile(third),
                tile(third),
                tile(third),
                pl.BlockSpec((heads, TILE, PAIR), lambda i, s: (0, i, 0)),
                pl.BlockSpec((third, TILE), lambda i, s: (0, i)),
                pl.BlockSpec((third, TILE), lambda i, s: (0, i)),
                pl.BlockSpec((width, cols), whole),
                pl.BlockSpec((cols, width), whole),
            ],
        ),
        out_shape=[
            jax.ShapeDtypeStruct((width, total), BF16),
            jax.ShapeDtypeStruct((total, third), BF16),
            jax.ShapeDtypeStruct((total, third), BF16),
            jax.ShapeDtypeStruct((total, third), BF16),
            jax.ShapeDtypeStruct((heads, total, PAIR), BF16),
            jax.ShapeDtypeStruct((third, total), BF16),
            jax.ShapeDtypeStruct((third, total), BF16),
            jax.ShapeDtypeStruct((width, cols), BF16),
            jax.ShapeDtypeStruct((cols, width), BF16),
        ],
        compiler_params=params(),
        cost_estimate=cost(1),
    )(place, own, other, wa, wb, vec, cos, sin, mk)


def attend_kernel(base_ref, info_ref, q_ref, kaug_ref, vt_ref, mq_ref, out_ref, lse_ref, qaug, scores, acc):
    step = pl.program_id(0) + base_ref[0]
    width = out_ref.shape[1]
    heads = width // HEAD
    mq = mq_ref[...]
    for h in range(heads):
        pair = h // 2
        q = q_ref[:, pair * PAIR : (pair + 1) * PAIR]
        qaug[h] = jnp.where(head_lanes(q.shape, h % 2), q, mq)
    lo, hi = tile_bounds(info_ref, step, kaug_ref.shape[1])

    def first(kt, best):
        keys = pl.ds(pl.multiple_of(kt * TILE, TILE), TILE)
        out = []
        for h in range(heads):
            s = nt(kaug_ref[h, keys, :], qaug[h])
            scores[h, keys, :] = s
            out.append(jnp.maximum(best[h], jnp.max(s.reshape(TILE // 8, 8, TILE), axis=0)))
        return tuple(out)

    best = lax.fori_loop(lo, hi, first, tuple(jnp.full((8, TILE), -jnp.inf, F32) for _ in range(heads)))
    best = [jnp.max(b, axis=0, keepdims=True) for b in best]
    acc[...] = jnp.zeros_like(acc)

    def second(kt, sums):
        keys = pl.ds(pl.multiple_of(kt * TILE, TILE), TILE)
        out = []
        for h in range(heads):
            p = jnp.exp(scores[h, keys, :] - best[h])
            out.append(sums[h] + jnp.sum(p.reshape(TILE // 8, 8, TILE), axis=0))
            own = slice(h * HEAD, (h + 1) * HEAD)
            acc[own, :] += nn(vt_ref[own, keys], p.astype(BF16))
        return tuple(out)

    sums = lax.fori_loop(lo, hi, second, tuple(jnp.zeros((8, TILE), F32) for _ in range(heads)))
    lses = []
    outs = []
    for h in range(heads):
        tot = jnp.sum(sums[h], axis=0, keepdims=True)
        outs.append(acc[h * HEAD : (h + 1) * HEAD, :] / tot)
        lses.append(best[h] + jnp.log(tot))
    lses += [jnp.zeros_like(lses[0])] * (8 - heads)
    lse_ref[...] = jnp.concatenate(lses, axis=0)
    out_ref[...] = jnp.concatenate(outs, axis=0).T.astype(BF16)


def attend_call(base, info, q, kaug, vt, mq):
    total, width = q.shape
    heads = width // HEAD
    rows = total // 2
    whole = lambda i, b, s: (0, 0)
    return pl.pallas_call(
        attend_kernel,
        grid_spec=pltpu.PrefetchScalarGridSpec(
            num_scalar_prefetch=2,
            grid=(rows // TILE,),
            in_specs=[
                pl.BlockSpec((TILE, width), lambda i, b, s: (b[0] + i, 0)),
                pl.BlockSpec(kaug.shape, lambda i, b, s: (0, 0, 0)),
                pl.BlockSpec(vt.shape, whole),
                pl.BlockSpec((TILE, PAIR), lambda i, b, s: (b[0] + i, 0)),
            ],
            out_specs=[
                pl.BlockSpec((TILE, width), lambda i, b, s: (i, 0)),
                pl.BlockSpec((8, TILE), lambda i, b, s: (0, i)),
            ],
            scratch_shapes=[
                pltpu.VMEM((heads, TILE, PAIR), BF16),
                pltpu.VMEM((heads, total, TILE), F32),
                pltpu.VMEM((width, TILE), F32),
            ],
        ),
        out_shape=[
            jax.ShapeDtypeStruct((rows, width), BF16),
            jax.ShapeDtypeStruct((8, rows), F32),
        ],
        compiler_params=params(),
        cost_estimate=cost(4),
    )(base, info, q, kaug, vt, mq)


def phi_parts(x):
    cdf = 0.5 * (1.0 + lax.erf(x * 0.7071067811865476))
    pdf = jnp.exp(-0.5 * x * x) * 0.3989422804014327
    return cdf, pdf


def pre_kernel(place_ref, mine_ref, got_ref, x_ref, wo_ref, vec_ref, att_ref, res_ref, normed_ref):
    width = x_ref.shape[1]
    half = width // 2
    lanes = lambda at: pl.ds(pl.multiple_of(at * half, PAIR), half)
    att_ref[:, lanes(place_ref[0])] = mine_ref[...]
    att_ref[:, lanes(1 - place_ref[0])] = got_ref[...]
    wo = wo_ref[...].reshape(width, width)
    r = x_ref[...].astype(F32) + (nn(att_ref[...], wo) + vec_ref[OUT_BIAS])
    res_ref[...] = r
    cen = r - jnp.mean(r, axis=1, keepdims=True)
    var = jnp.mean(cen * cen, axis=1, keepdims=True)
    normed_ref[...] = (cen * lax.rsqrt(var + EPS) * vec_ref[GAIN_TWO] + vec_ref[SHIFT_TWO]).astype(BF16)


def pack_spec(packed, parts, width, at):
    if packed.shape[0] == parts:
        return pl.BlockSpec((1, width, width), lambda j, s: (at(j), 0, 0))
    return pl.BlockSpec((packed.shape[0], packed.shape[1] // parts, width), lambda j, s: (0, at(j), 0))


def pre_call(place, mine, got, x, packed, parts, vec):
    rows, width = x.shape
    tile = lambda c: pl.BlockSpec((TILE, c), lambda j, s: (j, 0))
    return pl.pallas_call(
        pre_kernel,
        grid_spec=pltpu.PrefetchScalarGridSpec(
            num_scalar_prefetch=1,
            grid=(rows // TILE,),
            in_specs=[
                tile(width // 2),
                tile(width // 2),
                tile(width),
                pack_spec(packed, parts, width, lambda j: 0),
                pl.BlockSpec(vec.shape, lambda j, s: (0, 0)),
            ],
            out_specs=[tile(width), tile(width), tile(width)],
        ),
        out_shape=[
            jax.ShapeDtypeStruct((rows, width), BF16),
            jax.ShapeDtypeStruct((rows, width), F32),
            jax.ShapeDtypeStruct((rows, width), BF16),
        ],
        compiler_params=params(),
        cost_estimate=cost(30),
    )(place, mine, got, x, packed, vec)


def ffn_kernel(
    place_ref, att_ref, res_ref, normed_ref, cot_ref, wo_ref, wu_ref, *rest, chips,
):
    down = rest[: max(1, 2 * chips)]
    (
        vec_ref, ub_ref,
        hid_ref, gres_ref, gatt_ref, gwp_ref, send_ref, keep_ref, gub_ref, sums_ref,
        acc, gacc, act, gup, wd_s,
    ) = rest[max(1, 2 * chips) :]
    step = pl.program_id(0)
    steps = pl.num_programs(0) - 1
    rows, width = res_ref.shape
    half = width // 2
    core = place_ref[1]
    chunks = [pl.ds(r, TILE) for r in range(0, rows, TILE)]
    lanes = lambda at: pl.ds(pl.multiple_of(at * half, PAIR), half)

    @pl.when(step == 0)
    def _():
        acc[...] = jnp.zeros_like(acc)
        gacc[...] = jnp.zeros_like(gacc)

    @pl.when(step < steps)
    def _():
        if chips:
            deep = down[0].shape[1]
            for t in range(chips):
                for r in (0, 1):
                    at = 2 * t * deep + (place_ref[0] ^ r) * deep
                    spot_rows = pl.ds(pl.multiple_of(at, 16), deep)
                    wd_s[spot_rows, lanes(core)] = down[t][r]
                    wd_s[spot_rows, lanes(1 - core)] = down[chips + t][r]
            wd_ref = wd_s
        else:
            wd_ref = down[0]
        bias_sum = jnp.zeros((1, ub_ref.shape[1]), F32)
        wu = wu_ref[...].reshape(width, width)
        for ch in chunks:
            up = nn(normed_ref[ch, :], wu) + ub_ref[...]
            cdf, pdf = phi_parts(up)
            a = (up * cdf).astype(BF16)
            act[ch, :] = a
            g = (nt(cot_ref[ch, :], wd_ref[...]) * (cdf + up * pdf)).astype(BF16)
            gup[ch, :] = g
            bias_sum += jnp.sum(g.astype(F32), axis=0, keepdims=True)
            acc[ch, :] += nn(a, wd_ref[...])
            gacc[ch, :] += nt(g, wu)
        gub_ref[...] = bias_sum
        send_ref[...] = tn(act[...], cot_ref[:, lanes(1 - core)]).astype(BF16)
        keep_ref[...] = tn(act[...], cot_ref[:, lanes(core)]).astype(BF16)
        gwp_ref[...] = tn(normed_ref[...], gup[...]).astype(BF16).reshape(gwp_ref.shape)

    @pl.when(step == steps)
    def _():
        zero = jnp.zeros((1, width), F32)
        s_out, s_down, s_gain, s_shift = zero, zero, zero, zero
        gain = vec_ref[GAIN_TWO]
        wo = wo_ref[...].reshape(width, width)
        for ch in chunks:
            r = res_ref[ch, :]
            hid_ref[ch, :] = (r + acc[ch, :] + vec_ref[DOWN_BIAS]).astype(BF16)
            cen = r - jnp.mean(r, axis=1, keepdims=True)
            rs = lax.rsqrt(jnp.mean(cen * cen, axis=1, keepdims=True) + EPS)
            xh = cen * rs
            e = gacc[ch, :]
            eg = e * gain
            cot = cot_ref[ch, :].astype(F32)
            g = cot + rs * (
                eg - jnp.mean(eg, axis=1, keepdims=True) - xh * jnp.mean(eg * xh, axis=1, keepdims=True)
            )
            gres_ref[ch, :] = g
            gb = g.astype(BF16)
            act[ch, :] = gb
            ga = nt(gb, wo).astype(BF16)
            gatt_ref[0, ch, :] = ga[:, :half]
            gatt_ref[1, ch, :] = ga[:, half:]
            s_out += jnp.sum(gb.astype(F32), axis=0, keepdims=True)
            s_down += jnp.sum(cot, axis=0, keepdims=True)
            s_gain += jnp.sum(e * xh, axis=0, keepdims=True)
            s_shift += jnp.sum(e, axis=0, keepdims=True)
        gwp_ref[...] = tn(att_ref[...], act[...]).astype(BF16).reshape(gwp_ref.shape)
        sums_ref[...] = jnp.concatenate([s_out, s_down, s_gain, s_shift] + [zero] * 4, axis=0)


def ffn_call(place, att, res, normed, cot, packed, down_a, down_b, vec, ub):
    rows, width = res.shape
    half = width // 2
    hidden = ub.shape[1]
    steps = hidden // width
    last = steps - 1
    whole = lambda j, s: (0, 0)
    one = lambda r, c: pl.BlockSpec((r, c), whole)
    pack = lambda at: pack_spec(packed, steps + 1, width, at)
    clip = lambda j: jnp.minimum(j, last)
    if down_b is None:
        chips = 0
        down = (down_a,)
        down_specs = [pl.BlockSpec((width, width), lambda j, s: (clip(j), 0))]
    else:
        deep = down_a.shape[3]
        chips = width // (2 * deep)

        def piece(t):
            def at(j, s):
                chip = (clip(j) * chips + t) ^ s[2]
                return (chip & 1, 0, chip >> 1, 0, 0)

            return pl.BlockSpec((pl.squeezed, 2, pl.squeezed, deep, half), at)

        down_specs = [piece(t) for t in range(chips)] * 2
        down = (down_a,) * chips + (down_b,) * chips
    return pl.pallas_call(
        lambda *refs: ffn_kernel(*refs, chips=chips),
        grid_spec=pltpu.PrefetchScalarGridSpec(
            num_scalar_prefetch=1,
            grid=(steps + 1,),
            in_specs=[
                one(rows, width),
                one(rows, width),
                one(rows, width),
                one(rows, width),
                pack(lambda j: 0),
                pack(lambda j: 1 + clip(j)),
                *down_specs,
                one(*vec.shape),
                pl.BlockSpec((1, width), lambda j, s: (0, clip(j))),
            ],
            out_specs=[
                one(rows, width),
                one(rows, width),
                pl.BlockSpec((2, rows, half), lambda j, s: (0, 0, 0)),
                pack(lambda j: jnp.where(j < steps, 1 + j, 0)),
                pl.BlockSpec((width, half), lambda j, s: (clip(j), 0)),
                pl.BlockSpec((width, half), lambda j, s: (clip(j), 0)),
                pl.BlockSpec((1, width), lambda j, s: (0, clip(j))),
                one(8, width),
            ],
            scratch_shapes=[
                pltpu.VMEM((rows, width), F32),
                pltpu.VMEM((rows, width), F32),
                pltpu.VMEM((rows, width), BF16),
                pltpu.VMEM((rows, width), BF16),
                pltpu.VMEM((width, width), BF16),
            ],
        ),
        out_shape=[
            jax.ShapeDtypeStruct((rows, width), BF16),
            jax.ShapeDtypeStruct((rows, width), F32),
            jax.ShapeDtypeStruct((2, rows, half), BF16),
            jax.ShapeDtypeStruct(packed.shape, BF16),
            jax.ShapeDtypeStruct((hidden, half), BF16),
            jax.ShapeDtypeStruct((hidden, half), BF16),
            jax.ShapeDtypeStruct((1, hidden), F32),
            jax.ShapeDtypeStruct((8, width), F32),
        ],
        compiler_params=params(),
        cost_estimate=cost(38),
    )(place, att, res, normed, cot, packed, packed, *down, vec, ub)


def attend_back_kernel(base_ref, info_ref, do_ref, o_ref, lse_ref, q_ref, kaug_ref, kt_ref, v_ref, mq_ref, cos_ref, sin_ref, pos_ref, *rest, final, head):
    if final:
        k_ref, cos_all, sin_all, pos_all, dk_in, dv_in, gq_ref, gk_ref, gv_ref, sums_ref = rest[:10]
        qaug, qm, dom, dqt, delta, dk, dv = rest[10:]
    else:
        gq_ref, dk, dv, sums_ref = rest[:4]
        qaug, qm, dom, dqt, delta = rest[4:]
    step = pl.program_id(0)
    tile = step + base_ref[0]
    width = do_ref.shape[1]
    heads = width // HEAD
    pairs = heads // 2
    total = v_ref.shape[0]

    @pl.when(step == 0)
    def _():
        if final:
            dk[...] = dk_in[...]
            dv[...] = dv_in[...]
        else:
            dk[...] = jnp.zeros_like(dk)
            dv[...] = jnp.zeros_like(dv)
        sums_ref[...] = jnp.zeros_like(sums_ref)

    mq = mq_ref[...]
    for h in range(heads):
        pair = slice((h // 2) * PAIR, (h // 2 + 1) * PAIR)
        q = q_ref[:, pair]
        lanes = head_lanes(q.shape, h % 2)
        qaug[h] = jnp.where(lanes, q, mq)
        qm[h] = jnp.where(lanes, q, jnp.zeros_like(q))
        dom[h] = jnp.where(lanes, do_ref[:, pair], jnp.zeros_like(q))
    inner = do_ref[...].astype(F32) * o_ref[...].astype(F32)
    pick = (
        lax.broadcasted_iota(jnp.int32, (8, width), 1) // HEAD == lax.broadcasted_iota(jnp.int32, (8, width), 0)
    ).astype(F32)
    delta[...] = lax.dot_general(
        pick, inner, (((1,), (1,)), ((), ())), precision=lax.Precision.HIGHEST, preferred_element_type=F32
    )
    dqt[...] = jnp.zeros_like(dqt)

    def body(kt, carry):
        keys = pl.ds(pl.multiple_of(kt * TILE, TILE), TILE)
        for pr in range(pairs):
            pair = slice(pr * PAIR, (pr + 1) * PAIR)
            v = v_ref[keys, pair]
            dv_new = dv[keys, pair]
            dk_new = dk[keys, pair]
            for h in (2 * pr, 2 * pr + 1):
                own = slice(h * HEAD, (h + 1) * HEAD)
                s = nt(kaug_ref[h, keys, :], qaug[h])
                p = jnp.exp(s - lse_ref[head + h : head + h + 1, :])
                dp = nt(v, dom[h])
                ds = (p * (dp - delta[h : h + 1, :])).astype(BF16)
                dv_new += nn(p.astype(BF16), dom[h])
                dk_new += nn(ds, qm[h])
                dqt[own, :] += nn(kt_ref[own, keys], ds)
            dv[keys, pair] = dv_new
            dk[keys, pair] = dk_new
        return carry

    lo, hi = tile_bounds(info_ref, tile, total)
    lax.fori_loop(lo, hi, body, 0)

    def unrotate(u, c, s):
        return (u * c - swap_halves(u) * s).astype(BF16)

    def freq_sum(u, rot, pos):
        w = u * swap_halves(rot)
        sums_ref[3:4, :] += jnp.sum(w * pos[:, 0:1], axis=0, keepdims=True)
        sums_ref[4:5, :] += jnp.sum(w * pos[:, 1:2], axis=0, keepdims=True)

    dq = dqt[...].T * 0.125
    freq_sum(dq, q_ref[...].astype(F32) * 8.0, pos_ref[...])
    gq = unrotate(dq, cos_ref[...], sin_ref[...])
    gq_ref[...] = gq
    sums_ref[0:1, :] += jnp.sum(gq.astype(F32), axis=0, keepdims=True)

    if final:

        @pl.when(step == pl.num_programs(0) - 1)
        def _():
            for t in range(total // TILE):
                at = pl.ds(t * TILE, TILE)
                u = dk[at, :]
                freq_sum(u, k_ref[at, :].astype(F32), pos_all[at, :])
                gk = unrotate(u, cos_all[at, :], sin_all[at, :])
                gv = dv[at, :].astype(BF16)
                gk_ref[at, :] = gk
                gv_ref[at, :] = gv
                sums_ref[1:2, :] += jnp.sum(gk.astype(F32), axis=0, keepdims=True)
                sums_ref[2:3, :] += jnp.sum(gv.astype(F32), axis=0, keepdims=True)


def attend_back_call(base, info, do, o, lse, q, k, kaug, kt, v, mq, cos, sin, pos, first, pairs, held=None):
    total = q.shape[0]
    width = pairs * PAIR
    heads = 2 * pairs
    spot = first // pairs
    rows = total // 2
    final = held is not None
    here = lambda c: pl.BlockSpec((TILE, c), lambda i, b, s: (i, spot))
    there = lambda c: pl.BlockSpec((TILE, c), lambda i, b, s: (b[0] + i, spot))
    flat = lambda c: pl.BlockSpec((TILE, c), lambda i, b, s: (b[0] + i, 0))
    tall = pl.BlockSpec((total, width), lambda i, b, s: (0, spot))
    whole = lambda a: pl.BlockSpec(a.shape, lambda i, b, s: (0,) * len(a.shape))
    args = [do, o, lse, q, kaug, kt, v, mq, cos, sin, pos]
    in_specs = [
        here(width), here(width), pl.BlockSpec((8, TILE), lambda i, b, s: (0, i)), there(width),
        pl.BlockSpec((heads, total, PAIR), lambda i, b, s: (spot, 0, 0)),
        pl.BlockSpec((width, total), lambda i, b, s: (spot, 0)),
        tall, flat(PAIR), there(width), there(width), flat(PAIR),
    ]
    big = jax.ShapeDtypeStruct((total, width), F32)
    low = jax.ShapeDtypeStruct((total, width), BF16)
    sums = jax.ShapeDtypeStruct((8, width), F32)
    scratch = [
        pltpu.VMEM((heads, TILE, PAIR), BF16),
        pltpu.VMEM((heads, TILE, PAIR), BF16),
        pltpu.VMEM((heads, TILE, PAIR), BF16),
        pltpu.VMEM((width, TILE), F32),
        pltpu.VMEM((8, TILE), F32),
    ]
    if final:
        args += [k, cos, sin, pos, *held]
        in_specs += [tall, tall, tall, whole(pos), tall, tall]
        grads = [low, low]
        scratch += [pltpu.VMEM((total, width), F32), pltpu.VMEM((total, width), F32)]
    else:
        grads = [big, big]
    return pl.pallas_call(
        lambda *refs: attend_back_kernel(*refs, final=final, head=2 * first),
        grid_spec=pltpu.PrefetchScalarGridSpec(
            num_scalar_prefetch=2,
            grid=(rows // TILE,),
            in_specs=in_specs,
            out_specs=[pl.BlockSpec((TILE, width), lambda i, b, s: (i, 0)), whole(big), whole(big), whole(sums)],
            scratch_shapes=scratch,
        ),
        out_shape=[jax.ShapeDtypeStruct((rows, width), BF16), *grads, sums],
        compiler_params=params(),
        cost_estimate=cost(10 * pairs),
    )(base, info, *args)


def part_kernel(base_ref, *refs, lanes):
    w_ref, out_ref = refs[-2:]
    total = jnp.zeros(out_ref.shape, F32)
    for ref, at in zip(refs, lanes):
        total += nn(ref[...], w_ref[at : at + ref.shape[1], :])
    out_ref[...] = total.astype(out_ref.dtype)


def part_call(base, queries, keys, w, kind):
    rows = queries[0][0].shape[0]
    here = lambda c: pl.BlockSpec((TILE, c), lambda i, b: (i, 0))
    there = lambda c: pl.BlockSpec((TILE, c), lambda i, b: (b[0] + i, 0))
    arrays = [a for a, _ in queries + keys]
    lanes = [at for _, at in queries + keys]
    return pl.pallas_call(
        lambda *refs: part_kernel(*refs, lanes=lanes),
        grid_spec=pltpu.PrefetchScalarGridSpec(
            num_scalar_prefetch=1,
            grid=(rows // TILE,),
            in_specs=[here(a.shape[1]) for a, _ in queries]
            + [there(a.shape[1]) for a, _ in keys]
            + [pl.BlockSpec(w.shape, lambda i, b: (0, 0))],
            out_specs=pl.BlockSpec((TILE, w.shape[1]), lambda i, b: (i, 0)),
        ),
        out_shape=jax.ShapeDtypeStruct((rows, w.shape[1]), kind),
        compiler_params=params(),
        cost_estimate=cost(5.6),
    )(base, *arrays, w)


def weight_kernel(place_ref, xh_ref, own_ref, *rest, depth, lanes):
    keys = 3 * len(lanes)
    grads = rest[:keys]
    w_ref, col_ref, vec_ref = rest[keys : keys + 3]
    *outs, spare = rest[keys + 3 :]
    sums_ref = outs[-1]
    third = w_ref.shape[1] // 3
    rows = own_ref.shape[0]
    block = w_ref.shape[0]
    flat = vec_ref[:, pl.ds(pl.multiple_of(pl.program_id(0) * block, PAIR), block)].T
    gain = flat[:, GAIN_ONE]
    shift = flat[:, SHIFT_ONE]
    total = jnp.zeros(gain.shape, F32)
    bias = jnp.zeros(gain.shape, F32)
    half = lambda at: pl.ds(pl.multiple_of(at * rows, TILE), rows)
    for g, (lane, width) in enumerate(lanes):
        for i in range(3):
            ref = grads[3 * g + i]
            at = slice(i * third + lane, i * third + lane + width)
            if i:
                x = nn(xh_ref[...], ref[...])
            else:
                own = own_ref[:, lane : lane + width]
                x = nn(xh_ref[:, half(place_ref[0])], own) + nn(xh_ref[:, half(1 - place_ref[0])], ref[...])
            w = w_ref[:, at].astype(F32)
            col = col_ref[:, at]
            total += jnp.sum(x * w, axis=1, keepdims=True)
            bias += jnp.sum(w * col, axis=1, keepdims=True)
            spare[:, at] = (x * gain + shift * col).astype(BF16)
    lane = lax.broadcasted_iota(jnp.int32, (block, PAIR), 1)
    both = jnp.where(lane == 0, total, jnp.where(lane == 1, bias, 0.0))
    sums_ref[...] = both.T[:8, :]
    if depth is None:
        outs[0][...] = spare[...]
        return
    core = place_ref[1]
    for t in range(spare.shape[0] // (2 * depth)):
        at = 2 * t * depth
        rows = slice(t * depth, (t + 1) * depth)
        outs[0][rows, :] = spare[pl.ds(pl.multiple_of(at + (1 - core) * depth, 16), depth), :]
        outs[1][rows, :] = spare[pl.ds(pl.multiple_of(at + core * depth, 16), depth), :]


def weight_call(place, xh, own, grads, w, col, vec, depth, lanes):
    model, total = xh.shape
    cols = w.shape[1]
    block = model // 2
    whole = lambda a: pl.BlockSpec(a.shape, lambda i, s: (0, 0))
    if depth is None:
        out_shape = [jax.ShapeDtypeStruct((model, cols), BF16)]
        out_specs = [pl.BlockSpec((block, cols), lambda i, s: (i, 0))]
    else:
        out_shape = [jax.ShapeDtypeStruct((model // 2, cols), BF16)] * 2
        out_specs = [pl.BlockSpec((block // 2, cols), lambda i, s: (i, 0))] * 2
    return pl.pallas_call(
        lambda *refs: weight_kernel(*refs, depth=depth, lanes=lanes),
        grid_spec=pltpu.PrefetchScalarGridSpec(
            num_scalar_prefetch=1,
            grid=(model // block,),
            in_specs=[
                pl.BlockSpec((block, total), lambda i, s: (i, 0)),
                whole(own),
                *[whole(g) for g in grads],
                pl.BlockSpec((block, cols), lambda i, s: (i, 0)),
                whole(col),
                whole(vec),
            ],
            out_specs=out_specs + [pl.BlockSpec((8, block), lambda i, s: (0, i))],
            scratch_shapes=[pltpu.VMEM((block, cols), BF16)],
        ),
        out_shape=out_shape + [jax.ShapeDtypeStruct((8, model), F32)],
        compiler_params=params(),
        cost_estimate=cost(9),
    )(place, xh, own, *grads, w, col, vec)


def norm_back_kernel(x_ref, own_ref, got_ref, gres_ref, vec_ref, out_ref):
    x = x_ref[...].astype(F32)
    cen = x - jnp.mean(x, axis=1, keepdims=True)
    rs = lax.rsqrt(jnp.mean(cen * cen, axis=1, keepdims=True) + EPS)
    xh = cen * rs
    eg = (own_ref[...] + got_ref[...].astype(F32)) * vec_ref[GAIN_ONE]
    out_ref[...] = gres_ref[...] + rs * (
        eg - jnp.mean(eg, axis=1, keepdims=True) - xh * jnp.mean(eg * xh, axis=1, keepdims=True)
    )


def norm_back_call(x, own, got, gres, vec):
    rows, width = x.shape
    tile = pl.BlockSpec((TILE, width), lambda i: (i, 0))
    return pl.pallas_call(
        norm_back_kernel,
        grid=(rows // TILE,),
        in_specs=[tile, tile, tile, tile, pl.BlockSpec(vec.shape, lambda i: (0, 0))],
        out_specs=tile,
        out_shape=jax.ShapeDtypeStruct((rows, width), F32),
        compiler_params=params(),
        cost_estimate=cost(6),
    )(x, own, got, gres, vec)


def collect_kernel(place_ref, own_ref, far_a_ref, far_b_ref, up_ref, two_ref, one_ref, qkv_ref, down_ref, rest_ref, out_ref):
    width = out_ref.shape[1]
    half = own_ref.shape[1]
    lanes = pl.ds(pl.multiple_of(place_ref[0] * half, PAIR), half)
    sums = own_ref[...] + jnp.concatenate([far_a_ref[...], far_b_ref[...]], axis=1)
    out_ref[...] = jnp.zeros_like(out_ref)
    for row in range(3):
        out_ref[row : row + 1, lanes] = sums[row : row + 1, :]
    for row in range(up_ref.shape[1] // width):
        out_ref[3 + row : 4 + row, :] = up_ref[:, row * width : (row + 1) * width]
    for row in range(4):
        out_ref[7 + row : 8 + row, :] = two_ref[row : row + 1, :]
    for row in range(2):
        out_ref[11 + row : 12 + row, :] = one_ref[row : row + 1, :]
        out_ref[13 + row : 14 + row, lanes] = sums[3 + row : 4 + row, :]
    total = jnp.zeros((1, 1), F32)
    for ref, scale in ((qkv_ref, 1.0), (down_ref, 1.0), (rest_ref, 0.5)):
        v = ref[...].astype(F32)
        total += scale * jnp.sum(jnp.sum(v * v, axis=0, keepdims=True), axis=1, keepdims=True)
    lane = lax.broadcasted_iota(jnp.int32, (1, width), 1)
    out_ref[15:16, :] = jnp.where(lane == 0, total, 0.0)


def collect_call(place, *arrays):
    width = arrays[4].shape[1]
    whole = lambda a: pl.BlockSpec(a.shape, lambda i, s: (0, 0))
    return pl.pallas_call(
        collect_kernel,
        grid_spec=pltpu.PrefetchScalarGridSpec(
            num_scalar_prefetch=1,
            grid=(1,),
            in_specs=[whole(a) for a in arrays],
            out_specs=pl.BlockSpec((16, width), lambda i, s: (0, 0)),
        ),
        out_shape=jax.ShapeDtypeStruct((16, width), F32),
        compiler_params=params(),
        cost_estimate=cost(3),
    )(place, *arrays)


def finish_kernel(in_ref, qkv_ref, up_ref, *rest):
    vectors, freq_ref, norm_ref = rest[:-2], rest[-2], rest[-1]
    width = in_ref.shape[1]
    value = in_ref[...]
    for row in range(3):
        qkv_ref[pl.ds(row * width, width)] = value[row]
    for row in range(4):
        up_ref[pl.ds(row * width, width)] = value[3 + row]
    for row in range(6):
        vectors[row][...] = value[7 + row]
    turned = value[13:15]
    turned = jnp.concatenate([turned] * 4, axis=0)
    turned = pltpu.roll(turned, width - HEAD // 2, 1) - turned
    freq_ref[...] = turned
    lane = lax.broadcasted_iota(jnp.int32, (2, width), 1) % HEAD
    square = lambda u: jnp.sum(jnp.sum(u * u, axis=0, keepdims=True), axis=1, keepdims=True)
    freqs = square(jnp.where(lane < HEAD // 2, turned[:2], 0.0))
    main = square(value[:13]) + value[15:16, 0:1]
    at = lax.broadcasted_iota(jnp.int32, (8, PAIR), 1)
    norm_ref[...] = jnp.sqrt(jnp.where(at == 0, main, freqs))


def finish_call(value, hidden):
    width = value.shape[1]
    shapes = [(3 * width,), (hidden,)] + [(width,)] * 6 + [(8, width), (8, PAIR)]
    whole = lambda shape: pl.BlockSpec(shape, lambda: (0,) * len(shape))
    return pl.pallas_call(
        finish_kernel,
        in_specs=[whole(value.shape)],
        out_specs=[whole(shape) for shape in shapes],
        out_shape=[jax.ShapeDtypeStruct(shape, F32) for shape in shapes],
        compiler_params=params(),
        cost_estimate=cost(2),
    )(value)


def partners(count, mask):
    return [(i, i ^ mask) for i in range(count)]


def chip_groups(count):
    bits = count.bit_length() - 1
    groups = []
    at = 1
    while at < bits:
        size = 1 if at == 1 else min(2, bits - at)
        groups.append((at, size))
        at += size
    return groups


def spot(mask, count):
    at = 0
    scale = 1
    for low, size in chip_groups(count)[::-1]:
        at = at + ((mask >> (low - 1)) & ((1 << size) - 1)) * scale
        scale <<= size
    return at


def gather_parts(held, axis, count, group):
    low, size = group
    return [held] + [lax.ppermute(held, axis, partners(count, m << low)) for m in range(1, 1 << size)]


def gather_stage(held, axis, count, group):
    return jnp.concatenate(gather_parts(held, axis, count, group), axis=0)


def scatter_chips(held, axis, count, groups):
    index = lax.axis_index(axis)
    chips, rows, cols = held.shape
    for low, size in groups:
        span = 1 << size
        blocks = held.reshape((chips // span, span, rows, cols))
        me = (index >> low) & (span - 1)
        sums = lax.dynamic_index_in_dim(blocks, me, 1, False).astype(F32)
        for m in range(1, span):
            send = lax.dynamic_index_in_dim(blocks, me ^ m, 1, False)
            sums = sums + lax.ppermute(send, axis, partners(count, m << low)).astype(F32)
        chips //= span
        held = sums if chips == 1 else sums.astype(BF16)
    return held.reshape(rows, cols) if chips == 1 else held


def sum_over(value, count, held):
    axes = ("seq", "rows")
    bits = count.bit_length()
    at = 0
    while at < bits:
        size = min(2, bits - at)
        if at + size == bits:
            value, *held = lax.optimization_barrier((value, *held))
        got = [lax.ppermute(value, axes, partners(2 * count, m << at)) for m in range(1, 1 << size)]
        value = value + got[0]
        if size == 2:
            value = value + (got[1] + got[2])
        at += size
    return value, held


def after(value, *others):
    return lax.optimization_barrier((value,) + others)[0]


def body(
    patches, lengths, w_qkv, qkv_bias, w_out, out_bias, w_up, up_bias, w_down, down_bias,
    gain_one, shift_one, gain_two, shift_two, rope_freqs, cotangent,
):
    _, rows, width = patches.shape
    count = lax.axis_size("seq")
    index = lax.axis_index("seq")
    side = lax.axis_index("rows")
    flip = [(0, 1), (1, 0)]
    total = 2 * rows
    heads = rope_freqs.shape[1]
    half = width // 2
    hidden = up_bias.shape[0]
    depth = w_out.shape[0]
    deep = w_down.shape[0]
    direct = count == 16
    blocks = hidden // width
    per = rows // TILE
    info = jnp.concatenate([jnp.stack([side, index % 2, index // 2]).astype(jnp.int32), lengths[0]])
    base_own = (side * per)[None].astype(jnp.int32)
    base_far = ((1 - side) * per)[None].astype(jnp.int32)
    vec = jnp.concatenate(
        [qkv_bias, out_bias, down_bias, gain_one, shift_one, gain_two, shift_two, jnp.zeros((7 * width,), BF16)]
    )
    vec = vec.astype(F32).reshape(16, width)
    up_row = up_bias.astype(F32)[None, :]

    x = patches[0]
    cot = cotangent[0]
    if direct:
        packed, own_cols = pack_call(info, w_out, w_up, w_qkv)
    else:
        packed = jnp.concatenate([w_out] + [w_up[:, c : c + width] for c in range(0, hidden, width)], axis=0)
        own_cols = lax.dynamic_index_in_dim(w_qkv.reshape(depth, 3, 2, half), side, 2, False).reshape(depth, 3 * half)
    own_freqs = lax.dynamic_slice_in_dim(rope_freqs, side * (heads // 2), heads // 2, 1)
    lane_freqs = jnp.concatenate([own_freqs, own_freqs], axis=-1).reshape(2, half)
    cos, sin, mq, mk, pos = table_call(info, lane_freqs, total)
    x_other = lax.ppermute(x, "rows", flip)
    core_pairs = partners(count, 1)
    if direct:
        near, far = chip_groups(count)
        down_got = lax.ppermute(
            lax.dynamic_slice_in_dim(w_down, (1 - index % 2) * half, half, 1), "seq", core_pairs
        )
        down = lax.dynamic_slice_in_dim(w_down, index % 2 * half, half, 1)
        down = jnp.where(index % 2 == side, down, down_got)
        qkv_a = gather_stage(own_cols[None], "seq", count, far)
        qkv_a, down, cos, sin, mq, mk, pos, vec, up_row = lax.optimization_barrier(
            (qkv_a, down, cos, sin, mq, mk, pos, vec, up_row)
        )
        down_parts = gather_parts(down[None], "seq", count, far)
        qkv_a = gather_stage(qkv_a, "seq", count, near)
        qkv_b = lax.ppermute(after(qkv_a, x_other), "seq", core_pairs)
        packed = lax.all_gather(packed, "seq", axis=0, tiled=False)
        qkv_a, qkv_b = qkv_a.reshape(-1, 3 * half), qkv_b.reshape(-1, 3 * half)
    else:
        packed = lax.all_gather(packed, "seq", axis=0, tiled=False)
        packed = packed.reshape(count, blocks + 1, depth, width).transpose(1, 0, 2, 3).reshape(blocks + 1, width, width)
        qkv_a = lax.all_gather(own_cols, "seq", axis=0, tiled=True)
        qkv_b = jnp.zeros((8, 3 * half), BF16)

    xh, q, k, v, kaug, kt, vt, w_own, w_turn = qkv_call(
        info, x, x_other, qkv_a, qkv_b, depth if direct else None, vec, cos, sin, mk
    )
    if direct:
        *down_parts, q = lax.optimization_barrier((*down_parts, q))
        down = jnp.concatenate(down_parts, axis=0)
        down_got = lax.ppermute(down, "rows", flip)
    att_far, lse_far = attend_call(base_far, info, q, kaug, vt, mq)
    att_got = lax.ppermute(att_far, "rows", flip)
    if direct:
        down, down_got, att_far = lax.optimization_barrier((down, down_got, att_far))
        down = jnp.stack([down, down_got], axis=0)[None]
        down = gather_stage(down, "seq", count, near)
    att_own, lse_own = attend_call(base_own, info, after(q, att_far), kaug, vt, mq)

    if direct:
        down_a = after(down, att_own)
        down_b = lax.ppermute(down_a, "seq", core_pairs)
    else:
        down_a, down_b = lax.all_gather(w_down, "seq", axis=0, tiled=True), None
    att, res, normed = pre_call(info, att_own, att_got, x, packed, blocks + 1, vec)
    hid, gres, gatt, gwp, gwd_send, gwd_keep, gub, sums_two = ffn_call(
        info, att, res, normed, cot, packed, down_a, down_b, vec, up_row
    )
    do_own = lax.dynamic_index_in_dim(gatt, side, 0, False)
    do_send = lax.dynamic_index_in_dim(gatt, 1 - side, 0, False)
    do_far = lax.ppermute(do_send, "rows", flip)

    if not direct:
        gwp = gwp.reshape(blocks + 1, count, depth, width).transpose(1, 0, 2, 3)
    shard_p = lax.psum_scatter(gwp.reshape(-1, width), "seq", scatter_dimension=0, tiled=True)

    gwd_got = lax.ppermute(gwd_send, "seq", core_pairs)

    back = (q, k, kaug, kt, v, mq, cos, sin, pos)
    all_pairs = half // PAIR
    gq_own, dk, dv, sums_own = attend_back_call(base_own, info, do_own, att_own, lse_own, *back, 0, all_pairs)
    gwd_got, gq_own, do_far = lax.optimization_barrier((gwd_got, gq_own, do_far))
    gwd = (gwd_keep.astype(F32) + gwd_got.astype(F32)).astype(BF16).reshape(count // 2, 2, deep, half)
    gwd_keep = lax.dynamic_index_in_dim(gwd, side, 1, False)
    gwd_got = lax.ppermute(lax.dynamic_index_in_dim(gwd, 1 - side, 1, False), "rows", flip)

    queries, keys, sums_far, grads, lanes = [], [], [], [], []
    for step, (first, pairs) in enumerate(((0, 2), (2, 1))):
        lane = first * PAIR
        gq, gk, gv, sums = attend_back_call(
            base_far, info, do_far, att_far, lse_far, *back, first, pairs, held=(dk, dv)
        )
        if step == 0:
            gwd_got, gq, dk = lax.optimization_barrier((gwd_got, gq, dk))
            gwd = (gwd_keep.astype(F32) + gwd_got.astype(F32)).astype(BF16)
            gwd = scatter_chips(gwd, "seq", count, chip_groups(count)[:1])
        else:
            gwd, gq = lax.optimization_barrier((gwd, gq))
            gwd = scatter_chips(gwd, "seq", count, chip_groups(count)[1:]).astype(BF16)
        queries.append((gq, lane))
        keys += [(gk, half + lane), (gv, 2 * half + lane)]
        sums_far.append(sums)
        grads += [gq, gk, gv]
        lanes.append((lane, pairs * PAIR))
    col = (sums_own[:3] + jnp.concatenate(sums_far, axis=1)[:3]).reshape(1, 3 * half)
    *gw, sums_one = weight_call(info, xh, gq_own, grads, w_own, col, vec, depth if direct else None, lanes)
    if not direct:
        gw = gw[0].reshape(count // 2, 2, depth, 3 * half)
        gw = [lax.dynamic_index_in_dim(gw, c, 1, False).reshape(-1, 3 * half) for c in (1 - index % 2, index % 2)]
    gw_got = lax.ppermute(gw[0], "seq", core_pairs)
    shard_got = lax.ppermute(shard_p, "rows", flip)
    w_turn, sums_one, shard_got = lax.optimization_barrier((w_turn, sums_one, shard_got))
    part_far = part_call(base_far, queries, keys, w_turn, BF16)
    part_got = lax.ppermute(part_far, "rows", flip)
    gw = (gw[1].astype(F32) + gw_got.astype(F32)).astype(BF16).reshape(count // 2, depth, 3 * half)
    gw = after(gw, part_far)
    shard_own = scatter_chips(gw, "seq", count, chip_groups(count))
    shard_far = lax.ppermute(shard_own, "rows", flip)
    own_keys = [(gq_own, 0)]
    part_own = part_call(base_own, own_keys, keys, after(w_turn, part_far), F32)
    patch_grad = norm_back_call(x, part_own, after(part_got, shard_own), gres, vec)

    swaps = []
    for mask in (0, 1):
        swaps.append([(2 * i + r, 2 * (i - i % 2 + r) + ((i % 2) ^ mask)) for i in range(count) for r in range(2)])
    same_half, other_half = (lax.ppermute(after(gwd, shard_own), ("seq", "rows"), p) for p in swaps)
    shard_p = shard_p.astype(F32) + shard_got.astype(F32)
    shard_out = shard_p[:depth]
    shard_up = jnp.concatenate([shard_p[(1 + c) * depth : (2 + c) * depth] for c in range(blocks)], axis=1)
    small = collect_call(info, sums_own, *sums_far, gub, sums_two, sums_one, shard_own, gwd, shard_p)
    small, (shard_far, same_half, other_half) = sum_over(small, count, (shard_far, same_half, other_half))
    first = jnp.where(side == 0, shard_own, shard_far).reshape(depth, 3, 1, half)
    second = jnp.where(side == 0, shard_far, shard_own).reshape(depth, 3, 1, half)
    shard_qkv = jnp.concatenate([first, second], axis=2).reshape(depth, 6 * half)

    low = side == 0
    shard_down = jnp.concatenate(
        [jnp.where(low, same_half, other_half), jnp.where(low, other_half, same_half)], axis=1
    ).astype(F32)

    s_qkv, s_up, s_out, s_down, s_gain2, s_shift2, s_gain1, s_shift1, freqs, norms = finish_call(small, hidden)
    freqs = freqs[:2].reshape(2, heads, HEAD)[:, :, : HEAD // 2]
    return (
        hid[None],
        patch_grad[None],
        shard_qkv,
        s_qkv,
        shard_out,
        s_out,
        shard_up,
        s_up,
        shard_down,
        s_down,
        s_gain1,
        s_shift1,
        s_gain2,
        s_shift2,
        freqs,
        norms[0, 0],
        norms[0, 1],
    )


def solution(mesh):
    in_specs = (
        P("seq", "rows", None),
        P("seq", None),
        P("seq", None),
        P(),
        P("seq", None),
        P(),
        P("seq", None),
        P(),
        P("seq", None),
        P(),
        P(),
        P(),
        P(),
        P(),
        P(),
        P("seq", "rows", None),
    )
    out_specs = (
        P("seq", "rows", None),
        P("seq", "rows", None),
        P("seq", None),
        P(),
        P("seq", None),
        P(),
        P("seq", None),
        P(),
        P("seq", None),
        P(),
        P(),
        P(),
        P(),
        P(),
        P(),
        P(),
        P(),
    )
    return jax.shard_map(body, mesh=mesh, in_specs=in_specs, out_specs=out_specs, check_vma=False)
```

```python
import jax
import jax.numpy as jnp
from jax import lax
from jax.experimental import pallas as pl
from jax.experimental.pallas import tpu as pltpu
from jax.sharding import PartitionSpec as P

SIDE_S = 14
SIDE_M = 20
SIDE_L = 24
EPS = 1e-06
NEG = -1e30
HEAD = 64
PAIR = 128
TILE = 256
F32 = jnp.float32
BF16 = jnp.bfloat16
VMEM_LIMIT = 60 * 1024 * 1024
OUT_BIAS, DOWN_BIAS, GAIN_ONE, SHIFT_ONE, GAIN_TWO, SHIFT_TWO = (slice(r, r + 1) for r in range(3, 9))


def cost(us):
    return pl.CostEstimate(flops=int(us * 1150000000), bytes_accessed=10**5, transcendentals=0)


def params(**kw):
    return pltpu.CompilerParams(vmem_limit_bytes=VMEM_LIMIT, **kw)


def nn(a, b):
    return lax.dot_general(a, b, (((1,), (0,)), ((), ())), preferred_element_type=F32)


def nt(a, b):
    return lax.dot_general(a, b, (((1,), (1,)), ((), ())), preferred_element_type=F32)


def tn(a, b):
    return lax.dot_general(a, b, (((0,), (0,)), ((), ())), preferred_element_type=F32)


def swap_halves(u):
    width = u.shape[-1]
    lane = lax.broadcasted_iota(jnp.int32, u.shape, 1) % HEAD
    return jnp.where(
        lane < HEAD // 2,
        pltpu.roll(u, width - HEAD // 2, 1),
        pltpu.roll(u, HEAD // 2, 1),
    )


def head_lanes(shape, odd):
    lane = lax.broadcasted_iota(jnp.int32, shape, 1)
    return (lane >= HEAD) if odd else (lane < HEAD)


def tile_bounds(info_ref, tile, total):
    first = tile * TILE
    last = first + TILE - 1
    run = jnp.int32(0)
    low = jnp.int32(-1)
    high = jnp.int32(total)
    for s in range(3, info_ref.shape[0]):
        end = run + info_ref[s]
        low = jnp.where((first >= run) & (first < end), run, low)
        high = jnp.where((last >= run) & (last < end), end, high)
        run = end
    low = jnp.where(low < 0, run, low)
    return lax.div(low, TILE), lax.div(high + (TILE - 1), TILE)


def pack_kernel(info_ref, down_ref, out_ref, up_ref, qkv_ref, packed_ref, cols_ref):
    depth, width = out_ref.shape
    half = width // 2
    share = packed_ref.shape[0] - depth * (1 + up_ref.shape[1] // width)
    packed_ref[:share, :] = down_ref[:share, :]
    packed_ref[share : share + depth, :] = out_ref[...]
    for c in range(up_ref.shape[1] // width):
        at = share + (c + 1) * depth
        packed_ref[at : at + depth, :] = up_ref[:, c * width : (c + 1) * width]
    for i in range(3):
        at = pl.multiple_of(i * width + info_ref[0] * half, PAIR)
        cols_ref[:, i * half : (i + 1) * half] = qkv_ref[:, pl.ds(at, half)]


def pack_call(info, w_down, w_out, w_up, w_qkv, share):
    depth, width = w_out.shape
    whole = lambda r, c: pl.BlockSpec((r, c), lambda i, s: (0, 0))
    length = share + depth * (w_up.shape[1] // width + 1)
    arrays = (w_down, w_out, w_up, w_qkv)
    return pl.pallas_call(
        pack_kernel,
        grid_spec=pltpu.PrefetchScalarGridSpec(
            num_scalar_prefetch=1,
            grid=(1,),
            in_specs=[whole(*a.shape) for a in arrays],
            out_specs=[whole(length, width), whole(depth, 3 * width // 2)],
        ),
        out_shape=[
            jax.ShapeDtypeStruct((length, width), BF16),
            jax.ShapeDtypeStruct((depth, 3 * width // 2), BF16),
        ],
        compiler_params=params(),
        cost_estimate=cost(2.5),
    )(info, *arrays)


def table_kernel(info_ref, freq_ref, cos_ref, sin_ref, mq_ref, mk_ref, pos_ref):
    step = pl.program_id(0)
    slots = info_ref.shape[0] - 3

    def place(shape):
        at = lax.broadcasted_iota(jnp.int32, shape, 0) + step * TILE
        block = jnp.full(shape, slots, jnp.int32)
        offset = jnp.zeros(shape, jnp.int32)
        side = jnp.ones(shape, F32)
        run = jnp.int32(0)
        for s in range(slots):
            count = info_ref[3 + s]
            inside = (at >= run) & (at < run + count)
            width = jnp.where(count == SIDE_S * SIDE_S, SIDE_S, jnp.where(count == SIDE_M * SIDE_M, SIDE_M, SIDE_L))
            block = jnp.where(inside, s, block)
            offset = jnp.where(inside, at - run, offset)
            side = jnp.where(inside, width.astype(F32), side)
            run = run + count
        offset = offset.astype(F32)
        row = jnp.floor((offset + 0.5) / side)
        return block, row, offset - row * side

    block, row, col = place((TILE, PAIR))
    lane = lax.broadcasted_iota(jnp.int32, (TILE, PAIR), 1)
    slot = lane % HEAD
    same = slot == block
    mk_ref[...] = same.astype(F32).astype(BF16)
    mq_ref[...] = jnp.where(same | (slot > slots), 0.0, NEG).astype(BF16)
    pos_ref[...] = jnp.where(lane == 0, row, jnp.where(lane == 1, col, 0.0))
    half = TILE // 2
    width = cos_ref.shape[1]
    front = lax.broadcasted_iota(jnp.int32, (half, width), 1) % HEAD < HEAD // 2
    both = lambda u: (u[:half, 0:1], u[half:, 0:1])
    row_a, row_b = both(row)
    col_a, col_b = both(col)
    angle = jnp.where(front, row_a, row_b) * freq_ref[0:1, :] + jnp.where(front, col_a, col_b) * freq_ref[1:2, :]
    for ref, value in ((cos_ref, jnp.cos(angle)), (sin_ref, jnp.sin(angle))):
        up = pltpu.roll(value, HEAD // 2, 1)
        down = pltpu.roll(value, width - HEAD // 2, 1)
        sign = -1.0 if ref is sin_ref else 1.0
        ref[:half, :] = jnp.where(front, sign * value, up)
        ref[half:, :] = jnp.where(front, sign * down, value)


def table_call(info, freqs, total):
    width = freqs.shape[1]
    tile = lambda c: pl.BlockSpec((TILE, c), lambda i, s: (i, 0))
    return pl.pallas_call(
        table_kernel,
        grid_spec=pltpu.PrefetchScalarGridSpec(
            num_scalar_prefetch=1,
            grid=(total // TILE,),
            in_specs=[pl.BlockSpec(freqs.shape, lambda i, s: (0, 0))],
            out_specs=[tile(width), tile(width), tile(PAIR), tile(PAIR), tile(PAIR)],
        ),
        out_shape=[
            jax.ShapeDtypeStruct((total, width), F32),
            jax.ShapeDtypeStruct((total, width), F32),
            jax.ShapeDtypeStruct((total, PAIR), BF16),
            jax.ShapeDtypeStruct((total, PAIR), BF16),
            jax.ShapeDtypeStruct((total, PAIR), F32),
        ],
        compiler_params=params(),
        cost_estimate=cost(9),
    )(info, freqs)


def qkv_kernel(
    place_ref, own_ref, other_ref, wa_ref, wb_ref, vec_ref, cos_ref, sin_ref, mk_ref,
    xh_ref, q_ref, k_ref, v_ref, kaug_ref, kt_ref, vt_ref, w_ref, wt_ref, *, depth,
):
    step = pl.program_id(0)
    half = pl.num_programs(0) // 2
    width = cos_ref.shape[1]

    @pl.when(step == 0)
    def _():
        if depth is None:
            w_ref[...] = wa_ref[...]
        else:
            core = place_ref[1]
            pieces = wa_ref.shape[0] // depth
            for m in range(pieces):
                at = (place_ref[2] ^ m) * (2 * depth)
                held = spot(m, 2 * pieces)
                rows = slice(held * depth, (held + 1) * depth)
                w_ref[pl.ds(pl.multiple_of(at + core * depth, 16), depth), :] = wa_ref[rows, :]
                w_ref[pl.ds(pl.multiple_of(at + (1 - core) * depth, 16), depth), :] = wb_ref[rows, :]
        wt_ref[...] = w_ref[...].T

    mine = (step // half) == place_ref[0]
    x = jnp.where(mine, own_ref[...].astype(F32), other_ref[...].astype(F32))
    mean = jnp.mean(x, axis=1, keepdims=True)
    cen = x - mean
    var = jnp.mean(cen * cen, axis=1, keepdims=True)
    xh = cen * lax.rsqrt(var + EPS)
    xh_ref[...] = xh.astype(BF16).T
    normed = (xh * vec_ref[GAIN_ONE] + vec_ref[SHIFT_ONE]).astype(BF16)
    mid = pl.ds(pl.multiple_of(place_ref[0] * width, PAIR), width)
    bias = jnp.concatenate([vec_ref[i : i + 1, mid] for i in range(3)], axis=1)
    proj = nn(normed, w_ref[...]) + bias
    c = cos_ref[...]
    s = sin_ref[...]
    q = proj[:, :width]
    k = proj[:, width : 2 * width]
    q = (q * c + swap_halves(q) * s).astype(BF16)
    k = (k * c + swap_halves(k) * s).astype(BF16)
    v = proj[:, 2 * width :].astype(BF16)
    q_ref[...] = (q.astype(F32) * 0.125).astype(BF16)
    k_ref[...] = k
    v_ref[...] = v
    kt_ref[...] = k.T
    vt_ref[...] = v.T
    mk = mk_ref[...]
    for h in range(width // HEAD):
        pair = h // 2
        kp = k[:, pair * PAIR : (pair + 1) * PAIR]
        kaug_ref[h] = jnp.where(head_lanes(kp.shape, h % 2), kp, mk)


def qkv_call(place, own, other, wa, wb, depth, vec, cos, sin, mk):
    rows, width = own.shape
    total = 2 * rows
    cols = wa.shape[1]
    third = cols // 3
    heads = third // HEAD
    per = rows // TILE
    last = per - 1
    whole = lambda i, s: (0, 0)
    tile = lambda c: pl.BlockSpec((TILE, c), lambda i, s: (i, 0))
    return pl.pallas_call(
        lambda *refs: qkv_kernel(*refs, depth=depth),
        grid_spec=pltpu.PrefetchScalarGridSpec(
            num_scalar_prefetch=1,
            grid=(total // TILE,),
            in_specs=[
                pl.BlockSpec((TILE, width), lambda i, s: (jnp.clip(i - per * s[0], 0, last), 0)),
                pl.BlockSpec((TILE, width), lambda i, s: (jnp.clip(i - per * (1 - s[0]), 0, last), 0)),
                pl.BlockSpec(wa.shape, whole),
                pl.BlockSpec(wb.shape, whole),
                pl.BlockSpec(vec.shape, whole),
                tile(third),
                tile(third),
                tile(PAIR),
            ],
            out_specs=[
                pl.BlockSpec((width, TILE), lambda i, s: (0, i)),
                tile(third),
                tile(third),
                tile(third),
                pl.BlockSpec((heads, TILE, PAIR), lambda i, s: (0, i, 0)),
                pl.BlockSpec((third, TILE), lambda i, s: (0, i)),
                pl.BlockSpec((third, TILE), lambda i, s: (0, i)),
                pl.BlockSpec((width, cols), whole),
                pl.BlockSpec((cols, width), whole),
            ],
        ),
        out_shape=[
            jax.ShapeDtypeStruct((width, total), BF16),
            jax.ShapeDtypeStruct((total, third), BF16),
            jax.ShapeDtypeStruct((total, third), BF16),
            jax.ShapeDtypeStruct((total, third), BF16),
            jax.ShapeDtypeStruct((heads, total, PAIR), BF16),
            jax.ShapeDtypeStruct((third, total), BF16),
            jax.ShapeDtypeStruct((third, total), BF16),
            jax.ShapeDtypeStruct((width, cols), BF16),
            jax.ShapeDtypeStruct((cols, width), BF16),
        ],
        compiler_params=params(),
        cost_estimate=cost(1),
    )(place, own, other, wa, wb, vec, cos, sin, mk)


def attend_kernel(base_ref, info_ref, q_ref, kaug_ref, vt_ref, mq_ref, out_ref, lse_ref, qaug, scores, acc):
    step = pl.program_id(0) + base_ref[0]
    width = out_ref.shape[1]
    heads = width // HEAD
    mq = mq_ref[...]
    for h in range(heads):
        pair = h // 2
        q = q_ref[:, pair * PAIR : (pair + 1) * PAIR]
        qaug[h] = jnp.where(head_lanes(q.shape, h % 2), q, mq)
    lo, hi = tile_bounds(info_ref, step, kaug_ref.shape[1])

    def first(kt, best):
        keys = pl.ds(pl.multiple_of(kt * TILE, TILE), TILE)
        out = []
        for h in range(heads):
            s = nt(kaug_ref[h, keys, :], qaug[h])
            scores[h, keys, :] = s
            out.append(jnp.maximum(best[h], jnp.max(s.reshape(TILE // 8, 8, TILE), axis=0)))
        return tuple(out)

    best = lax.fori_loop(lo, hi, first, tuple(jnp.full((8, TILE), -jnp.inf, F32) for _ in range(heads)))
    best = [jnp.max(b, axis=0, keepdims=True) for b in best]
    acc[...] = jnp.zeros_like(acc)

    def second(kt, sums):
        keys = pl.ds(pl.multiple_of(kt * TILE, TILE), TILE)
        out = []
        for h in range(heads):
            p = jnp.exp(scores[h, keys, :] - best[h])
            out.append(sums[h] + jnp.sum(p.reshape(TILE // 8, 8, TILE), axis=0))
            own = slice(h * HEAD, (h + 1) * HEAD)
            acc[own, :] += nn(vt_ref[own, keys], p.astype(BF16))
        return tuple(out)

    sums = lax.fori_loop(lo, hi, second, tuple(jnp.zeros((8, TILE), F32) for _ in range(heads)))
    lses = []
    outs = []
    for h in range(heads):
        tot = jnp.sum(sums[h], axis=0, keepdims=True)
        outs.append(acc[h * HEAD : (h + 1) * HEAD, :] / tot)
        lses.append(best[h] + jnp.log(tot))
    lses += [jnp.zeros_like(lses[0])] * (8 - heads)
    lse_ref[...] = jnp.concatenate(lses, axis=0)
    out_ref[...] = jnp.concatenate(outs, axis=0).T.astype(BF16)


def attend_call(base, info, q, kaug, vt, mq):
    total, width = q.shape
    heads = width // HEAD
    rows = total // 2
    whole = lambda i, b, s: (0, 0)
    return pl.pallas_call(
        attend_kernel,
        grid_spec=pltpu.PrefetchScalarGridSpec(
            num_scalar_prefetch=2,
            grid=(rows // TILE,),
            in_specs=[
                pl.BlockSpec((TILE, width), lambda i, b, s: (b[0] + i, 0)),
                pl.BlockSpec(kaug.shape, lambda i, b, s: (0, 0, 0)),
                pl.BlockSpec(vt.shape, whole),
                pl.BlockSpec((TILE, PAIR), lambda i, b, s: (b[0] + i, 0)),
            ],
            out_specs=[
                pl.BlockSpec((TILE, width), lambda i, b, s: (i, 0)),
                pl.BlockSpec((8, TILE), lambda i, b, s: (0, i)),
            ],
            scratch_shapes=[
                pltpu.VMEM((heads, TILE, PAIR), BF16),
                pltpu.VMEM((heads, total, TILE), F32),
                pltpu.VMEM((width, TILE), F32),
            ],
        ),
        out_shape=[
            jax.ShapeDtypeStruct((rows, width), BF16),
            jax.ShapeDtypeStruct((8, rows), F32),
        ],
        compiler_params=params(),
        cost_estimate=cost(4),
    )(base, info, q, kaug, vt, mq)


def phi_parts(x):
    cdf = 0.5 * (1.0 + lax.erf(x * 0.7071067811865476))
    pdf = jnp.exp(-0.5 * x * x) * 0.3989422804014327
    return cdf, pdf


def pre_kernel(place_ref, mine_ref, got_ref, x_ref, wo_ref, vec_ref, att_ref, res_ref, normed_ref):
    width = x_ref.shape[1]
    half = width // 2
    lanes = lambda at: pl.ds(pl.multiple_of(at * half, PAIR), half)
    att_ref[:, lanes(place_ref[0])] = mine_ref[...]
    att_ref[:, lanes(1 - place_ref[0])] = got_ref[...]
    wo = wo_ref[...].reshape(width, width)
    r = x_ref[...].astype(F32) + (nn(att_ref[...], wo) + vec_ref[OUT_BIAS])
    res_ref[...] = r
    cen = r - jnp.mean(r, axis=1, keepdims=True)
    var = jnp.mean(cen * cen, axis=1, keepdims=True)
    normed_ref[...] = (cen * lax.rsqrt(var + EPS) * vec_ref[GAIN_TWO] + vec_ref[SHIFT_TWO]).astype(BF16)


def pack_spec(packed, depth, width, at):
    if packed.shape[1] == width:
        return pl.BlockSpec((1, width, width), lambda j, s: (at(j), 0, 0))
    skip = packed.shape[1] % (5 * depth) // depth
    return pl.BlockSpec((packed.shape[0], depth, width), lambda j, s: (0, skip + at(j), 0))


def pre_call(place, mine, got, x, packed, depth, vec):
    rows, width = x.shape
    tile = lambda c: pl.BlockSpec((TILE, c), lambda j, s: (j, 0))
    return pl.pallas_call(
        pre_kernel,
        grid_spec=pltpu.PrefetchScalarGridSpec(
            num_scalar_prefetch=1,
            grid=(rows // TILE,),
            in_specs=[
                tile(width // 2),
                tile(width // 2),
                tile(width),
                pack_spec(packed, depth, width, lambda j: 0),
                pl.BlockSpec(vec.shape, lambda j, s: (0, 0)),
            ],
            out_specs=[tile(width), tile(width), tile(width)],
        ),
        out_shape=[
            jax.ShapeDtypeStruct((rows, width), BF16),
            jax.ShapeDtypeStruct((rows, width), F32),
            jax.ShapeDtypeStruct((rows, width), BF16),
        ],
        compiler_params=params(),
        cost_estimate=cost(30),
    )(place, mine, got, x, packed, vec)


def ffn_kernel(
    place_ref, att_ref, res_ref, normed_ref, cot_ref, wo_ref, wu_ref, *rest, chips,
):
    many = 2 * chips + 1
    down = rest[:many]
    (
        vec_ref, ub_ref,
        hid_ref, gres_ref, gatt_ref, gwp_ref, send_ref, keep_ref, gub_ref, sums_ref,
        acc, gacc, act, gup, wd_s,
    ) = rest[many:]
    step = pl.program_id(0)
    steps = pl.num_programs(0) - 1
    rows, width = res_ref.shape
    half = width // 2
    core = place_ref[1]
    chunks = [pl.ds(r, TILE) for r in range(0, rows, TILE)]
    lanes = lambda at: pl.ds(pl.multiple_of(at * half, PAIR), half)

    @pl.when(step == 0)
    def _():
        acc[...] = jnp.zeros_like(acc)
        gacc[...] = jnp.zeros_like(gacc)

    @pl.when(step < steps)
    def _():
        if chips:
            deep = width // (2 * chips)
            share = down[-1].shape[1]
            for t in range(2 * chips):
                wd_s[t * deep : t * deep + share, :] = down[-1][t]
            for t in range(chips):
                for r in (0, 1):
                    at = 2 * t * deep + (place_ref[0] ^ r) * deep + share
                    spot_rows = pl.ds(pl.multiple_of(at, 16), deep - share)
                    wd_s[spot_rows, lanes(core)] = down[t][r]
                    wd_s[spot_rows, lanes(1 - core)] = down[chips + t][r]
            wd_ref = wd_s
        else:
            wd_ref = down[0]
        bias_sum = jnp.zeros((1, ub_ref.shape[1]), F32)
        wu = wu_ref[...].reshape(width, width)
        for ch in chunks:
            up = nn(normed_ref[ch, :], wu) + ub_ref[...]
            cdf, pdf = phi_parts(up)
            a = (up * cdf).astype(BF16)
            act[ch, :] = a
            g = (nt(cot_ref[ch, :], wd_ref[...]) * (cdf + up * pdf)).astype(BF16)
            gup[ch, :] = g
            bias_sum += jnp.sum(g.astype(F32), axis=0, keepdims=True)
            acc[ch, :] += nn(a, wd_ref[...])
            gacc[ch, :] += nt(g, wu)
        gub_ref[...] = bias_sum
        send_ref[...] = tn(act[...], cot_ref[:, lanes(1 - core)]).astype(BF16)
        keep_ref[...] = tn(act[...], cot_ref[:, lanes(core)]).astype(BF16)
        gwp_ref[...] = tn(normed_ref[...], gup[...]).astype(BF16).reshape(gwp_ref.shape)

    @pl.when(step == steps)
    def _():
        zero = jnp.zeros((1, width), F32)
        s_out, s_down, s_gain, s_shift = zero, zero, zero, zero
        gain = vec_ref[GAIN_TWO]
        wo = wo_ref[...].reshape(width, width)
        for ch in chunks:
            r = res_ref[ch, :]
            hid_ref[ch, :] = (r + acc[ch, :] + vec_ref[DOWN_BIAS]).astype(BF16)
            cen = r - jnp.mean(r, axis=1, keepdims=True)
            rs = lax.rsqrt(jnp.mean(cen * cen, axis=1, keepdims=True) + EPS)
            xh = cen * rs
            e = gacc[ch, :]
            eg = e * gain
            cot = cot_ref[ch, :].astype(F32)
            g = cot + rs * (
                eg - jnp.mean(eg, axis=1, keepdims=True) - xh * jnp.mean(eg * xh, axis=1, keepdims=True)
            )
            gres_ref[ch, :] = g
            gb = g.astype(BF16)
            act[ch, :] = gb
            ga = nt(gb, wo).astype(BF16)
            gatt_ref[0, ch, :] = ga[:, :half]
            gatt_ref[1, ch, :] = ga[:, half:]
            s_out += jnp.sum(gb.astype(F32), axis=0, keepdims=True)
            s_down += jnp.sum(cot, axis=0, keepdims=True)
            s_gain += jnp.sum(e * xh, axis=0, keepdims=True)
            s_shift += jnp.sum(e, axis=0, keepdims=True)
        gwp_ref[...] = tn(att_ref[...], act[...]).astype(BF16).reshape(gwp_ref.shape)
        sums_ref[...] = jnp.concatenate([s_out, s_down, s_gain, s_shift] + [zero] * 4, axis=0)


def ffn_call(place, att, res, normed, cot, packed, depth, down_a, down_b, vec, ub):
    rows, width = res.shape
    half = width // 2
    hidden = ub.shape[1]
    steps = hidden // width
    last = steps - 1
    whole = lambda j, s: (0, 0)
    one = lambda r, c: pl.BlockSpec((r, c), whole)
    pack = lambda at: pack_spec(packed, depth, width, at)
    clip = lambda j: jnp.minimum(j, last)
    if down_b is None:
        chips = 0
        down = (down_a,)
        down_specs = [pl.BlockSpec((width, width), lambda j, s: (clip(j), 0))]
        grads = jax.ShapeDtypeStruct(packed.shape, BF16)
    else:
        count = packed.shape[0]
        share = packed.shape[1] - (steps + 1) * depth
        piece_rows = down_a.shape[3]
        chips = width * count // (2 * hidden)
        grads = jax.ShapeDtypeStruct((count, (steps + 1) * depth, width), BF16)

        def piece(t):
            def at(j, s):
                chip = (clip(j) * chips + t) ^ s[2]
                return (chip & 1, 0, chip >> 1, 0, 0)

            return pl.BlockSpec((pl.squeezed, 2, pl.squeezed, piece_rows, half), at)

        down_specs = [piece(t) for t in range(chips)] * 2
        down_specs.append(pl.BlockSpec((2 * chips, share, width), lambda j, s: (clip(j), 0, 0)))
        down = (down_a,) * chips + (down_b,) * chips + (packed,)
    return pl.pallas_call(
        lambda *refs: ffn_kernel(*refs, chips=chips),
        grid_spec=pltpu.PrefetchScalarGridSpec(
            num_scalar_prefetch=1,
            grid=(steps + 1,),
            in_specs=[
                one(rows, width),
                one(rows, width),
                one(rows, width),
                one(rows, width),
                pack(lambda j: 0),
                pack(lambda j: 1 + clip(j)),
                *down_specs,
                one(*vec.shape),
                pl.BlockSpec((1, width), lambda j, s: (0, clip(j))),
            ],
            out_specs=[
                one(rows, width),
                one(rows, width),
                pl.BlockSpec((2, rows, half), lambda j, s: (0, 0, 0)),
                pack_spec(grads, depth, width, lambda j: jnp.where(j < steps, 1 + j, 0)),
                pl.BlockSpec((width, half), lambda j, s: (clip(j), 0)),
                pl.BlockSpec((width, half), lambda j, s: (clip(j), 0)),
                pl.BlockSpec((1, width), lambda j, s: (0, clip(j))),
                one(8, width),
            ],
            scratch_shapes=[
                pltpu.VMEM((rows, width), F32),
                pltpu.VMEM((rows, width), F32),
                pltpu.VMEM((rows, width), BF16),
                pltpu.VMEM((rows, width), BF16),
                pltpu.VMEM((width, width), BF16),
            ],
        ),
        out_shape=[
            jax.ShapeDtypeStruct((rows, width), BF16),
            jax.ShapeDtypeStruct((rows, width), F32),
            jax.ShapeDtypeStruct((2, rows, half), BF16),
            grads,
            jax.ShapeDtypeStruct((hidden, half), BF16),
            jax.ShapeDtypeStruct((hidden, half), BF16),
            jax.ShapeDtypeStruct((1, hidden), F32),
            jax.ShapeDtypeStruct((8, width), F32),
        ],
        compiler_params=params(),
        cost_estimate=cost(38),
    )(place, att, res, normed, cot, packed, packed, *down, vec, ub)


def attend_back_kernel(base_ref, info_ref, do_ref, o_ref, lse_ref, q_ref, kaug_ref, kt_ref, v_ref, mq_ref, cos_ref, sin_ref, pos_ref, *rest, final, head):
    if final:
        k_ref, cos_all, sin_all, pos_all, dk_in, dv_in, gq_ref, gk_ref, gv_ref, sums_ref = rest[:10]
        qaug, qm, dom, dqt, delta, dk, dv = rest[10:]
    else:
        gq_ref, dk, dv, sums_ref = rest[:4]
        qaug, qm, dom, dqt, delta = rest[4:]
    step = pl.program_id(0)
    tile = step + base_ref[0]
    width = do_ref.shape[1]
    heads = width // HEAD
    pairs = heads // 2
    total = v_ref.shape[0]

    @pl.when(step == 0)
    def _():
        if final:
            dk[...] = dk_in[...]
            dv[...] = dv_in[...]
        else:
            dk[...] = jnp.zeros_like(dk)
            dv[...] = jnp.zeros_like(dv)
        sums_ref[...] = jnp.zeros_like(sums_ref)

    mq = mq_ref[...]
    for h in range(heads):
        pair = slice((h // 2) * PAIR, (h // 2 + 1) * PAIR)
        q = q_ref[:, pair]
        lanes = head_lanes(q.shape, h % 2)
        qaug[h] = jnp.where(lanes, q, mq)
        qm[h] = jnp.where(lanes, q, jnp.zeros_like(q))
        dom[h] = jnp.where(lanes, do_ref[:, pair], jnp.zeros_like(q))
    inner = do_ref[...].astype(F32) * o_ref[...].astype(F32)
    pick = (
        lax.broadcasted_iota(jnp.int32, (8, width), 1) // HEAD == lax.broadcasted_iota(jnp.int32, (8, width), 0)
    ).astype(F32)
    delta[...] = lax.dot_general(
        pick, inner, (((1,), (1,)), ((), ())), precision=lax.Precision.HIGHEST, preferred_element_type=F32
    )
    dqt[...] = jnp.zeros_like(dqt)

    def body(kt, carry):
        keys = pl.ds(pl.multiple_of(kt * TILE, TILE), TILE)
        for pr in range(pairs):
            pair = slice(pr * PAIR, (pr + 1) * PAIR)
            v = v_ref[keys, pair]
            dv_new = dv[keys, pair]
            dk_new = dk[keys, pair]
            for h in (2 * pr, 2 * pr + 1):
                own = slice(h * HEAD, (h + 1) * HEAD)
                s = nt(kaug_ref[h, keys, :], qaug[h])
                p = jnp.exp(s - lse_ref[head + h : head + h + 1, :])
                dp = nt(v, dom[h])
                ds = (p * (dp - delta[h : h + 1, :])).astype(BF16)
                dv_new += nn(p.astype(BF16), dom[h])
                dk_new += nn(ds, qm[h])
                dqt[own, :] += nn(kt_ref[own, keys], ds)
            dv[keys, pair] = dv_new
            dk[keys, pair] = dk_new
        return carry

    lo, hi = tile_bounds(info_ref, tile, total)
    lax.fori_loop(lo, hi, body, 0)

    def unrotate(u, c, s):
        return (u * c - swap_halves(u) * s).astype(BF16)

    def freq_sum(u, rot, pos):
        w = u * swap_halves(rot)
        sums_ref[3:4, :] += jnp.sum(w * pos[:, 0:1], axis=0, keepdims=True)
        sums_ref[4:5, :] += jnp.sum(w * pos[:, 1:2], axis=0, keepdims=True)

    dq = dqt[...].T * 0.125
    freq_sum(dq, q_ref[...].astype(F32) * 8.0, pos_ref[...])
    gq = unrotate(dq, cos_ref[...], sin_ref[...])
    gq_ref[...] = gq
    sums_ref[0:1, :] += jnp.sum(gq.astype(F32), axis=0, keepdims=True)

    if final:

        @pl.when(step == pl.num_programs(0) - 1)
        def _():
            for t in range(total // TILE):
                at = pl.ds(t * TILE, TILE)
                u = dk[at, :]
                freq_sum(u, k_ref[at, :].astype(F32), pos_all[at, :])
                gk = unrotate(u, cos_all[at, :], sin_all[at, :])
                gv = dv[at, :].astype(BF16)
                gk_ref[at, :] = gk
                gv_ref[at, :] = gv
                sums_ref[1:2, :] += jnp.sum(gk.astype(F32), axis=0, keepdims=True)
                sums_ref[2:3, :] += jnp.sum(gv.astype(F32), axis=0, keepdims=True)


def attend_back_call(base, info, do, o, lse, q, k, kaug, kt, v, mq, cos, sin, pos, first, pairs, held=None):
    total = q.shape[0]
    width = pairs * PAIR
    heads = 2 * pairs
    spot = first // pairs
    rows = total // 2
    final = held is not None
    here = lambda c: pl.BlockSpec((TILE, c), lambda i, b, s: (i, spot))
    there = lambda c: pl.BlockSpec((TILE, c), lambda i, b, s: (b[0] + i, spot))
    flat = lambda c: pl.BlockSpec((TILE, c), lambda i, b, s: (b[0] + i, 0))
    tall = pl.BlockSpec((total, width), lambda i, b, s: (0, spot))
    whole = lambda a: pl.BlockSpec(a.shape, lambda i, b, s: (0,) * len(a.shape))
    args = [do, o, lse, q, kaug, kt, v, mq, cos, sin, pos]
    in_specs = [
        here(width), here(width), pl.BlockSpec((8, TILE), lambda i, b, s: (0, i)), there(width),
        pl.BlockSpec((heads, total, PAIR), lambda i, b, s: (spot, 0, 0)),
        pl.BlockSpec((width, total), lambda i, b, s: (spot, 0)),
        tall, flat(PAIR), there(width), there(width), flat(PAIR),
    ]
    big = jax.ShapeDtypeStruct((total, width), F32)
    low = jax.ShapeDtypeStruct((total, width), BF16)
    sums = jax.ShapeDtypeStruct((8, width), F32)
    scratch = [
        pltpu.VMEM((heads, TILE, PAIR), BF16),
        pltpu.VMEM((heads, TILE, PAIR), BF16),
        pltpu.VMEM((heads, TILE, PAIR), BF16),
        pltpu.VMEM((width, TILE), F32),
        pltpu.VMEM((8, TILE), F32),
    ]
    if final:
        args += [k, cos, sin, pos, *held]
        in_specs += [tall, tall, tall, whole(pos), tall, tall]
        grads = [low, low]
        scratch += [pltpu.VMEM((total, width), F32), pltpu.VMEM((total, width), F32)]
    else:
        grads = [big, big]
    return pl.pallas_call(
        lambda *refs: attend_back_kernel(*refs, final=final, head=2 * first),
        grid_spec=pltpu.PrefetchScalarGridSpec(
            num_scalar_prefetch=2,
            grid=(rows // TILE,),
            in_specs=in_specs,
            out_specs=[pl.BlockSpec((TILE, width), lambda i, b, s: (i, 0)), whole(big), whole(big), whole(sums)],
            scratch_shapes=scratch,
        ),
        out_shape=[jax.ShapeDtypeStruct((rows, width), BF16), *grads, sums],
        compiler_params=params(),
        cost_estimate=cost(10 * pairs),
    )(base, info, *args)


def part_kernel(base_ref, *refs, lanes):
    w_ref, out_ref = refs[-2:]
    total = jnp.zeros(out_ref.shape, F32)
    for ref, at in zip(refs, lanes):
        total += nn(ref[...], w_ref[at : at + ref.shape[1], :])
    out_ref[...] = total.astype(out_ref.dtype)


def part_call(base, queries, keys, w, kind):
    rows = queries[0][0].shape[0]
    here = lambda c: pl.BlockSpec((TILE, c), lambda i, b: (i, 0))
    there = lambda c: pl.BlockSpec((TILE, c), lambda i, b: (b[0] + i, 0))
    arrays = [a for a, _ in queries + keys]
    lanes = [at for _, at in queries + keys]
    return pl.pallas_call(
        lambda *refs: part_kernel(*refs, lanes=lanes),
        grid_spec=pltpu.PrefetchScalarGridSpec(
            num_scalar_prefetch=1,
            grid=(rows // TILE,),
            in_specs=[here(a.shape[1]) for a, _ in queries]
            + [there(a.shape[1]) for a, _ in keys]
            + [pl.BlockSpec(w.shape, lambda i, b: (0, 0))],
            out_specs=pl.BlockSpec((TILE, w.shape[1]), lambda i, b: (i, 0)),
        ),
        out_shape=jax.ShapeDtypeStruct((rows, w.shape[1]), kind),
        compiler_params=params(),
        cost_estimate=cost(5.6),
    )(base, *arrays, w)


def weight_kernel(place_ref, xh_ref, own_ref, *rest, depth, lanes):
    keys = 3 * len(lanes)
    grads = rest[:keys]
    w_ref, col_ref, vec_ref = rest[keys : keys + 3]
    *outs, spare = rest[keys + 3 :]
    sums_ref = outs[-1]
    third = w_ref.shape[1] // 3
    rows = own_ref.shape[0]
    block = w_ref.shape[0]
    flat = vec_ref[:, pl.ds(pl.multiple_of(pl.program_id(0) * block, PAIR), block)].T
    gain = flat[:, GAIN_ONE]
    shift = flat[:, SHIFT_ONE]
    total = jnp.zeros(gain.shape, F32)
    bias = jnp.zeros(gain.shape, F32)
    half = lambda at: pl.ds(pl.multiple_of(at * rows, TILE), rows)
    for g, (lane, width) in enumerate(lanes):
        for i in range(3):
            ref = grads[3 * g + i]
            at = slice(i * third + lane, i * third + lane + width)
            if i:
                x = nn(xh_ref[...], ref[...])
            else:
                own = own_ref[:, lane : lane + width]
                x = nn(xh_ref[:, half(place_ref[0])], own) + nn(xh_ref[:, half(1 - place_ref[0])], ref[...])
            w = w_ref[:, at].astype(F32)
            col = col_ref[:, at]
            total += jnp.sum(x * w, axis=1, keepdims=True)
            bias += jnp.sum(w * col, axis=1, keepdims=True)
            spare[:, at] = (x * gain + shift * col).astype(BF16)
    lane = lax.broadcasted_iota(jnp.int32, (block, PAIR), 1)
    both = jnp.where(lane == 0, total, jnp.where(lane == 1, bias, 0.0))
    sums_ref[...] = both.T[:8, :]
    if depth is None:
        outs[0][...] = spare[...]
        return
    core = place_ref[1]
    for t in range(spare.shape[0] // (2 * depth)):
        at = 2 * t * depth
        rows = slice(t * depth, (t + 1) * depth)
        outs[0][rows, :] = spare[pl.ds(pl.multiple_of(at + (1 - core) * depth, 16), depth), :]
        outs[1][rows, :] = spare[pl.ds(pl.multiple_of(at + core * depth, 16), depth), :]


def weight_call(place, xh, own, grads, w, col, vec, depth, lanes):
    model, total = xh.shape
    cols = w.shape[1]
    block = model // 2
    whole = lambda a: pl.BlockSpec(a.shape, lambda i, s: (0, 0))
    if depth is None:
        out_shape = [jax.ShapeDtypeStruct((model, cols), BF16)]
        out_specs = [pl.BlockSpec((block, cols), lambda i, s: (i, 0))]
    else:
        out_shape = [jax.ShapeDtypeStruct((model // 2, cols), BF16)] * 2
        out_specs = [pl.BlockSpec((block // 2, cols), lambda i, s: (i, 0))] * 2
    return pl.pallas_call(
        lambda *refs: weight_kernel(*refs, depth=depth, lanes=lanes),
        grid_spec=pltpu.PrefetchScalarGridSpec(
            num_scalar_prefetch=1,
            grid=(model // block,),
            in_specs=[
                pl.BlockSpec((block, total), lambda i, s: (i, 0)),
                whole(own),
                *[whole(g) for g in grads],
                pl.BlockSpec((block, cols), lambda i, s: (i, 0)),
                whole(col),
                whole(vec),
            ],
            out_specs=out_specs + [pl.BlockSpec((8, block), lambda i, s: (0, i))],
            scratch_shapes=[pltpu.VMEM((block, cols), BF16)],
        ),
        out_shape=out_shape + [jax.ShapeDtypeStruct((8, model), F32)],
        compiler_params=params(),
        cost_estimate=cost(9),
    )(place, xh, own, *grads, w, col, vec)


def norm_back_kernel(x_ref, own_ref, got_ref, gres_ref, vec_ref, out_ref):
    x = x_ref[...].astype(F32)
    cen = x - jnp.mean(x, axis=1, keepdims=True)
    rs = lax.rsqrt(jnp.mean(cen * cen, axis=1, keepdims=True) + EPS)
    xh = cen * rs
    eg = (own_ref[...] + got_ref[...].astype(F32)) * vec_ref[GAIN_ONE]
    out_ref[...] = gres_ref[...] + rs * (
        eg - jnp.mean(eg, axis=1, keepdims=True) - xh * jnp.mean(eg * xh, axis=1, keepdims=True)
    )


def norm_back_call(x, own, got, gres, vec):
    rows, width = x.shape
    tile = pl.BlockSpec((TILE, width), lambda i: (i, 0))
    return pl.pallas_call(
        norm_back_kernel,
        grid=(rows // TILE,),
        in_specs=[tile, tile, tile, tile, pl.BlockSpec(vec.shape, lambda i: (0, 0))],
        out_specs=tile,
        out_shape=jax.ShapeDtypeStruct((rows, width), F32),
        compiler_params=params(),
        cost_estimate=cost(6),
    )(x, own, got, gres, vec)


def collect_kernel(place_ref, own_ref, far_a_ref, far_b_ref, up_ref, two_ref, one_ref, qkv_ref, down_ref, rest_ref, out_ref):
    width = out_ref.shape[1]
    half = own_ref.shape[1]
    lanes = pl.ds(pl.multiple_of(place_ref[0] * half, PAIR), half)
    sums = own_ref[...] + jnp.concatenate([far_a_ref[...], far_b_ref[...]], axis=1)
    out_ref[...] = jnp.zeros_like(out_ref)
    for row in range(3):
        out_ref[row : row + 1, lanes] = sums[row : row + 1, :]
    for row in range(up_ref.shape[1] // width):
        out_ref[3 + row : 4 + row, :] = up_ref[:, row * width : (row + 1) * width]
    for row in range(4):
        out_ref[7 + row : 8 + row, :] = two_ref[row : row + 1, :]
    for row in range(2):
        out_ref[11 + row : 12 + row, :] = one_ref[row : row + 1, :]
        out_ref[13 + row : 14 + row, lanes] = sums[3 + row : 4 + row, :]
    total = jnp.zeros((1, 1), F32)
    for ref, scale in ((qkv_ref, 1.0), (down_ref, 1.0), (rest_ref, 0.5)):
        v = ref[...].astype(F32)
        total += scale * jnp.sum(jnp.sum(v * v, axis=0, keepdims=True), axis=1, keepdims=True)
    lane = lax.broadcasted_iota(jnp.int32, (1, width), 1)
    out_ref[15:16, :] = jnp.where(lane == 0, total, 0.0)


def collect_call(place, *arrays):
    width = arrays[4].shape[1]
    whole = lambda a: pl.BlockSpec(a.shape, lambda i, s: (0, 0))
    return pl.pallas_call(
        collect_kernel,
        grid_spec=pltpu.PrefetchScalarGridSpec(
            num_scalar_prefetch=1,
            grid=(1,),
            in_specs=[whole(a) for a in arrays],
            out_specs=pl.BlockSpec((16, width), lambda i, s: (0, 0)),
        ),
        out_shape=jax.ShapeDtypeStruct((16, width), F32),
        compiler_params=params(),
        cost_estimate=cost(3),
    )(place, *arrays)


def finish_kernel(in_ref, qkv_ref, up_ref, *rest):
    vectors, freq_ref, norm_ref = rest[:-2], rest[-2], rest[-1]
    width = in_ref.shape[1]
    value = in_ref[...]
    for row in range(3):
        qkv_ref[pl.ds(row * width, width)] = value[row]
    for row in range(4):
        up_ref[pl.ds(row * width, width)] = value[3 + row]
    for row in range(6):
        vectors[row][...] = value[7 + row]
    turned = value[13:15]
    turned = jnp.concatenate([turned] * 4, axis=0)
    turned = pltpu.roll(turned, width - HEAD // 2, 1) - turned
    freq_ref[...] = turned
    lane = lax.broadcasted_iota(jnp.int32, (2, width), 1) % HEAD
    square = lambda u: jnp.sum(jnp.sum(u * u, axis=0, keepdims=True), axis=1, keepdims=True)
    freqs = square(jnp.where(lane < HEAD // 2, turned[:2], 0.0))
    main = square(value[:13]) + value[15:16, 0:1]
    at = lax.broadcasted_iota(jnp.int32, (8, PAIR), 1)
    norm_ref[...] = jnp.sqrt(jnp.where(at == 0, main, freqs))


def finish_call(value, hidden):
    width = value.shape[1]
    shapes = [(3 * width,), (hidden,)] + [(width,)] * 6 + [(8, width), (8, PAIR)]
    whole = lambda shape: pl.BlockSpec(shape, lambda: (0,) * len(shape))
    return pl.pallas_call(
        finish_kernel,
        in_specs=[whole(value.shape)],
        out_specs=[whole(shape) for shape in shapes],
        out_shape=[jax.ShapeDtypeStruct(shape, F32) for shape in shapes],
        compiler_params=params(),
        cost_estimate=cost(2),
    )(value)


def partners(count, mask):
    return [(i, i ^ mask) for i in range(count)]


def chip_groups(count):
    bits = count.bit_length() - 1
    groups = []
    at = 1
    while at < bits:
        size = 1 if at == 1 else min(2, bits - at)
        groups.append((at, size))
        at += size
    return groups


def spot(mask, count):
    at = 0
    scale = 1
    for low, size in chip_groups(count)[::-1]:
        at = at + ((mask >> (low - 1)) & ((1 << size) - 1)) * scale
        scale <<= size
    return at


def gather_parts(held, axis, count, group):
    low, size = group
    return [held] + [lax.ppermute(held, axis, partners(count, m << low)) for m in range(1, 1 << size)]


def gather_stage(held, axis, count, group):
    return jnp.concatenate(gather_parts(held, axis, count, group), axis=0)


def scatter_chips(held, axis, count, groups):
    index = lax.axis_index(axis)
    chips, rows, cols = held.shape
    for low, size in groups:
        span = 1 << size
        blocks = held.reshape((chips // span, span, rows, cols))
        me = (index >> low) & (span - 1)
        sums = lax.dynamic_index_in_dim(blocks, me, 1, False).astype(F32)
        for m in range(1, span):
            send = lax.dynamic_index_in_dim(blocks, me ^ m, 1, False)
            sums = sums + lax.ppermute(send, axis, partners(count, m << low)).astype(F32)
        chips //= span
        held = sums if chips == 1 else sums.astype(BF16)
    return held.reshape(rows, cols) if chips == 1 else held


def sum_over(value, count, held):
    axes = ("seq", "rows")
    bits = count.bit_length()
    at = 0
    while at < bits:
        size = min(2, bits - at)
        if at + size == bits:
            value, *held = lax.optimization_barrier((value, *held))
        got = [lax.ppermute(value, axes, partners(2 * count, m << at)) for m in range(1, 1 << size)]
        value = value + got[0]
        if size == 2:
            value = value + (got[1] + got[2])
        at += size
    return value, held


def after(value, *others):
    return lax.optimization_barrier((value,) + others)[0]


def body(
    patches, lengths, w_qkv, qkv_bias, w_out, out_bias, w_up, up_bias, w_down, down_bias,
    gain_one, shift_one, gain_two, shift_two, rope_freqs, cotangent,
):
    _, rows, width = patches.shape
    count = lax.axis_size("seq")
    index = lax.axis_index("seq")
    side = lax.axis_index("rows")
    flip = [(0, 1), (1, 0)]
    total = 2 * rows
    heads = rope_freqs.shape[1]
    half = width // 2
    hidden = up_bias.shape[0]
    depth = w_out.shape[0]
    deep = w_down.shape[0]
    direct = count == 16
    share = deep // 2
    blocks = hidden // width
    per = rows // TILE
    info = jnp.concatenate([jnp.stack([side, index % 2, index // 2]).astype(jnp.int32), lengths[0]])
    base_own = (side * per)[None].astype(jnp.int32)
    base_far = ((1 - side) * per)[None].astype(jnp.int32)
    vec = jnp.concatenate(
        [qkv_bias, out_bias, down_bias, gain_one, shift_one, gain_two, shift_two, jnp.zeros((7 * width,), BF16)]
    )
    vec = vec.astype(F32).reshape(16, width)
    up_row = up_bias.astype(F32)[None, :]

    x = patches[0]
    cot = cotangent[0]
    if direct:
        packed, own_cols = pack_call(info, w_down, w_out, w_up, w_qkv, share)
    else:
        packed = jnp.concatenate([w_out] + [w_up[:, c : c + width] for c in range(0, hidden, width)], axis=0)
        own_cols = lax.dynamic_index_in_dim(w_qkv.reshape(depth, 3, 2, half), side, 2, False).reshape(depth, 3 * half)
    own_freqs = lax.dynamic_slice_in_dim(rope_freqs, side * (heads // 2), heads // 2, 1)
    lane_freqs = jnp.concatenate([own_freqs, own_freqs], axis=-1).reshape(2, half)
    cos, sin, mq, mk, pos = table_call(info, lane_freqs, total)
    x_other = lax.ppermute(x, "rows", flip)
    core_pairs = partners(count, 1)
    if direct:
        near, far = chip_groups(count)
        down_got = lax.ppermute(
            lax.dynamic_slice_in_dim(w_down[share:], (1 - index % 2) * half, half, 1), "seq", core_pairs
        )
        down = lax.dynamic_slice_in_dim(w_down[share:], index % 2 * half, half, 1)
        down = jnp.where(index % 2 == side, down, down_got)
        qkv_a = gather_stage(own_cols[None], "seq", count, far)
        qkv_a, down, cos, sin, mq, mk, pos, vec, up_row = lax.optimization_barrier(
            (qkv_a, down, cos, sin, mq, mk, pos, vec, up_row)
        )
        down_parts = gather_parts(down[None], "seq", count, far)
        qkv_a = gather_stage(qkv_a, "seq", count, near)
        qkv_b = lax.ppermute(after(qkv_a, x_other), "seq", core_pairs)
        packed = lax.all_gather(packed, "seq", axis=0, tiled=False)
        qkv_a, qkv_b = qkv_a.reshape(-1, 3 * half), qkv_b.reshape(-1, 3 * half)
    else:
        packed = lax.all_gather(packed, "seq", axis=0, tiled=False)
        packed = packed.reshape(count, blocks + 1, depth, width).transpose(1, 0, 2, 3).reshape(blocks + 1, width, width)
        qkv_a = lax.all_gather(own_cols, "seq", axis=0, tiled=True)
        qkv_b = jnp.zeros((8, 3 * half), BF16)

    xh, q, k, v, kaug, kt, vt, w_own, w_turn = qkv_call(
        info, x, x_other, qkv_a, qkv_b, depth if direct else None, vec, cos, sin, mk
    )
    if direct:
        *down_parts, q = lax.optimization_barrier((*down_parts, q))
        down = jnp.concatenate(down_parts, axis=0)
        down_got = lax.ppermute(down, "rows", flip)
    att_far, lse_far = attend_call(base_far, info, q, kaug, vt, mq)
    att_got = lax.ppermute(att_far, "rows", flip)
    if direct:
        down, down_got, att_far = lax.optimization_barrier((down, down_got, att_far))
        down = jnp.stack([down, down_got], axis=0)[None]
        down = gather_stage(down, "seq", count, near)
    att_own, lse_own = attend_call(base_own, info, after(q, att_far), kaug, vt, mq)

    if direct:
        down_a = after(down, att_own)
        down_b = lax.ppermute(down_a, "seq", core_pairs)
    else:
        down_a, down_b = lax.all_gather(w_down, "seq", axis=0, tiled=True), None
    att, res, normed = pre_call(info, att_own, att_got, x, packed, depth, vec)
    hid, gres, gatt, gwp, gwd_send, gwd_keep, gub, sums_two = ffn_call(
        info, att, res, normed, cot, packed, depth, down_a, down_b, vec, up_row
    )
    do_own = lax.dynamic_index_in_dim(gatt, side, 0, False)
    do_send = lax.dynamic_index_in_dim(gatt, 1 - side, 0, False)
    do_far = lax.ppermute(do_send, "rows", flip)

    if not direct:
        gwp = gwp.reshape(blocks + 1, count, depth, width).transpose(1, 0, 2, 3)
    shard_p = lax.psum_scatter(gwp.reshape(-1, width), "seq", scatter_dimension=0, tiled=True)

    gwd_got = lax.ppermute(gwd_send, "seq", core_pairs)

    back = (q, k, kaug, kt, v, mq, cos, sin, pos)
    all_pairs = half // PAIR
    gq_own, dk, dv, sums_own = attend_back_call(base_own, info, do_own, att_own, lse_own, *back, 0, all_pairs)
    gwd_got, gq_own, do_far = lax.optimization_barrier((gwd_got, gq_own, do_far))
    gwd = (gwd_keep.astype(F32) + gwd_got.astype(F32)).astype(BF16).reshape(count // 2, 2, deep, half)
    gwd_keep = lax.dynamic_index_in_dim(gwd, side, 1, False)
    gwd_got = lax.ppermute(lax.dynamic_index_in_dim(gwd, 1 - side, 1, False), "rows", flip)

    queries, keys, sums_far, grads, lanes = [], [], [], [], []
    for step, (first, pairs) in enumerate(((0, 2), (2, 1))):
        lane = first * PAIR
        gq, gk, gv, sums = attend_back_call(
            base_far, info, do_far, att_far, lse_far, *back, first, pairs, held=(dk, dv)
        )
        if step == 0:
            gwd_got, gq, dk = lax.optimization_barrier((gwd_got, gq, dk))
            gwd = (gwd_keep.astype(F32) + gwd_got.astype(F32)).astype(BF16)
            gwd = scatter_chips(gwd, "seq", count, chip_groups(count)[:1])
        else:
            gwd, gq = lax.optimization_barrier((gwd, gq))
            gwd = scatter_chips(gwd, "seq", count, chip_groups(count)[1:]).astype(BF16)
        queries.append((gq, lane))
        keys += [(gk, half + lane), (gv, 2 * half + lane)]
        sums_far.append(sums)
        grads += [gq, gk, gv]
        lanes.append((lane, pairs * PAIR))
    col = (sums_own[:3] + jnp.concatenate(sums_far, axis=1)[:3]).reshape(1, 3 * half)
    part_far = part_call(base_far, queries, keys, w_turn, BF16)
    part_got = lax.ppermute(part_far, "rows", flip)
    shard_got = lax.ppermute(shard_p, "rows", flip)
    xh = after(xh, part_far)
    *gw, sums_one = weight_call(info, xh, gq_own, grads, w_own, col, vec, depth if direct else None, lanes)
    if not direct:
        gw = gw[0].reshape(count // 2, 2, depth, 3 * half)
        gw = [lax.dynamic_index_in_dim(gw, c, 1, False).reshape(-1, 3 * half) for c in (1 - index % 2, index % 2)]
    gw_got = lax.ppermute(gw[0], "seq", core_pairs)
    gw = (gw[1].astype(F32) + gw_got.astype(F32)).astype(BF16).reshape(count // 2, depth, 3 * half)
    gw = after(gw, shard_p)
    shard_own = scatter_chips(gw, "seq", count, chip_groups(count)).astype(BF16)
    shard_far = lax.ppermute(shard_own, "rows", flip)
    own_keys = [(gq_own, 0)]
    part_own = part_call(base_own, own_keys, keys, after(w_turn, sums_one), F32)
    patch_grad = norm_back_call(x, part_own, part_got, gres, vec)

    swaps = []
    for mask in (0, 1):
        swaps.append([(2 * i + r, 2 * (i - i % 2 + r) + ((i % 2) ^ mask)) for i in range(count) for r in range(2)])
    same_half, other_half = (lax.ppermute(after(gwd, shard_own), ("seq", "rows"), p) for p in swaps)
    shard_p = shard_p.astype(F32) + shard_got.astype(F32)
    shard_out = shard_p[:depth]
    shard_up = jnp.concatenate([shard_p[(1 + c) * depth : (2 + c) * depth] for c in range(blocks)], axis=1)
    small = collect_call(info, sums_own, *sums_far, gub, sums_two, sums_one, after(shard_own, patch_grad), gwd, shard_p)
    small, (shard_far, same_half, other_half) = sum_over(small, count, (shard_far, same_half, other_half))
    first = jnp.where(side == 0, shard_own, shard_far).reshape(depth, 3, 1, half)
    second = jnp.where(side == 0, shard_far, shard_own).reshape(depth, 3, 1, half)
    shard_qkv = jnp.concatenate([first, second], axis=2).reshape(depth, 6 * half).astype(F32)

    low = side == 0
    shard_down = jnp.concatenate(
        [jnp.where(low, same_half, other_half), jnp.where(low, other_half, same_half)], axis=1
    ).astype(F32)

    s_qkv, s_up, s_out, s_down, s_gain2, s_shift2, s_gain1, s_shift1, freqs, norms = finish_call(small, hidden)
    freqs = freqs[:2].reshape(2, heads, HEAD)[:, :, : HEAD // 2]
    return (
        hid[None],
        patch_grad[None],
        shard_qkv,
        s_qkv,
        shard_out,
        s_out,
        shard_up,
        s_up,
        shard_down,
        s_down,
        s_gain1,
        s_shift1,
        s_gain2,
        s_shift2,
        freqs,
        norms[0, 0],
        norms[0, 1],
    )


def solution(mesh):
    in_specs = (
        P("seq", "rows", None),
        P("seq", None),
        P("seq", None),
        P(),
        P("seq", None),
        P(),
        P("seq", None),
        P(),
        P("seq", None),
        P(),
        P(),
        P(),
        P(),
        P(),
        P(),
        P("seq", "rows", None),
    )
    out_specs = (
        P("seq", "rows", None),
        P("seq", "rows", None),
        P("seq", None),
        P(),
        P("seq", None),
        P(),
        P("seq", None),
        P(),
        P("seq", None),
        P(),
        P(),
        P(),
        P(),
        P(),
        P(),
        P(),
        P(),
    )
    return jax.shard_map(body, mesh=mesh, in_specs=in_specs, out_specs=out_specs, check_vma=False)
```

```python
import jax
import jax.numpy as jnp
from jax import lax
from jax.experimental import pallas as pl
from jax.experimental.pallas import tpu as pltpu
from jax.sharding import PartitionSpec as P

SIDE_S = 14
SIDE_M = 20
SIDE_L = 24
EPS = 1e-06
NEG = -1e30
HEAD = 64
PAIR = 128
TILE = 256
F32 = jnp.float32
BF16 = jnp.bfloat16
OUT_BIAS, DOWN_BIAS, GAIN_ONE, SHIFT_ONE, GAIN_TWO, SHIFT_TWO = (slice(r, r + 1) for r in range(3, 9))


def cost(us):
    return pl.CostEstimate(flops=int(us * 1150000000), bytes_accessed=10**5, transcendentals=0)


def params(mib):
    return pltpu.CompilerParams(vmem_limit_bytes=mib * 1024 * 1024)


def nn(a, b):
    return lax.dot_general(a, b, (((1,), (0,)), ((), ())), preferred_element_type=F32)


def nt(a, b):
    return lax.dot_general(a, b, (((1,), (1,)), ((), ())), preferred_element_type=F32)


def tn(a, b):
    return lax.dot_general(a, b, (((0,), (0,)), ((), ())), preferred_element_type=F32)


def swap_halves(u):
    width = u.shape[-1]
    lane = lax.broadcasted_iota(jnp.int32, u.shape, 1) % HEAD
    return jnp.where(
        lane < HEAD // 2,
        pltpu.roll(u, width - HEAD // 2, 1),
        pltpu.roll(u, HEAD // 2, 1),
    )


def head_lanes(shape, odd):
    lane = lax.broadcasted_iota(jnp.int32, shape, 1)
    return (lane >= HEAD) if odd else (lane < HEAD)


def tile_bounds(info_ref, tile, total):
    first = tile * TILE
    last = first + TILE - 1
    run = jnp.int32(0)
    low = jnp.int32(-1)
    high = jnp.int32(total)
    for s in range(3, info_ref.shape[0]):
        end = run + info_ref[s]
        low = jnp.where((first >= run) & (first < end), run, low)
        high = jnp.where((last >= run) & (last < end), end, high)
        run = end
    low = jnp.where(low < 0, run, low)
    return lax.div(low, TILE), lax.div(high + (TILE - 1), TILE)


def pack_kernel(info_ref, down_ref, out_ref, up_ref, qkv_ref, packed_ref, cols_ref):
    depth, width = out_ref.shape
    half = width // 2
    share = packed_ref.shape[0] - depth * (1 + up_ref.shape[1] // width)
    packed_ref[:share, :] = down_ref[:share, :]
    packed_ref[share : share + depth, :] = out_ref[...]
    for c in range(up_ref.shape[1] // width):
        at = share + (c + 1) * depth
        packed_ref[at : at + depth, :] = up_ref[:, c * width : (c + 1) * width]
    for i in range(3):
        at = pl.multiple_of(i * width + info_ref[0] * half, PAIR)
        cols_ref[:, i * half : (i + 1) * half] = qkv_ref[:, pl.ds(at, half)]


def pack_call(info, w_down, w_out, w_up, w_qkv, share):
    depth, width = w_out.shape
    whole = lambda r, c: pl.BlockSpec((r, c), lambda i, s: (0, 0))
    length = share + depth * (w_up.shape[1] // width + 1)
    arrays = (w_down, w_out, w_up, w_qkv)
    return pl.pallas_call(
        pack_kernel,
        grid_spec=pltpu.PrefetchScalarGridSpec(
            num_scalar_prefetch=1,
            grid=(1,),
            in_specs=[whole(*a.shape) for a in arrays],
            out_specs=[whole(length, width), whole(depth, 3 * width // 2)],
        ),
        out_shape=[
            jax.ShapeDtypeStruct((length, width), BF16),
            jax.ShapeDtypeStruct((depth, 3 * width // 2), BF16),
        ],
        compiler_params=params(60),
        cost_estimate=cost(2.5),
    )(info, *arrays)


def table_kernel(info_ref, freq_ref, cos_ref, sin_ref, mq_ref, mk_ref, pos_ref):
    step = pl.program_id(0)
    slots = info_ref.shape[0] - 3

    def place(shape):
        at = lax.broadcasted_iota(jnp.int32, shape, 0) + step * TILE
        block = jnp.full(shape, slots, jnp.int32)
        offset = jnp.zeros(shape, jnp.int32)
        side = jnp.ones(shape, F32)
        run = jnp.int32(0)
        for s in range(slots):
            count = info_ref[3 + s]
            inside = (at >= run) & (at < run + count)
            width = jnp.where(count == SIDE_S * SIDE_S, SIDE_S, jnp.where(count == SIDE_M * SIDE_M, SIDE_M, SIDE_L))
            block = jnp.where(inside, s, block)
            offset = jnp.where(inside, at - run, offset)
            side = jnp.where(inside, width.astype(F32), side)
            run = run + count
        offset = offset.astype(F32)
        row = jnp.floor((offset + 0.5) / side)
        return block, row, offset - row * side

    block, row, col = place((TILE, PAIR))
    lane = lax.broadcasted_iota(jnp.int32, (TILE, PAIR), 1)
    slot = lane % HEAD
    same = slot == block
    mk_ref[...] = same.astype(F32).astype(BF16)
    mq_ref[...] = jnp.where(same | (slot > slots), 0.0, NEG).astype(BF16)
    pos_ref[...] = jnp.where(lane == 0, row, jnp.where(lane == 1, col, 0.0))
    half = TILE // 2
    width = cos_ref.shape[1]
    front = lax.broadcasted_iota(jnp.int32, (half, width), 1) % HEAD < HEAD // 2
    both = lambda u: (u[:half, 0:1], u[half:, 0:1])
    row_a, row_b = both(row)
    col_a, col_b = both(col)
    angle = jnp.where(front, row_a, row_b) * freq_ref[0:1, :] + jnp.where(front, col_a, col_b) * freq_ref[1:2, :]
    for ref, value in ((cos_ref, jnp.cos(angle)), (sin_ref, jnp.sin(angle))):
        up = pltpu.roll(value, HEAD // 2, 1)
        down = pltpu.roll(value, width - HEAD // 2, 1)
        sign = -1.0 if ref is sin_ref else 1.0
        ref[:half, :] = jnp.where(front, sign * value, up)
        ref[half:, :] = jnp.where(front, sign * down, value)


def table_call(info, freqs, total):
    width = freqs.shape[1]
    tile = lambda c: pl.BlockSpec((TILE, c), lambda i, s: (i, 0))
    return pl.pallas_call(
        table_kernel,
        grid_spec=pltpu.PrefetchScalarGridSpec(
            num_scalar_prefetch=1,
            grid=(total // TILE,),
            in_specs=[pl.BlockSpec(freqs.shape, lambda i, s: (0, 0))],
            out_specs=[tile(width), tile(width), tile(PAIR), tile(PAIR), tile(PAIR)],
        ),
        out_shape=[
            jax.ShapeDtypeStruct((total, width), F32),
            jax.ShapeDtypeStruct((total, width), F32),
            jax.ShapeDtypeStruct((total, PAIR), BF16),
            jax.ShapeDtypeStruct((total, PAIR), BF16),
            jax.ShapeDtypeStruct((total, PAIR), F32),
        ],
        compiler_params=params(60),
        cost_estimate=cost(9),
    )(info, freqs)


def qkv_kernel(
    place_ref, own_ref, other_ref, wa_ref, wb_ref, vec_ref, cos_ref, sin_ref, mk_ref,
    xh_ref, q_ref, k_ref, v_ref, kaug_ref, kt_ref, vt_ref, w_ref, wt_ref, *, depth,
):
    step = pl.program_id(0)
    half = pl.num_programs(0) // 2
    width = cos_ref.shape[1]

    @pl.when(step == 0)
    def _():
        if depth is None:
            w_ref[...] = wa_ref[...]
        else:
            core = place_ref[1]
            pieces = wa_ref.shape[0] // depth
            for m in range(pieces):
                at = (place_ref[2] ^ m) * (2 * depth)
                held = spot(m, 2 * pieces)
                rows = slice(held * depth, (held + 1) * depth)
                w_ref[pl.ds(pl.multiple_of(at + core * depth, 16), depth), :] = wa_ref[rows, :]
                w_ref[pl.ds(pl.multiple_of(at + (1 - core) * depth, 16), depth), :] = wb_ref[rows, :]
        wt_ref[...] = w_ref[...].T

    mine = (step // half) == place_ref[0]
    x = jnp.where(mine, own_ref[...].astype(F32), other_ref[...].astype(F32))
    mean = jnp.mean(x, axis=1, keepdims=True)
    cen = x - mean
    var = jnp.mean(cen * cen, axis=1, keepdims=True)
    xh = cen * lax.rsqrt(var + EPS)
    xh_ref[...] = xh.astype(BF16).T
    normed = (xh * vec_ref[GAIN_ONE] + vec_ref[SHIFT_ONE]).astype(BF16)
    mid = pl.ds(pl.multiple_of(place_ref[0] * width, PAIR), width)
    bias = jnp.concatenate([vec_ref[i : i + 1, mid] for i in range(3)], axis=1)
    proj = nn(normed, w_ref[...]) + bias
    c = cos_ref[...]
    s = sin_ref[...]
    q = proj[:, :width]
    k = proj[:, width : 2 * width]
    q = (q * c + swap_halves(q) * s).astype(BF16)
    k = (k * c + swap_halves(k) * s).astype(BF16)
    v = proj[:, 2 * width :].astype(BF16)
    q_ref[...] = (q.astype(F32) * 0.125).astype(BF16)
    k_ref[...] = k
    v_ref[...] = v
    kt_ref[...] = k.T
    vt_ref[...] = v.T
    mk = mk_ref[...]
    for h in range(width // HEAD):
        pair = h // 2
        kp = k[:, pair * PAIR : (pair + 1) * PAIR]
        kaug_ref[h] = jnp.where(head_lanes(kp.shape, h % 2), kp, mk)


def qkv_call(place, own, other, wa, wb, depth, vec, cos, sin, mk):
    rows, width = own.shape
    total = 2 * rows
    cols = wa.shape[1]
    third = cols // 3
    heads = third // HEAD
    per = rows // TILE
    last = per - 1
    whole = lambda i, s: (0, 0)
    tile = lambda c: pl.BlockSpec((TILE, c), lambda i, s: (i, 0))
    return pl.pallas_call(
        lambda *refs: qkv_kernel(*refs, depth=depth),
        grid_spec=pltpu.PrefetchScalarGridSpec(
            num_scalar_prefetch=1,
            grid=(total // TILE,),
            in_specs=[
                pl.BlockSpec((TILE, width), lambda i, s: (jnp.clip(i - per * s[0], 0, last), 0)),
                pl.BlockSpec((TILE, width), lambda i, s: (jnp.clip(i - per * (1 - s[0]), 0, last), 0)),
                pl.BlockSpec(wa.shape, whole),
                pl.BlockSpec(wb.shape, whole),
                pl.BlockSpec(vec.shape, whole),
                tile(third),
                tile(third),
                tile(PAIR),
            ],
            out_specs=[
                pl.BlockSpec((width, TILE), lambda i, s: (0, i)),
                tile(third),
                tile(third),
                tile(third),
                pl.BlockSpec((heads, TILE, PAIR), lambda i, s: (0, i, 0)),
                pl.BlockSpec((third, TILE), lambda i, s: (0, i)),
                pl.BlockSpec((third, TILE), lambda i, s: (0, i)),
                pl.BlockSpec((width, cols), whole),
                pl.BlockSpec((cols, width), whole),
            ],
        ),
        out_shape=[
            jax.ShapeDtypeStruct((width, total), BF16),
            jax.ShapeDtypeStruct((total, third), BF16),
            jax.ShapeDtypeStruct((total, third), BF16),
            jax.ShapeDtypeStruct((total, third), BF16),
            jax.ShapeDtypeStruct((heads, total, PAIR), BF16),
            jax.ShapeDtypeStruct((third, total), BF16),
            jax.ShapeDtypeStruct((third, total), BF16),
            jax.ShapeDtypeStruct((width, cols), BF16),
            jax.ShapeDtypeStruct((cols, width), BF16),
        ],
        compiler_params=params(60),
        cost_estimate=cost(1),
    )(place, own, other, wa, wb, vec, cos, sin, mk)


def attend_kernel(base_ref, info_ref, q_ref, kaug_ref, vt_ref, mq_ref, out_ref, lse_ref, qaug, scores, acc):
    step = pl.program_id(0) + base_ref[0]
    width = out_ref.shape[1]
    heads = width // HEAD
    mq = mq_ref[...]
    for h in range(heads):
        pair = h // 2
        q = q_ref[:, pair * PAIR : (pair + 1) * PAIR]
        qaug[h] = jnp.where(head_lanes(q.shape, h % 2), q, mq)
    lo, hi = tile_bounds(info_ref, step, kaug_ref.shape[1])

    def first(kt, best):
        keys = pl.ds(pl.multiple_of(kt * TILE, TILE), TILE)
        out = []
        for h in range(heads):
            s = nt(kaug_ref[h, keys, :], qaug[h])
            scores[h, keys, :] = s
            out.append(jnp.maximum(best[h], jnp.max(s.reshape(TILE // 8, 8, TILE), axis=0)))
        return tuple(out)

    best = lax.fori_loop(lo, hi, first, tuple(jnp.full((8, TILE), -jnp.inf, F32) for _ in range(heads)))
    best = [jnp.max(b, axis=0, keepdims=True) for b in best]
    acc[...] = jnp.zeros_like(acc)

    def second(kt, sums):
        keys = pl.ds(pl.multiple_of(kt * TILE, TILE), TILE)
        out = []
        for h in range(heads):
            p = jnp.exp(scores[h, keys, :] - best[h])
            out.append(sums[h] + jnp.sum(p.reshape(TILE // 8, 8, TILE), axis=0))
            own = slice(h * HEAD, (h + 1) * HEAD)
            acc[own, :] += nn(vt_ref[own, keys], p.astype(BF16))
        return tuple(out)

    sums = lax.fori_loop(lo, hi, second, tuple(jnp.zeros((8, TILE), F32) for _ in range(heads)))
    lses = []
    outs = []
    for h in range(heads):
        tot = jnp.sum(sums[h], axis=0, keepdims=True)
        outs.append(acc[h * HEAD : (h + 1) * HEAD, :] / tot)
        lses.append(best[h] + jnp.log(tot))
    lses += [jnp.zeros_like(lses[0])] * (8 - heads)
    lse_ref[...] = jnp.concatenate(lses, axis=0)
    out_ref[...] = jnp.concatenate(outs, axis=0).T.astype(BF16)


def attend_call(base, info, q, kaug, vt, mq):
    total, width = q.shape
    heads = width // HEAD
    rows = total // 2
    whole = lambda i, b, s: (0, 0)
    return pl.pallas_call(
        attend_kernel,
        grid_spec=pltpu.PrefetchScalarGridSpec(
            num_scalar_prefetch=2,
            grid=(rows // TILE,),
            in_specs=[
                pl.BlockSpec((TILE, width), lambda i, b, s: (b[0] + i, 0)),
                pl.BlockSpec(kaug.shape, lambda i, b, s: (0, 0, 0)),
                pl.BlockSpec(vt.shape, whole),
                pl.BlockSpec((TILE, PAIR), lambda i, b, s: (b[0] + i, 0)),
            ],
            out_specs=[
                pl.BlockSpec((TILE, width), lambda i, b, s: (i, 0)),
                pl.BlockSpec((8, TILE), lambda i, b, s: (0, i)),
            ],
            scratch_shapes=[
                pltpu.VMEM((heads, TILE, PAIR), BF16),
                pltpu.VMEM((heads, total, TILE), F32),
                pltpu.VMEM((width, TILE), F32),
            ],
        ),
        out_shape=[
            jax.ShapeDtypeStruct((rows, width), BF16),
            jax.ShapeDtypeStruct((8, rows), F32),
        ],
        compiler_params=params(60),
        cost_estimate=cost(4),
    )(base, info, q, kaug, vt, mq)


def phi_parts(x):
    cdf = 0.5 * (1.0 + lax.erf(x * 0.7071067811865476))
    pdf = jnp.exp(-0.5 * x * x) * 0.3989422804014327
    return cdf, pdf


def pre_kernel(place_ref, mine_ref, got_ref, x_ref, wo_ref, vec_ref, att_ref, res_ref, normed_ref):
    width = x_ref.shape[1]
    half = width // 2
    lanes = lambda at: pl.ds(pl.multiple_of(at * half, PAIR), half)
    att_ref[:, lanes(place_ref[0])] = mine_ref[...]
    att_ref[:, lanes(1 - place_ref[0])] = got_ref[...]
    wo = wo_ref[...].reshape(width, width)
    r = x_ref[...].astype(F32) + (nn(att_ref[...], wo) + vec_ref[OUT_BIAS])
    res_ref[...] = r
    cen = r - jnp.mean(r, axis=1, keepdims=True)
    var = jnp.mean(cen * cen, axis=1, keepdims=True)
    normed_ref[...] = (cen * lax.rsqrt(var + EPS) * vec_ref[GAIN_TWO] + vec_ref[SHIFT_TWO]).astype(BF16)


def pack_spec(packed, depth, width, at):
    if packed.shape[1] == width:
        return pl.BlockSpec((1, width, width), lambda j, s: (at(j), 0, 0))
    skip = packed.shape[1] % (5 * depth) // depth
    return pl.BlockSpec((packed.shape[0], depth, width), lambda j, s: (0, skip + at(j), 0))


def pre_call(place, mine, got, x, packed, depth, vec):
    rows, width = x.shape
    tile = lambda c: pl.BlockSpec((TILE, c), lambda j, s: (j, 0))
    return pl.pallas_call(
        pre_kernel,
        grid_spec=pltpu.PrefetchScalarGridSpec(
            num_scalar_prefetch=1,
            grid=(rows // TILE,),
            in_specs=[
                tile(width // 2),
                tile(width // 2),
                tile(width),
                pack_spec(packed, depth, width, lambda j: 0),
                pl.BlockSpec(vec.shape, lambda j, s: (0, 0)),
            ],
            out_specs=[tile(width), tile(width), tile(width)],
        ),
        out_shape=[
            jax.ShapeDtypeStruct((rows, width), BF16),
            jax.ShapeDtypeStruct((rows, width), F32),
            jax.ShapeDtypeStruct((rows, width), BF16),
        ],
        compiler_params=params(60),
        cost_estimate=cost(30),
    )(place, mine, got, x, packed, vec)


def ffn_kernel(
    place_ref, att_ref, res_ref, normed_ref, cot_ref, wo_ref, wu_ref, *rest, chips,
):
    many = 2 * chips + 1
    down = rest[:many]
    (
        vec_ref, ub_ref,
        hid_ref, gres_ref, gown_ref, gfar_ref, gwp_ref, send_ref, keep_ref, gub_ref, sums_ref,
        acc, gacc, act, gup, wd_s,
    ) = rest[many:]
    step = pl.program_id(0)
    steps = pl.num_programs(0) - 1
    rows, width = res_ref.shape
    half = width // 2
    core = place_ref[1]
    chunks = [pl.ds(r, TILE) for r in range(0, rows, TILE)]
    lanes = lambda at: pl.ds(pl.multiple_of(at * half, PAIR), half)

    @pl.when(step == 0)
    def _():
        acc[...] = jnp.zeros_like(acc)
        gacc[...] = jnp.zeros_like(gacc)

    @pl.when(step < steps)
    def _():
        if chips:
            deep = width // (2 * chips)
            share = down[-1].shape[1]
            for t in range(2 * chips):
                wd_s[t * deep : t * deep + share, :] = down[-1][t]
            for t in range(chips):
                for r in (0, 1):
                    at = 2 * t * deep + (place_ref[0] ^ r) * deep + share
                    spot_rows = pl.ds(pl.multiple_of(at, 16), deep - share)
                    wd_s[spot_rows, lanes(core)] = down[t][r]
                    wd_s[spot_rows, lanes(1 - core)] = down[chips + t][r]
            wd_ref = wd_s
        else:
            wd_ref = down[0]
        bias_sum = jnp.zeros((1, ub_ref.shape[1]), F32)
        wu = wu_ref[...].reshape(width, width)
        for ch in chunks:
            up = nn(normed_ref[ch, :], wu) + ub_ref[...]
            cdf, pdf = phi_parts(up)
            a = (up * cdf).astype(BF16)
            act[ch, :] = a
            g = (nt(cot_ref[ch, :], wd_ref[...]) * (cdf + up * pdf)).astype(BF16)
            gup[ch, :] = g
            bias_sum += jnp.sum(g.astype(F32), axis=0, keepdims=True)
            acc[ch, :] += nn(a, wd_ref[...])
            gacc[ch, :] += nt(g, wu)
        gub_ref[...] = bias_sum
        send_ref[...] = tn(act[...], cot_ref[:, lanes(1 - core)]).astype(BF16)
        keep_ref[...] = tn(act[...], cot_ref[:, lanes(core)]).astype(BF16)
        gwp_ref[...] = tn(normed_ref[...], gup[...]).astype(BF16).reshape(gwp_ref.shape)

    @pl.when(step == steps)
    def _():
        zero = jnp.zeros((1, width), F32)
        s_out, s_down, s_gain, s_shift = zero, zero, zero, zero
        gain = vec_ref[GAIN_TWO]
        wo = wo_ref[...].reshape(width, width)
        for ch in chunks:
            r = res_ref[ch, :]
            hid_ref[ch, :] = (r + acc[ch, :] + vec_ref[DOWN_BIAS]).astype(BF16)
            cen = r - jnp.mean(r, axis=1, keepdims=True)
            rs = lax.rsqrt(jnp.mean(cen * cen, axis=1, keepdims=True) + EPS)
            xh = cen * rs
            e = gacc[ch, :]
            eg = e * gain
            cot = cot_ref[ch, :].astype(F32)
            g = cot + rs * (
                eg - jnp.mean(eg, axis=1, keepdims=True) - xh * jnp.mean(eg * xh, axis=1, keepdims=True)
            )
            gres_ref[ch, :] = g
            gb = g.astype(BF16)
            act[ch, :] = gb
            gup[ch, :] = nt(gb, wo).astype(BF16)
            gown_ref[ch, :] = gup[ch, lanes(place_ref[0])]
            gfar_ref[ch, :] = gup[ch, lanes(1 - place_ref[0])]
            s_out += jnp.sum(gb.astype(F32), axis=0, keepdims=True)
            s_down += jnp.sum(cot, axis=0, keepdims=True)
            s_gain += jnp.sum(e * xh, axis=0, keepdims=True)
            s_shift += jnp.sum(e, axis=0, keepdims=True)
        gwp_ref[...] = tn(att_ref[...], act[...]).astype(BF16).reshape(gwp_ref.shape)
        sums_ref[...] = jnp.concatenate([s_out, s_down, s_gain, s_shift] + [zero] * 4, axis=0)


def ffn_call(place, att, res, normed, cot, packed, depth, down_a, down_b, vec, ub):
    rows, width = res.shape
    half = width // 2
    hidden = ub.shape[1]
    steps = hidden // width
    last = steps - 1
    whole = lambda j, s: (0, 0)
    held = pl.BlockSpec(memory_space=pltpu.VMEM)
    one = lambda r, c: pl.BlockSpec((r, c), whole)
    pack = lambda at: pack_spec(packed, depth, width, at)
    clip = lambda j: jnp.minimum(j, last)
    if down_b is None:
        chips = 0
        down = (down_a,)
        down_specs = [pl.BlockSpec((width, width), lambda j, s: (clip(j), 0))]
        grads = jax.ShapeDtypeStruct(packed.shape, BF16)
    else:
        count = packed.shape[0]
        share = packed.shape[1] - (steps + 1) * depth
        piece_rows = down_a.shape[3]
        chips = width * count // (2 * hidden)
        grads = jax.ShapeDtypeStruct((count, (steps + 1) * depth, width), BF16)

        def piece(t):
            def at(j, s):
                chip = (clip(j) * chips + t) ^ s[2]
                return (chip & 1, 0, chip >> 1, 0, 0)

            return pl.BlockSpec((pl.squeezed, 2, pl.squeezed, piece_rows, half), at)

        down_specs = [piece(t) for t in range(chips)] * 2
        down_specs.append(pl.BlockSpec((2 * chips, share, width), lambda j, s: (clip(j), 0, 0)))
        down = (down_a,) * chips + (down_b,) * chips + (packed,)
    return pl.pallas_call(
        lambda *refs: ffn_kernel(*refs, chips=chips),
        grid_spec=pltpu.PrefetchScalarGridSpec(
            num_scalar_prefetch=1,
            grid=(steps + 1,),
            in_specs=[
                one(rows, width),
                one(rows, width),
                one(rows, width),
                one(rows, width),
                pack(lambda j: 0),
                pack(lambda j: 1 + clip(j)),
                *down_specs,
                one(*vec.shape),
                pl.BlockSpec((1, width), lambda j, s: (0, clip(j))),
            ],
            out_specs=[
                one(rows, width),
                one(rows, width),
                one(rows, half),
                one(rows, half),
                pack_spec(grads, depth, width, lambda j: jnp.where(j < steps, 1 + j, 0)),
                pl.BlockSpec((width, half), lambda j, s: (clip(j), 0)),
                pl.BlockSpec((width, half), lambda j, s: (clip(j), 0)),
                pl.BlockSpec((1, width), lambda j, s: (0, clip(j))),
                one(8, width),
            ],
            scratch_shapes=[
                pltpu.VMEM((rows, width), F32),
                pltpu.VMEM((rows, width), F32),
                pltpu.VMEM((rows, width), BF16),
                pltpu.VMEM((rows, width), BF16),
                pltpu.VMEM((width, width), BF16),
            ],
        ),
        out_shape=[
            jax.ShapeDtypeStruct((rows, width), BF16),
            jax.ShapeDtypeStruct((rows, width), F32),
            jax.ShapeDtypeStruct((rows, half), BF16),
            jax.ShapeDtypeStruct((rows, half), BF16),
            grads,
            jax.ShapeDtypeStruct((hidden, half), BF16),
            jax.ShapeDtypeStruct((hidden, half), BF16),
            jax.ShapeDtypeStruct((1, hidden), F32),
            jax.ShapeDtypeStruct((8, width), F32),
        ],
        compiler_params=params(60),
        cost_estimate=cost(38),
    )(place, att, res, normed, cot, packed, packed, *down, vec, ub)


def attend_back_kernel(base_ref, info_ref, do_ref, o_ref, lse_ref, q_ref, kaug_ref, kt_ref, v_ref, mq_ref, cos_ref, sin_ref, pos_ref, *rest, final, head):
    if final:
        k_ref, cos_all, sin_all, pos_all, dk_in, dv_in, gq_ref, gk_ref, gv_ref, sums_ref = rest[:10]
        qaug, qm, dom, dqt, delta, s_scr, dp_scr, p_scr, ds_scr, dk, dv = rest[10:]
    else:
        gq_ref, dk, dv, sums_ref = rest[:4]
        qaug, qm, dom, dqt, delta, s_scr, dp_scr, p_scr, ds_scr = rest[4:]
    step = pl.program_id(0)
    tile = step + base_ref[0]
    width = do_ref.shape[1]
    heads = width // HEAD
    pairs = heads // 2
    total = v_ref.shape[0]

    @pl.when(step == 0)
    def _():
        if final:
            dk[...] = dk_in[...]
            dv[...] = dv_in[...]
        else:
            dk[...] = jnp.zeros_like(dk)
            dv[...] = jnp.zeros_like(dv)
        sums_ref[...] = jnp.zeros_like(sums_ref)

    mq = mq_ref[...]
    for h in range(heads):
        pair = slice((h // 2) * PAIR, (h // 2 + 1) * PAIR)
        q = q_ref[:, pair]
        lanes = head_lanes(q.shape, h % 2)
        qaug[h] = jnp.where(lanes, q, mq)
        qm[h * TILE : (h + 1) * TILE, :] = jnp.where(lanes, q, jnp.zeros_like(q))
        dom[h * TILE : (h + 1) * TILE, :] = jnp.where(lanes, do_ref[:, pair], jnp.zeros_like(q))
    inner = do_ref[...].astype(F32) * o_ref[...].astype(F32)
    pick = (
        lax.broadcasted_iota(jnp.int32, (8, width), 1) // HEAD == lax.broadcasted_iota(jnp.int32, (8, width), 0)
    ).astype(F32)
    delta[...] = lax.dot_general(
        pick, inner, (((1,), (1,)), ((), ())), precision=lax.Precision.HIGHEST, preferred_element_type=F32
    )
    dqt[...] = jnp.zeros_like(dqt)

    def body(kt, carry):
        keys = pl.ds(pl.multiple_of(kt * TILE, TILE), TILE)
        for h in range(heads):
            s_scr[h] = nt(kaug_ref[h, keys, :], qaug[h])
            dp_scr[h] = nt(v_ref[keys, (h // 2) * PAIR : (h // 2 + 1) * PAIR], dom[h * TILE : (h + 1) * TILE, :])
        for h in range(heads):
            at = slice((h % 2) * TILE, (h % 2 + 1) * TILE)
            p = jnp.exp(s_scr[h] - lse_ref[head + h : head + h + 1, :])
            p_scr[h // 2, :, at] = p.astype(BF16)
            ds_scr[h // 2, :, at] = (p * (dp_scr[h] - delta[h : h + 1, :])).astype(BF16)
        for pr in range(pairs):
            pair = slice(pr * PAIR, (pr + 1) * PAIR)
            both = slice(2 * pr * TILE, 2 * (pr + 1) * TILE)
            dv[keys, pair] += nn(p_scr[pr], dom[both, :])
            dk[keys, pair] += nn(ds_scr[pr], qm[both, :])
            for e in (0, 1):
                own = slice((2 * pr + e) * HEAD, (2 * pr + e + 1) * HEAD)
                dqt[own, :] += nn(kt_ref[own, keys], ds_scr[pr, :, e * TILE : (e + 1) * TILE])
        return carry

    lo, hi = tile_bounds(info_ref, tile, total)
    lax.fori_loop(lo, hi, body, 0)

    def unrotate(u, c, s):
        return (u * c - swap_halves(u) * s).astype(BF16)

    def freq_sum(u, rot, pos):
        w = u * swap_halves(rot)
        sums_ref[3:4, :] += jnp.sum(w * pos[:, 0:1], axis=0, keepdims=True)
        sums_ref[4:5, :] += jnp.sum(w * pos[:, 1:2], axis=0, keepdims=True)

    dq = dqt[...].T * 0.125
    freq_sum(dq, q_ref[...].astype(F32) * 8.0, pos_ref[...])
    gq = unrotate(dq, cos_ref[...], sin_ref[...])
    gq_ref[...] = gq
    sums_ref[0:1, :] += jnp.sum(gq.astype(F32), axis=0, keepdims=True)

    if final:

        @pl.when(step == pl.num_programs(0) - 1)
        def _():
            for t in range(total // TILE):
                at = pl.ds(t * TILE, TILE)
                u = dk[at, :]
                freq_sum(u, k_ref[at, :].astype(F32), pos_all[at, :])
                gk = unrotate(u, cos_all[at, :], sin_all[at, :])
                gv = dv[at, :].astype(BF16)
                gk_ref[at, :] = gk
                gv_ref[at, :] = gv
                sums_ref[1:2, :] += jnp.sum(gk.astype(F32), axis=0, keepdims=True)
                sums_ref[2:3, :] += jnp.sum(gv.astype(F32), axis=0, keepdims=True)


def attend_back_call(base, info, do, o, lse, q, k, kaug, kt, v, mq, cos, sin, pos, first, pairs, held=None):
    total = q.shape[0]
    width = pairs * PAIR
    heads = 2 * pairs
    spot = first // pairs
    rows = total // 2
    final = held is not None
    here = lambda c: pl.BlockSpec((TILE, c), lambda i, b, s: (i, spot))
    there = lambda c: pl.BlockSpec((TILE, c), lambda i, b, s: (b[0] + i, spot))
    flat = lambda c: pl.BlockSpec((TILE, c), lambda i, b, s: (b[0] + i, 0))
    tall = pl.BlockSpec((total, width), lambda i, b, s: (0, spot))
    held_in = pl.BlockSpec(memory_space=pltpu.VMEM)
    whole = lambda a: pl.BlockSpec(a.shape, lambda i, b, s: (0,) * len(a.shape))
    args = [do, o, lse, q, kaug, kt, v, mq, cos, sin, pos]
    in_specs = [
        here(width), here(width), pl.BlockSpec((8, TILE), lambda i, b, s: (0, i)), there(width),
        pl.BlockSpec((heads, total, PAIR), lambda i, b, s: (spot, 0, 0)),
        pl.BlockSpec((width, total), lambda i, b, s: (spot, 0)),
        tall, flat(PAIR), there(width), there(width), flat(PAIR),
    ]
    big = jax.ShapeDtypeStruct((total, width), F32)
    low = jax.ShapeDtypeStruct((total, width), BF16)
    sums = jax.ShapeDtypeStruct((8, width), F32)
    scratch = [
        pltpu.VMEM((heads, TILE, PAIR), BF16),
        pltpu.VMEM((heads * TILE, PAIR), BF16),
        pltpu.VMEM((heads * TILE, PAIR), BF16),
        pltpu.VMEM((width, TILE), F32),
        pltpu.VMEM((8, TILE), F32),
        pltpu.VMEM((heads, TILE, TILE), F32),
        pltpu.VMEM((heads, TILE, TILE), F32),
        pltpu.VMEM((pairs, TILE, 2 * TILE), BF16),
        pltpu.VMEM((pairs, TILE, 2 * TILE), BF16),
    ]
    if final:
        args += [k, cos, sin, pos, *held]
        in_specs += [tall, tall, tall, whole(pos), held_in, held_in]
        grads = [low, low]
        scratch += [pltpu.VMEM((total, width), F32), pltpu.VMEM((total, width), F32)]
    else:
        grads = [big, big]
    return pl.pallas_call(
        lambda *refs: attend_back_kernel(*refs, final=final, head=2 * first),
        grid_spec=pltpu.PrefetchScalarGridSpec(
            num_scalar_prefetch=2,
            grid=(rows // TILE,),
            in_specs=in_specs,
            out_specs=[pl.BlockSpec((TILE, width), lambda i, b, s: (i, 0)), held_in, held_in, whole(sums)],
            scratch_shapes=scratch,
        ),
        out_shape=[jax.ShapeDtypeStruct((rows, width), BF16), *grads, sums],
        compiler_params=params(50),
        cost_estimate=cost(10 * pairs),
    )(base, info, *args)


def part_kernel(base_ref, *refs, lanes):
    w_ref, out_ref = refs[-2:]
    total = jnp.zeros(out_ref.shape, F32)
    for ref, at in zip(refs, lanes):
        total += nn(ref[...], w_ref[at : at + ref.shape[1], :])
    out_ref[...] = total.astype(out_ref.dtype)


def part_call(base, queries, keys, w, kind):
    rows = queries[0][0].shape[0]
    here = lambda c: pl.BlockSpec((TILE, c), lambda i, b: (i, 0))
    there = lambda c: pl.BlockSpec((TILE, c), lambda i, b: (b[0] + i, 0))
    arrays = [a for a, _ in queries + keys]
    lanes = [at for _, at in queries + keys]
    return pl.pallas_call(
        lambda *refs: part_kernel(*refs, lanes=lanes),
        grid_spec=pltpu.PrefetchScalarGridSpec(
            num_scalar_prefetch=1,
            grid=(rows // TILE,),
            in_specs=[here(a.shape[1]) for a, _ in queries]
            + [there(a.shape[1]) for a, _ in keys]
            + [pl.BlockSpec(w.shape, lambda i, b: (0, 0))],
            out_specs=pl.BlockSpec((TILE, w.shape[1]), lambda i, b: (i, 0)),
        ),
        out_shape=jax.ShapeDtypeStruct((rows, w.shape[1]), kind),
        compiler_params=params(10),
        cost_estimate=cost(5.6),
    )(base, *arrays, w)


def weight_kernel(place_ref, xh_ref, own_ref, *rest, depth, lanes):
    keys = 3 * len(lanes)
    grads = rest[:keys]
    w_ref, col_ref, vec_ref = rest[keys : keys + 3]
    *outs, spare = rest[keys + 3 :]
    sums_ref = outs[-1]
    third = w_ref.shape[1] // 3
    rows = own_ref.shape[0]
    block = w_ref.shape[0]
    flat = vec_ref[:, pl.ds(pl.multiple_of(pl.program_id(0) * block, PAIR), block)].T
    gain = flat[:, GAIN_ONE]
    shift = flat[:, SHIFT_ONE]
    total = jnp.zeros(gain.shape, F32)
    bias = jnp.zeros(gain.shape, F32)
    half = lambda at: pl.ds(pl.multiple_of(at * rows, TILE), rows)
    for g, (lane, width) in enumerate(lanes):
        for i in range(3):
            ref = grads[3 * g + i]
            at = slice(i * third + lane, i * third + lane + width)
            if i:
                x = nn(xh_ref[...], ref[...])
            else:
                own = own_ref[:, lane : lane + width]
                x = nn(xh_ref[:, half(place_ref[0])], own) + nn(xh_ref[:, half(1 - place_ref[0])], ref[...])
            w = w_ref[:, at].astype(F32)
            col = col_ref[:, at]
            total += jnp.sum(x * w, axis=1, keepdims=True)
            bias += jnp.sum(w * col, axis=1, keepdims=True)
            spare[:, at] = (x * gain + shift * col).astype(BF16)
    lane = lax.broadcasted_iota(jnp.int32, (block, PAIR), 1)
    both = jnp.where(lane == 0, total, jnp.where(lane == 1, bias, 0.0))
    sums_ref[...] = both.T[:8, :]
    if depth is None:
        outs[0][...] = spare[...]
        return
    core = place_ref[1]
    for t in range(spare.shape[0] // (2 * depth)):
        at = 2 * t * depth
        rows = slice(t * depth, (t + 1) * depth)
        outs[0][rows, :] = spare[pl.ds(pl.multiple_of(at + (1 - core) * depth, 16), depth), :]
        outs[1][rows, :] = spare[pl.ds(pl.multiple_of(at + core * depth, 16), depth), :]


def weight_call(place, xh, own, grads, w, col, vec, depth, lanes):
    model, total = xh.shape
    cols = w.shape[1]
    block = model // 2
    whole = lambda a: pl.BlockSpec(a.shape, lambda i, s: (0, 0))
    if depth is None:
        out_shape = [jax.ShapeDtypeStruct((model, cols), BF16)]
        out_specs = [pl.BlockSpec((block, cols), lambda i, s: (i, 0))]
    else:
        out_shape = [jax.ShapeDtypeStruct((model // 2, cols), BF16)] * 2
        out_specs = [pl.BlockSpec((block // 2, cols), lambda i, s: (i, 0))] * 2
    return pl.pallas_call(
        lambda *refs: weight_kernel(*refs, depth=depth, lanes=lanes),
        grid_spec=pltpu.PrefetchScalarGridSpec(
            num_scalar_prefetch=1,
            grid=(model // block,),
            in_specs=[
                pl.BlockSpec((block, total), lambda i, s: (i, 0)),
                whole(own),
                *[whole(g) for g in grads],
                pl.BlockSpec((block, cols), lambda i, s: (i, 0)),
                whole(col),
                whole(vec),
            ],
            out_specs=out_specs + [pl.BlockSpec((8, block), lambda i, s: (0, i))],
            scratch_shapes=[pltpu.VMEM((block, cols), BF16)],
        ),
        out_shape=out_shape + [jax.ShapeDtypeStruct((8, model), F32)],
        compiler_params=params(16),
        cost_estimate=cost(9),
    )(place, xh, own, *grads, w, col, vec)


def norm_back_kernel(x_ref, own_ref, got_ref, gres_ref, vec_ref, out_ref):
    x = x_ref[...].astype(F32)
    cen = x - jnp.mean(x, axis=1, keepdims=True)
    rs = lax.rsqrt(jnp.mean(cen * cen, axis=1, keepdims=True) + EPS)
    xh = cen * rs
    eg = (own_ref[...] + got_ref[...].astype(F32)) * vec_ref[GAIN_ONE]
    out_ref[...] = gres_ref[...] + rs * (
        eg - jnp.mean(eg, axis=1, keepdims=True) - xh * jnp.mean(eg * xh, axis=1, keepdims=True)
    )


def norm_back_call(x, own, got, gres, vec):
    rows, width = x.shape
    tile = pl.BlockSpec((TILE, width), lambda i: (i, 0))
    return pl.pallas_call(
        norm_back_kernel,
        grid=(rows // TILE,),
        in_specs=[tile, tile, tile, tile, pl.BlockSpec(vec.shape, lambda i: (0, 0))],
        out_specs=tile,
        out_shape=jax.ShapeDtypeStruct((rows, width), F32),
        compiler_params=params(56),
        cost_estimate=cost(6),
    )(x, own, got, gres, vec)


def collect_kernel(place_ref, own_ref, far_ref, up_ref, two_ref, one_ref, qkv_ref, down_ref, rest_ref, out_ref):
    width = out_ref.shape[1]
    half = own_ref.shape[1]
    lanes = pl.ds(pl.multiple_of(place_ref[0] * half, PAIR), half)
    sums = own_ref[...] + far_ref[...]
    out_ref[...] = jnp.zeros_like(out_ref)
    for row in range(3):
        out_ref[row : row + 1, lanes] = sums[row : row + 1, :]
    for row in range(up_ref.shape[1] // width):
        out_ref[3 + row : 4 + row, :] = up_ref[:, row * width : (row + 1) * width]
    for row in range(4):
        out_ref[7 + row : 8 + row, :] = two_ref[row : row + 1, :]
    for row in range(2):
        out_ref[11 + row : 12 + row, :] = one_ref[row : row + 1, :]
        out_ref[13 + row : 14 + row, lanes] = sums[3 + row : 4 + row, :]
    total = jnp.zeros((1, 1), F32)
    for ref, scale in ((qkv_ref, 1.0), (down_ref, 1.0), (rest_ref, 0.5)):
        v = ref[...].astype(F32)
        total += scale * jnp.sum(jnp.sum(v * v, axis=0, keepdims=True), axis=1, keepdims=True)
    lane = lax.broadcasted_iota(jnp.int32, (1, width), 1)
    out_ref[15:16, :] = jnp.where(lane == 0, total, 0.0)


def collect_call(place, *arrays):
    width = arrays[3].shape[1]
    whole = lambda a: pl.BlockSpec(a.shape, lambda i, s: (0, 0))
    return pl.pallas_call(
        collect_kernel,
        grid_spec=pltpu.PrefetchScalarGridSpec(
            num_scalar_prefetch=1,
            grid=(1,),
            in_specs=[whole(a) for a in arrays],
            out_specs=pl.BlockSpec((16, width), lambda i, s: (0, 0)),
        ),
        out_shape=jax.ShapeDtypeStruct((16, width), F32),
        compiler_params=params(6),
        cost_estimate=cost(3),
    )(place, *arrays)


def finish_kernel(in_ref, qkv_ref, up_ref, *rest):
    vectors, freq_ref, norm_ref = rest[:-2], rest[-2], rest[-1]
    width = in_ref.shape[1]
    value = in_ref[...]
    for row in range(3):
        qkv_ref[pl.ds(row * width, width)] = value[row]
    for row in range(4):
        up_ref[pl.ds(row * width, width)] = value[3 + row]
    for row in range(6):
        vectors[row][...] = value[7 + row]
    turned = value[13:15]
    turned = jnp.concatenate([turned] * 4, axis=0)
    turned = pltpu.roll(turned, width - HEAD // 2, 1) - turned
    freq_ref[...] = turned
    lane = lax.broadcasted_iota(jnp.int32, (2, width), 1) % HEAD
    square = lambda u: jnp.sum(jnp.sum(u * u, axis=0, keepdims=True), axis=1, keepdims=True)
    freqs = square(jnp.where(lane < HEAD // 2, turned[:2], 0.0))
    main = square(value[:13]) + value[15:16, 0:1]
    at = lax.broadcasted_iota(jnp.int32, (8, PAIR), 1)
    norm_ref[...] = jnp.sqrt(jnp.where(at == 0, main, freqs))


def finish_call(value, hidden):
    width = value.shape[1]
    shapes = [(3 * width,), (hidden,)] + [(width,)] * 6 + [(8, width), (8, PAIR)]
    whole = lambda shape: pl.BlockSpec(shape, lambda: (0,) * len(shape))
    return pl.pallas_call(
        finish_kernel,
        in_specs=[whole(value.shape)],
        out_specs=[whole(shape) for shape in shapes],
        out_shape=[jax.ShapeDtypeStruct(shape, F32) for shape in shapes],
        compiler_params=params(2),
        cost_estimate=cost(2),
    )(value)


def partners(count, mask):
    return [(i, i ^ mask) for i in range(count)]


def chip_groups(count):
    bits = count.bit_length() - 1
    groups = []
    at = 1
    while at < bits:
        size = 1 if at == 1 else min(2, bits - at)
        groups.append((at, size))
        at += size
    return groups


def spot(mask, count):
    at = 0
    scale = 1
    for low, size in chip_groups(count)[::-1]:
        at = at + ((mask >> (low - 1)) & ((1 << size) - 1)) * scale
        scale <<= size
    return at


def gather_parts(held, axis, count, group):
    low, size = group
    return [held] + [lax.ppermute(held, axis, partners(count, m << low)) for m in range(1, 1 << size)]


def gather_stage(held, axis, count, group):
    return jnp.concatenate(gather_parts(held, axis, count, group), axis=0)


def scatter_chips(held, axis, count, groups):
    index = lax.axis_index(axis)
    chips, rows, cols = held.shape
    for low, size in groups:
        span = 1 << size
        blocks = held.reshape((chips // span, span, rows, cols))
        me = (index >> low) & (span - 1)
        sums = lax.dynamic_index_in_dim(blocks, me, 1, False).astype(F32)
        for m in range(1, span):
            send = lax.dynamic_index_in_dim(blocks, me ^ m, 1, False)
            sums = sums + lax.ppermute(send, axis, partners(count, m << low)).astype(F32)
        chips //= span
        held = sums if chips == 1 else sums.astype(BF16)
    return held.reshape(rows, cols) if chips == 1 else held


def sum_over(value, count, held):
    axes = ("seq", "rows")
    bits = count.bit_length()
    at = 0
    while at < bits:
        size = min(2, bits - at)
        if at + size == bits:
            value, *held = lax.optimization_barrier((value, *held))
        got = [lax.ppermute(value, axes, partners(2 * count, m << at)) for m in range(1, 1 << size)]
        value = value + got[0]
        if size == 2:
            value = value + (got[1] + got[2])
        at += size
    return value, held


def after(value, *others):
    return lax.optimization_barrier((value,) + others)[0]


def body(
    patches, lengths, w_qkv, qkv_bias, w_out, out_bias, w_up, up_bias, w_down, down_bias,
    gain_one, shift_one, gain_two, shift_two, rope_freqs, cotangent,
):
    _, rows, width = patches.shape
    count = lax.axis_size("seq")
    index = lax.axis_index("seq")
    side = lax.axis_index("rows")
    flip = [(0, 1), (1, 0)]
    total = 2 * rows
    heads = rope_freqs.shape[1]
    half = width // 2
    hidden = up_bias.shape[0]
    depth = w_out.shape[0]
    deep = w_down.shape[0]
    direct = count == 16
    share = deep // 2
    blocks = hidden // width
    per = rows // TILE
    info = jnp.concatenate([jnp.stack([side, index % 2, index // 2]).astype(jnp.int32), lengths[0]])
    base_own = (side * per)[None].astype(jnp.int32)
    base_far = ((1 - side) * per)[None].astype(jnp.int32)
    vec = jnp.concatenate(
        [qkv_bias, out_bias, down_bias, gain_one, shift_one, gain_two, shift_two, jnp.zeros((7 * width,), BF16)]
    )
    vec = vec.astype(F32).reshape(16, width)
    up_row = up_bias.astype(F32)[None, :]

    x = patches[0]
    cot = cotangent[0]
    if direct:
        packed, own_cols = pack_call(info, w_down, w_out, w_up, w_qkv, share)
    else:
        packed = jnp.concatenate([w_out] + [w_up[:, c : c + width] for c in range(0, hidden, width)], axis=0)
        own_cols = lax.dynamic_index_in_dim(w_qkv.reshape(depth, 3, 2, half), side, 2, False).reshape(depth, 3 * half)
    own_freqs = lax.dynamic_slice_in_dim(rope_freqs, side * (heads // 2), heads // 2, 1)
    lane_freqs = jnp.concatenate([own_freqs, own_freqs], axis=-1).reshape(2, half)
    cos, sin, mq, mk, pos = table_call(info, lane_freqs, total)
    x_other = lax.ppermute(x, "rows", flip)
    core_pairs = partners(count, 1)
    if direct:
        near, far = chip_groups(count)
        down_got = lax.ppermute(
            lax.dynamic_slice_in_dim(w_down[share:], (1 - index % 2) * half, half, 1), "seq", core_pairs
        )
        down = lax.dynamic_slice_in_dim(w_down[share:], index % 2 * half, half, 1)
        down = jnp.where(index % 2 == side, down, down_got)
        qkv_a = gather_stage(own_cols[None], "seq", count, far)
        qkv_a, down = lax.optimization_barrier((qkv_a, down))
        down_parts = gather_parts(down[None], "seq", count, far)
        qkv_a = gather_stage(qkv_a, "seq", count, near)
        qkv_a, x_other, cos, sin, mq, mk, pos, vec, up_row = lax.optimization_barrier(
            (qkv_a, x_other, cos, sin, mq, mk, pos, vec, up_row)
        )
        qkv_b = lax.ppermute(qkv_a, "seq", core_pairs)
        packed = lax.all_gather(packed, "seq", axis=0, tiled=False)
        qkv_a, qkv_b = qkv_a.reshape(-1, 3 * half), qkv_b.reshape(-1, 3 * half)
    else:
        packed = lax.all_gather(packed, "seq", axis=0, tiled=False)
        packed = packed.reshape(count, blocks + 1, depth, width).transpose(1, 0, 2, 3).reshape(blocks + 1, width, width)
        qkv_a = lax.all_gather(own_cols, "seq", axis=0, tiled=True)
        qkv_b = jnp.zeros((8, 3 * half), BF16)

    xh, q, k, v, kaug, kt, vt, w_own, w_turn = qkv_call(
        info, x, x_other, qkv_a, qkv_b, depth if direct else None, vec, cos, sin, mk
    )
    if direct:
        *down_parts, q = lax.optimization_barrier((*down_parts, q))
        down = jnp.concatenate(down_parts, axis=0)
        down_got = lax.ppermute(down, "rows", flip)
    att_far, lse_far = attend_call(base_far, info, q, kaug, vt, mq)
    att_got = lax.ppermute(att_far, "rows", flip)
    if direct:
        down, down_got, att_far = lax.optimization_barrier((down, down_got, att_far))
        down = jnp.stack([down, down_got], axis=0)[None]
        down = gather_stage(down, "seq", count, near)
    att_own, lse_own = attend_call(base_own, info, after(q, att_far), kaug, vt, mq)

    if direct:
        down_a = after(down, att_own)
        down_b = lax.ppermute(down_a, "seq", core_pairs)
    else:
        down_a, down_b = lax.all_gather(w_down, "seq", axis=0, tiled=True), None
    att, res, normed = pre_call(info, att_own, att_got, x, packed, depth, vec)
    hid, gres, do_own, do_send, gwp, gwd_send, gwd_keep, gub, sums_two = ffn_call(
        info, att, res, normed, cot, packed, depth, down_a, down_b, vec, up_row
    )
    do_far = lax.ppermute(do_send, "rows", flip)

    if not direct:
        gwp = gwp.reshape(blocks + 1, count, depth, width).transpose(1, 0, 2, 3)
    shard_p = lax.psum_scatter(gwp.reshape(-1, width), "seq", scatter_dimension=0, tiled=True)

    gwd_got = lax.ppermute(gwd_send, "seq", core_pairs)

    back = (q, k, kaug, kt, v, mq, cos, sin, pos)
    all_pairs = half // PAIR
    gq_own, dk, dv, sums_own = attend_back_call(base_own, info, do_own, att_own, lse_own, *back, 0, all_pairs)
    gwd_got, gq_own, do_far = lax.optimization_barrier((gwd_got, gq_own, do_far))
    gwd = (gwd_keep.astype(F32) + gwd_got.astype(F32)).astype(BF16).reshape(count // 2, 2, deep, half)
    gwd_keep = lax.dynamic_index_in_dim(gwd, side, 1, False)
    gwd_got = lax.ppermute(lax.dynamic_index_in_dim(gwd, 1 - side, 1, False), "rows", flip)

    queries, keys, sums_far, grads, lanes = [], [], [], [], []
    for step, (first, pairs) in enumerate(((0, 3),)):
        lane = first * PAIR
        gq, gk, gv, sums = attend_back_call(
            base_far, info, do_far, att_far, lse_far, *back, first, pairs, held=(dk, dv)
        )
        queries.append((gq, lane))
        keys += [(gk, half + lane), (gv, 2 * half + lane)]
        sums_far.append(sums)
        grads += [gq, gk, gv]
        lanes.append((lane, pairs * PAIR))
    col = (sums_own[:3] + jnp.concatenate(sums_far, axis=1)[:3]).reshape(1, 3 * half)
    part_far = part_call(base_far, queries, keys, w_turn, BF16)
    part_got = lax.ppermute(part_far, "rows", flip)
    shard_got = lax.ppermute(shard_p, "rows", flip)
    gwd_got, xh, part_far = lax.optimization_barrier((gwd_got, xh, part_far))
    gwd = (gwd_keep.astype(F32) + gwd_got.astype(F32)).astype(BF16)
    gwd = scatter_chips(gwd, "seq", count, chip_groups(count)).astype(BF16)
    *gw, sums_one = weight_call(info, xh, gq_own, grads, w_own, col, vec, depth if direct else None, lanes)
    if not direct:
        gw = gw[0].reshape(count // 2, 2, depth, 3 * half)
        gw = [lax.dynamic_index_in_dim(gw, c, 1, False).reshape(-1, 3 * half) for c in (1 - index % 2, index % 2)]
    gw_got = lax.ppermute(gw[0], "seq", core_pairs)
    gw = (gw[1].astype(F32) + gw_got.astype(F32)).astype(BF16).reshape(count // 2, depth, 3 * half)
    gw = after(gw, shard_p)
    shard_own = scatter_chips(gw, "seq", count, chip_groups(count)).astype(BF16)
    shard_far = lax.ppermute(shard_own, "rows", flip)
    own_keys = [(gq_own, 0)]
    part_own = part_call(base_own, own_keys, keys, after(w_turn, sums_one), F32)
    patch_grad = norm_back_call(x, part_own, part_got, gres, vec)

    swaps = []
    for mask in (0, 1):
        swaps.append([(2 * i + r, 2 * (i - i % 2 + r) + ((i % 2) ^ mask)) for i in range(count) for r in range(2)])
    same_half, other_half = (lax.ppermute(after(gwd, shard_own), ("seq", "rows"), p) for p in swaps)
    shard_p = shard_p.astype(F32) + shard_got.astype(F32)
    shard_out = shard_p[:depth]
    shard_up = jnp.concatenate([shard_p[(1 + c) * depth : (2 + c) * depth] for c in range(blocks)], axis=1)
    small = collect_call(info, sums_own, *sums_far, gub, sums_two, sums_one, after(shard_own, patch_grad), gwd, shard_p)
    small, (shard_far, same_half, other_half) = sum_over(small, count, (shard_far, same_half, other_half))
    first = jnp.where(side == 0, shard_own, shard_far).reshape(depth, 3, 1, half)
    second = jnp.where(side == 0, shard_far, shard_own).reshape(depth, 3, 1, half)
    shard_qkv = jnp.concatenate([first, second], axis=2).reshape(depth, 6 * half).astype(F32)

    low = side == 0
    shard_down = jnp.concatenate(
        [jnp.where(low, same_half, other_half), jnp.where(low, other_half, same_half)], axis=1
    ).astype(F32)

    s_qkv, s_up, s_out, s_down, s_gain2, s_shift2, s_gain1, s_shift1, freqs, norms = finish_call(small, hidden)
    freqs = freqs[:2].reshape(2, heads, HEAD)[:, :, : HEAD // 2]
    return (
        hid[None],
        patch_grad[None],
        shard_qkv,
        s_qkv,
        shard_out,
        s_out,
        shard_up,
        s_up,
        shard_down,
        s_down,
        s_gain1,
        s_shift1,
        s_gain2,
        s_shift2,
        freqs,
        norms[0, 0],
        norms[0, 1],
    )


def solution(mesh):
    in_specs = (
        P("seq", "rows", None),
        P("seq", None),
        P("seq", None),
        P(),
        P("seq", None),
        P(),
        P("seq", None),
        P(),
        P("seq", None),
        P(),
        P(),
        P(),
        P(),
        P(),
        P(),
        P("seq", "rows", None),
    )
    out_specs = (
        P("seq", "rows", None),
        P("seq", "rows", None),
        P("seq", None),
        P(),
        P("seq", None),
        P(),
        P("seq", None),
        P(),
        P("seq", None),
        P(),
        P(),
        P(),
        P(),
        P(),
        P(),
        P(),
        P(),
    )
    return jax.shard_map(body, mesh=mesh, in_specs=in_specs, out_specs=out_specs, check_vma=False)
```

```python
import jax
import jax.numpy as jnp
from jax import lax
from jax.experimental import pallas as pl
from jax.experimental.pallas import tpu as pltpu
from jax.sharding import PartitionSpec as P

SIDE_S = 14
SIDE_M = 20
SIDE_L = 24
EPS = 1e-06
NEG = -1e30
HEAD = 64
PAIR = 128
TILE = 256
F32 = jnp.float32
BF16 = jnp.bfloat16
OUT_BIAS, DOWN_BIAS, GAIN_ONE, SHIFT_ONE, GAIN_TWO, SHIFT_TWO = (slice(r, r + 1) for r in range(3, 9))


def cost(us):
    return pl.CostEstimate(flops=int(us * 1150000000), bytes_accessed=10**5, transcendentals=0)


def params(mib):
    return pltpu.CompilerParams(vmem_limit_bytes=mib * 1024 * 1024)


def nn(a, b):
    return lax.dot_general(a, b, (((1,), (0,)), ((), ())), preferred_element_type=F32)


def nt(a, b):
    return lax.dot_general(a, b, (((1,), (1,)), ((), ())), preferred_element_type=F32)


def tn(a, b):
    return lax.dot_general(a, b, (((0,), (0,)), ((), ())), preferred_element_type=F32)


def swap_halves(u):
    width = u.shape[-1]
    lane = lax.broadcasted_iota(jnp.int32, u.shape, 1) % HEAD
    return jnp.where(
        lane < HEAD // 2,
        pltpu.roll(u, width - HEAD // 2, 1),
        pltpu.roll(u, HEAD // 2, 1),
    )


def head_lanes(shape, odd):
    lane = lax.broadcasted_iota(jnp.int32, shape, 1)
    return (lane >= HEAD) if odd else (lane < HEAD)


def tile_bounds(info_ref, tile, total):
    first = tile * TILE
    last = first + TILE - 1
    run = jnp.int32(0)
    low = jnp.int32(-1)
    high = jnp.int32(total)
    for s in range(3, info_ref.shape[0]):
        end = run + info_ref[s]
        low = jnp.where((first >= run) & (first < end), run, low)
        high = jnp.where((last >= run) & (last < end), end, high)
        run = end
    low = jnp.where(low < 0, run, low)
    return lax.div(low, TILE), lax.div(high + (TILE - 1), TILE)


def pack_kernel(info_ref, down_ref, out_ref, up_ref, qkv_ref, packed_ref, cols_ref):
    depth, width = out_ref.shape
    half = width // 2
    share = packed_ref.shape[0] - depth * (1 + up_ref.shape[1] // width)
    packed_ref[:share, :] = down_ref[:share, :]
    packed_ref[share : share + depth, :] = out_ref[...]
    for c in range(up_ref.shape[1] // width):
        at = share + (c + 1) * depth
        packed_ref[at : at + depth, :] = up_ref[:, c * width : (c + 1) * width]
    for i in range(3):
        at = pl.multiple_of(i * width + info_ref[0] * half, PAIR)
        cols_ref[:, i * half : (i + 1) * half] = qkv_ref[:, pl.ds(at, half)]


def pack_call(info, w_down, w_out, w_up, w_qkv, share):
    depth, width = w_out.shape
    whole = lambda r, c: pl.BlockSpec((r, c), lambda i, s: (0, 0))
    length = share + depth * (w_up.shape[1] // width + 1)
    arrays = (w_down, w_out, w_up, w_qkv)
    return pl.pallas_call(
        pack_kernel,
        grid_spec=pltpu.PrefetchScalarGridSpec(
            num_scalar_prefetch=1,
            grid=(1,),
            in_specs=[whole(*a.shape) for a in arrays],
            out_specs=[whole(length, width), whole(depth, 3 * width // 2)],
        ),
        out_shape=[
            jax.ShapeDtypeStruct((length, width), BF16),
            jax.ShapeDtypeStruct((depth, 3 * width // 2), BF16),
        ],
        compiler_params=params(60),
        cost_estimate=cost(2.5),
    )(info, *arrays)


def table_kernel(info_ref, freq_ref, cos_ref, sin_ref, mq_ref, mk_ref, pos_ref):
    step = pl.program_id(0)
    slots = info_ref.shape[0] - 3

    def place(shape):
        at = lax.broadcasted_iota(jnp.int32, shape, 0) + step * TILE
        block = jnp.full(shape, slots, jnp.int32)
        offset = jnp.zeros(shape, jnp.int32)
        side = jnp.ones(shape, F32)
        run = jnp.int32(0)
        for s in range(slots):
            count = info_ref[3 + s]
            inside = (at >= run) & (at < run + count)
            width = jnp.where(count == SIDE_S * SIDE_S, SIDE_S, jnp.where(count == SIDE_M * SIDE_M, SIDE_M, SIDE_L))
            block = jnp.where(inside, s, block)
            offset = jnp.where(inside, at - run, offset)
            side = jnp.where(inside, width.astype(F32), side)
            run = run + count
        offset = offset.astype(F32)
        row = jnp.floor((offset + 0.5) / side)
        return block, row, offset - row * side

    block, row, col = place((TILE, PAIR))
    lane = lax.broadcasted_iota(jnp.int32, (TILE, PAIR), 1)
    slot = lane % HEAD
    same = slot == block
    mk_ref[...] = same.astype(F32).astype(BF16)
    mq_ref[...] = jnp.where(same | (slot > slots), 0.0, NEG).astype(BF16)
    pos_ref[...] = jnp.where(lane == 0, row, jnp.where(lane == 1, col, 0.0))
    half = TILE // 2
    width = cos_ref.shape[1]
    front = lax.broadcasted_iota(jnp.int32, (half, width), 1) % HEAD < HEAD // 2
    both = lambda u: (u[:half, 0:1], u[half:, 0:1])
    row_a, row_b = both(row)
    col_a, col_b = both(col)
    angle = jnp.where(front, row_a, row_b) * freq_ref[0:1, :] + jnp.where(front, col_a, col_b) * freq_ref[1:2, :]
    for ref, value in ((cos_ref, jnp.cos(angle)), (sin_ref, jnp.sin(angle))):
        up = pltpu.roll(value, HEAD // 2, 1)
        down = pltpu.roll(value, width - HEAD // 2, 1)
        sign = -1.0 if ref is sin_ref else 1.0
        ref[:half, :] = jnp.where(front, sign * value, up)
        ref[half:, :] = jnp.where(front, sign * down, value)


def table_call(info, freqs, total):
    width = freqs.shape[1]
    tile = lambda c: pl.BlockSpec((TILE, c), lambda i, s: (i, 0))
    return pl.pallas_call(
        table_kernel,
        grid_spec=pltpu.PrefetchScalarGridSpec(
            num_scalar_prefetch=1,
            grid=(total // TILE,),
            in_specs=[pl.BlockSpec(freqs.shape, lambda i, s: (0, 0))],
            out_specs=[tile(width), tile(width), tile(PAIR), tile(PAIR), tile(PAIR)],
        ),
        out_shape=[
            jax.ShapeDtypeStruct((total, width), F32),
            jax.ShapeDtypeStruct((total, width), F32),
            jax.ShapeDtypeStruct((total, PAIR), BF16),
            jax.ShapeDtypeStruct((total, PAIR), BF16),
            jax.ShapeDtypeStruct((total, PAIR), F32),
        ],
        compiler_params=params(60),
        cost_estimate=cost(9),
    )(info, freqs)


def qkv_kernel(
    place_ref, own_ref, other_ref, wa_ref, wb_ref, vec_ref, cos_ref, sin_ref, mk_ref,
    xh_ref, q_ref, k_ref, v_ref, kaug_ref, kt_ref, vt_ref, w_ref, wt_ref, *, depth,
):
    step = pl.program_id(0)
    half = pl.num_programs(0) // 2
    width = cos_ref.shape[1]

    @pl.when(step == 0)
    def _():
        if depth is None:
            w_ref[...] = wa_ref[...]
        else:
            core = place_ref[1]
            pieces = wa_ref.shape[0] // depth
            for m in range(pieces):
                at = (place_ref[2] ^ m) * (2 * depth)
                held = spot(m, 2 * pieces)
                rows = slice(held * depth, (held + 1) * depth)
                w_ref[pl.ds(pl.multiple_of(at + core * depth, 16), depth), :] = wa_ref[rows, :]
                w_ref[pl.ds(pl.multiple_of(at + (1 - core) * depth, 16), depth), :] = wb_ref[rows, :]
        wt_ref[...] = w_ref[...].T

    mine = (step // half) == place_ref[0]
    x = jnp.where(mine, own_ref[...].astype(F32), other_ref[...].astype(F32))
    mean = jnp.mean(x, axis=1, keepdims=True)
    cen = x - mean
    var = jnp.mean(cen * cen, axis=1, keepdims=True)
    xh = cen * lax.rsqrt(var + EPS)
    xh_ref[...] = xh.astype(BF16).T
    normed = (xh * vec_ref[GAIN_ONE] + vec_ref[SHIFT_ONE]).astype(BF16)
    mid = pl.ds(pl.multiple_of(place_ref[0] * width, PAIR), width)
    bias = jnp.concatenate([vec_ref[i : i + 1, mid] for i in range(3)], axis=1)
    proj = nn(normed, w_ref[...]) + bias
    c = cos_ref[...]
    s = sin_ref[...]
    q = proj[:, :width]
    k = proj[:, width : 2 * width]
    q = (q * c + swap_halves(q) * s).astype(BF16)
    k = (k * c + swap_halves(k) * s).astype(BF16)
    v = proj[:, 2 * width :].astype(BF16)
    q_ref[...] = (q.astype(F32) * 0.125).astype(BF16)
    k_ref[...] = k
    v_ref[...] = v
    kt_ref[...] = k.T
    vt_ref[...] = v.T
    mk = mk_ref[...]
    for h in range(width // HEAD):
        pair = h // 2
        kp = k[:, pair * PAIR : (pair + 1) * PAIR]
        kaug_ref[h] = jnp.where(head_lanes(kp.shape, h % 2), kp, mk)


def qkv_call(place, own, other, wa, wb, depth, vec, cos, sin, mk):
    rows, width = own.shape
    total = 2 * rows
    cols = wa.shape[1]
    third = cols // 3
    heads = third // HEAD
    per = rows // TILE
    last = per - 1
    whole = lambda i, s: (0, 0)
    tile = lambda c: pl.BlockSpec((TILE, c), lambda i, s: (i, 0))
    return pl.pallas_call(
        lambda *refs: qkv_kernel(*refs, depth=depth),
        grid_spec=pltpu.PrefetchScalarGridSpec(
            num_scalar_prefetch=1,
            grid=(total // TILE,),
            in_specs=[
                pl.BlockSpec((TILE, width), lambda i, s: (jnp.clip(i - per * s[0], 0, last), 0)),
                pl.BlockSpec((TILE, width), lambda i, s: (jnp.clip(i - per * (1 - s[0]), 0, last), 0)),
                pl.BlockSpec(wa.shape, whole),
                pl.BlockSpec(wb.shape, whole),
                pl.BlockSpec(vec.shape, whole),
                tile(third),
                tile(third),
                tile(PAIR),
            ],
            out_specs=[
                pl.BlockSpec((width, TILE), lambda i, s: (0, i)),
                tile(third),
                tile(third),
                tile(third),
                pl.BlockSpec((heads, TILE, PAIR), lambda i, s: (0, i, 0)),
                pl.BlockSpec((third, TILE), lambda i, s: (0, i)),
                pl.BlockSpec((third, TILE), lambda i, s: (0, i)),
                pl.BlockSpec((width, cols), whole),
                pl.BlockSpec((cols, width), whole),
            ],
        ),
        out_shape=[
            jax.ShapeDtypeStruct((width, total), BF16),
            jax.ShapeDtypeStruct((total, third), BF16),
            jax.ShapeDtypeStruct((total, third), BF16),
            jax.ShapeDtypeStruct((total, third), BF16),
            jax.ShapeDtypeStruct((heads, total, PAIR), BF16),
            jax.ShapeDtypeStruct((third, total), BF16),
            jax.ShapeDtypeStruct((third, total), BF16),
            jax.ShapeDtypeStruct((width, cols), BF16),
            jax.ShapeDtypeStruct((cols, width), BF16),
        ],
        compiler_params=params(60),
        cost_estimate=cost(1),
    )(place, own, other, wa, wb, vec, cos, sin, mk)


def attend_kernel(base_ref, info_ref, q_ref, kaug_ref, vt_ref, mq_ref, out_ref, lse_ref, qaug, scores, acc):
    step = pl.program_id(0) + base_ref[0]
    width = out_ref.shape[1]
    heads = width // HEAD
    mq = mq_ref[...]
    for h in range(heads):
        pair = h // 2
        q = q_ref[:, pair * PAIR : (pair + 1) * PAIR]
        qaug[h] = jnp.where(head_lanes(q.shape, h % 2), q, mq)
    lo, hi = tile_bounds(info_ref, step, kaug_ref.shape[1])

    def first(kt, best):
        keys = pl.ds(pl.multiple_of(kt * TILE, TILE), TILE)
        out = []
        for h in range(heads):
            s = nt(kaug_ref[h, keys, :], qaug[h])
            scores[h, keys, :] = s
            out.append(jnp.maximum(best[h], jnp.max(s.reshape(TILE // 8, 8, TILE), axis=0)))
        return tuple(out)

    best = lax.fori_loop(lo, hi, first, tuple(jnp.full((8, TILE), -jnp.inf, F32) for _ in range(heads)))
    best = [jnp.max(b, axis=0, keepdims=True) for b in best]
    acc[...] = jnp.zeros_like(acc)

    def second(kt, sums):
        keys = pl.ds(pl.multiple_of(kt * TILE, TILE), TILE)
        out = []
        for h in range(heads):
            p = jnp.exp(scores[h, keys, :] - best[h])
            out.append(sums[h] + jnp.sum(p.reshape(TILE // 8, 8, TILE), axis=0))
            own = slice(h * HEAD, (h + 1) * HEAD)
            acc[own, :] += nn(vt_ref[own, keys], p.astype(BF16))
        return tuple(out)

    sums = lax.fori_loop(lo, hi, second, tuple(jnp.zeros((8, TILE), F32) for _ in range(heads)))
    lses = []
    outs = []
    for h in range(heads):
        tot = jnp.sum(sums[h], axis=0, keepdims=True)
        outs.append(acc[h * HEAD : (h + 1) * HEAD, :] / tot)
        lses.append(best[h] + jnp.log(tot))
    lses += [jnp.zeros_like(lses[0])] * (8 - heads)
    lse_ref[...] = jnp.concatenate(lses, axis=0)
    out_ref[...] = jnp.concatenate(outs, axis=0).T.astype(BF16)


def attend_call(base, info, q, kaug, vt, mq):
    total, width = q.shape
    heads = width // HEAD
    rows = total // 2
    whole = lambda i, b, s: (0, 0)
    return pl.pallas_call(
        attend_kernel,
        grid_spec=pltpu.PrefetchScalarGridSpec(
            num_scalar_prefetch=2,
            grid=(rows // TILE,),
            in_specs=[
                pl.BlockSpec((TILE, width), lambda i, b, s: (b[0] + i, 0)),
                pl.BlockSpec(kaug.shape, lambda i, b, s: (0, 0, 0)),
                pl.BlockSpec(vt.shape, whole),
                pl.BlockSpec((TILE, PAIR), lambda i, b, s: (b[0] + i, 0)),
            ],
            out_specs=[
                pl.BlockSpec((TILE, width), lambda i, b, s: (i, 0)),
                pl.BlockSpec((8, TILE), lambda i, b, s: (0, i)),
            ],
            scratch_shapes=[
                pltpu.VMEM((heads, TILE, PAIR), BF16),
                pltpu.VMEM((heads, total, TILE), F32),
                pltpu.VMEM((width, TILE), F32),
            ],
        ),
        out_shape=[
            jax.ShapeDtypeStruct((rows, width), BF16),
            jax.ShapeDtypeStruct((8, rows), F32),
        ],
        compiler_params=params(60),
        cost_estimate=cost(4),
    )(base, info, q, kaug, vt, mq)


def phi_parts(x):
    cdf = 0.5 * (1.0 + lax.erf(x * 0.7071067811865476))
    pdf = jnp.exp(-0.5 * x * x) * 0.3989422804014327
    return cdf, pdf


def pre_kernel(place_ref, mine_ref, got_ref, x_ref, wo_ref, vec_ref, att_ref, res_ref, normed_ref):
    width = x_ref.shape[1]
    half = width // 2
    lanes = lambda at: pl.ds(pl.multiple_of(at * half, PAIR), half)
    att_ref[:, lanes(place_ref[0])] = mine_ref[...]
    att_ref[:, lanes(1 - place_ref[0])] = got_ref[...]
    wo = wo_ref[...].reshape(width, width)
    r = x_ref[...].astype(F32) + (nn(att_ref[...], wo) + vec_ref[OUT_BIAS])
    res_ref[...] = r
    cen = r - jnp.mean(r, axis=1, keepdims=True)
    var = jnp.mean(cen * cen, axis=1, keepdims=True)
    normed_ref[...] = (cen * lax.rsqrt(var + EPS) * vec_ref[GAIN_TWO] + vec_ref[SHIFT_TWO]).astype(BF16)


def pack_spec(packed, depth, width, at):
    if packed.shape[1] == width:
        return pl.BlockSpec((1, width, width), lambda j, s: (at(j), 0, 0))
    skip = packed.shape[1] % (5 * depth) // depth
    return pl.BlockSpec((packed.shape[0], depth, width), lambda j, s: (0, skip + at(j), 0))


def pre_call(place, mine, got, x, packed, depth, vec):
    rows, width = x.shape
    tile = lambda c: pl.BlockSpec((TILE, c), lambda j, s: (j, 0))
    return pl.pallas_call(
        pre_kernel,
        grid_spec=pltpu.PrefetchScalarGridSpec(
            num_scalar_prefetch=1,
            grid=(rows // TILE,),
            in_specs=[
                tile(width // 2),
                tile(width // 2),
                tile(width),
                pack_spec(packed, depth, width, lambda j: 0),
                pl.BlockSpec(vec.shape, lambda j, s: (0, 0)),
            ],
            out_specs=[tile(width), tile(width), tile(width)],
        ),
        out_shape=[
            jax.ShapeDtypeStruct((rows, width), BF16),
            jax.ShapeDtypeStruct((rows, width), F32),
            jax.ShapeDtypeStruct((rows, width), BF16),
        ],
        compiler_params=params(60),
        cost_estimate=cost(30),
    )(place, mine, got, x, packed, vec)


def ffn_kernel(
    place_ref, att_ref, res_ref, normed_ref, cot_ref, wo_ref, wu_ref, *rest, chips,
):
    many = 2 * chips + 1
    down = rest[:many]
    (
        vec_ref, ub_ref,
        hid_ref, gres_ref, gown_ref, gfar_ref, gwp_ref, send_ref, keep_ref, gub_ref, sums_ref,
        acc, gacc, act, gup, wd_s,
    ) = rest[many:]
    step = pl.program_id(0)
    steps = pl.num_programs(0) - 1
    rows, width = res_ref.shape
    half = width // 2
    core = place_ref[1]
    chunks = [pl.ds(r, TILE) for r in range(0, rows, TILE)]
    lanes = lambda at: pl.ds(pl.multiple_of(at * half, PAIR), half)

    @pl.when(step == 0)
    def _():
        acc[...] = jnp.zeros_like(acc)
        gacc[...] = jnp.zeros_like(gacc)

    @pl.when(step < steps)
    def _():
        if chips:
            deep = width // (2 * chips)
            share = down[-1].shape[1]
            for t in range(2 * chips):
                wd_s[t * deep : t * deep + share, :] = down[-1][t]
            for t in range(chips):
                for r in (0, 1):
                    at = 2 * t * deep + (place_ref[0] ^ r) * deep + share
                    spot_rows = pl.ds(pl.multiple_of(at, 16), deep - share)
                    wd_s[spot_rows, lanes(core)] = down[t][r]
                    wd_s[spot_rows, lanes(1 - core)] = down[chips + t][r]
            wd_ref = wd_s
        else:
            wd_ref = down[0]
        bias_sum = jnp.zeros((1, ub_ref.shape[1]), F32)
        wu = wu_ref[...].reshape(width, width)
        for ch in chunks:
            up = nn(normed_ref[ch, :], wu) + ub_ref[...]
            cdf, pdf = phi_parts(up)
            a = (up * cdf).astype(BF16)
            act[ch, :] = a
            g = (nt(cot_ref[ch, :], wd_ref[...]) * (cdf + up * pdf)).astype(BF16)
            gup[ch, :] = g
            bias_sum += jnp.sum(g.astype(F32), axis=0, keepdims=True)
            acc[ch, :] += nn(a, wd_ref[...])
            gacc[ch, :] += nt(g, wu)
        gub_ref[...] = bias_sum
        send_ref[...] = tn(act[...], cot_ref[:, lanes(1 - core)]).astype(BF16)
        keep_ref[...] = tn(act[...], cot_ref[:, lanes(core)]).astype(BF16)
        gwp_ref[...] = tn(normed_ref[...], gup[...]).astype(BF16).reshape(gwp_ref.shape)

    @pl.when(step == steps)
    def _():
        zero = jnp.zeros((1, width), F32)
        s_out, s_down, s_gain, s_shift = zero, zero, zero, zero
        gain = vec_ref[GAIN_TWO]
        wo = wo_ref[...].reshape(width, width)
        for ch in chunks:
            r = res_ref[ch, :]
            hid_ref[ch, :] = (r + acc[ch, :] + vec_ref[DOWN_BIAS]).astype(BF16)
            cen = r - jnp.mean(r, axis=1, keepdims=True)
            rs = lax.rsqrt(jnp.mean(cen * cen, axis=1, keepdims=True) + EPS)
            xh = cen * rs
            e = gacc[ch, :]
            eg = e * gain
            cot = cot_ref[ch, :].astype(F32)
            g = cot + rs * (
                eg - jnp.mean(eg, axis=1, keepdims=True) - xh * jnp.mean(eg * xh, axis=1, keepdims=True)
            )
            gres_ref[ch, :] = g
            gb = g.astype(BF16)
            act[ch, :] = gb
            gup[ch, :] = nt(gb, wo).astype(BF16)
            gown_ref[ch, :] = gup[ch, lanes(place_ref[0])]
            gfar_ref[ch, :] = gup[ch, lanes(1 - place_ref[0])]
            s_out += jnp.sum(gb.astype(F32), axis=0, keepdims=True)
            s_down += jnp.sum(cot, axis=0, keepdims=True)
            s_gain += jnp.sum(e * xh, axis=0, keepdims=True)
            s_shift += jnp.sum(e, axis=0, keepdims=True)
        gwp_ref[...] = tn(att_ref[...], act[...]).astype(BF16).reshape(gwp_ref.shape)
        sums_ref[...] = jnp.concatenate([s_out, s_down, s_gain, s_shift] + [zero] * 4, axis=0)


def ffn_call(place, att, res, normed, cot, packed, depth, down_a, down_b, vec, ub):
    rows, width = res.shape
    half = width // 2
    hidden = ub.shape[1]
    steps = hidden // width
    last = steps - 1
    whole = lambda j, s: (0, 0)
    held = pl.BlockSpec(memory_space=pltpu.VMEM)
    one = lambda r, c: pl.BlockSpec((r, c), whole)
    pack = lambda at: pack_spec(packed, depth, width, at)
    clip = lambda j: jnp.minimum(j, last)
    if down_b is None:
        chips = 0
        down = (down_a,)
        down_specs = [pl.BlockSpec((width, width), lambda j, s: (clip(j), 0))]
        grads = jax.ShapeDtypeStruct(packed.shape, BF16)
    else:
        count = packed.shape[0]
        share = packed.shape[1] - (steps + 1) * depth
        piece_rows = down_a.shape[3]
        chips = width * count // (2 * hidden)
        grads = jax.ShapeDtypeStruct((count, (steps + 1) * depth, width), BF16)

        def piece(t):
            def at(j, s):
                chip = (clip(j) * chips + t) ^ s[2]
                return (chip & 1, 0, chip >> 1, 0, 0)

            return pl.BlockSpec((pl.squeezed, 2, pl.squeezed, piece_rows, half), at)

        down_specs = [piece(t) for t in range(chips)] * 2
        down_specs.append(pl.BlockSpec((2 * chips, share, width), lambda j, s: (clip(j), 0, 0)))
        down = (down_a,) * chips + (down_b,) * chips + (packed,)
    return pl.pallas_call(
        lambda *refs: ffn_kernel(*refs, chips=chips),
        grid_spec=pltpu.PrefetchScalarGridSpec(
            num_scalar_prefetch=1,
            grid=(steps + 1,),
            in_specs=[
                one(rows, width),
                one(rows, width),
                one(rows, width),
                one(rows, width),
                pack(lambda j: 0),
                pack(lambda j: 1 + clip(j)),
                *down_specs,
                one(*vec.shape),
                pl.BlockSpec((1, width), lambda j, s: (0, clip(j))),
            ],
            out_specs=[
                one(rows, width),
                one(rows, width),
                one(rows, half),
                one(rows, half),
                pack_spec(grads, depth, width, lambda j: jnp.where(j < steps, 1 + j, 0)),
                pl.BlockSpec((width, half), lambda j, s: (clip(j), 0)),
                pl.BlockSpec((width, half), lambda j, s: (clip(j), 0)),
                pl.BlockSpec((1, width), lambda j, s: (0, clip(j))),
                one(8, width),
            ],
            scratch_shapes=[
                pltpu.VMEM((rows, width), F32),
                pltpu.VMEM((rows, width), F32),
                pltpu.VMEM((rows, width), BF16),
                pltpu.VMEM((rows, width), BF16),
                pltpu.VMEM((width, width), BF16),
            ],
        ),
        out_shape=[
            jax.ShapeDtypeStruct((rows, width), BF16),
            jax.ShapeDtypeStruct((rows, width), F32),
            jax.ShapeDtypeStruct((rows, half), BF16),
            jax.ShapeDtypeStruct((rows, half), BF16),
            grads,
            jax.ShapeDtypeStruct((hidden, half), BF16),
            jax.ShapeDtypeStruct((hidden, half), BF16),
            jax.ShapeDtypeStruct((1, hidden), F32),
            jax.ShapeDtypeStruct((8, width), F32),
        ],
        compiler_params=params(60),
        cost_estimate=cost(38),
    )(place, att, res, normed, cot, packed, packed, *down, vec, ub)


def attend_back_kernel(base_ref, info_ref, do_ref, o_ref, lse_ref, q_ref, kaug_ref, kt_ref, v_ref, mq_ref, cos_ref, sin_ref, pos_ref, *rest, final, head):
    if final:
        k_ref, cos_all, sin_all, pos_all, dk_in, dv_in, gq_ref, gk_ref, gv_ref, sums_ref = rest[:10]
        qaug, qm, dom, dqt, delta, s_scr, dp_scr, p_scr, ds_scr, dk, dv = rest[10:]
    else:
        gq_ref, dk, dv, sums_ref = rest[:4]
        qaug, qm, dom, dqt, delta, s_scr, dp_scr, p_scr, ds_scr = rest[4:]
    step = pl.program_id(0)
    tile = step + base_ref[0]
    width = do_ref.shape[1]
    heads = width // HEAD
    pairs = heads // 2
    total = v_ref.shape[0]

    @pl.when(step == 0)
    def _():
        if final:
            dk[...] = dk_in[...]
            dv[...] = dv_in[...]
        else:
            dk[...] = jnp.zeros_like(dk)
            dv[...] = jnp.zeros_like(dv)
        sums_ref[...] = jnp.zeros_like(sums_ref)

    mq = mq_ref[...]
    for h in range(heads):
        pair = slice((h // 2) * PAIR, (h // 2 + 1) * PAIR)
        q = q_ref[:, pair]
        lanes = head_lanes(q.shape, h % 2)
        qaug[h] = jnp.where(lanes, q, mq)
        qm[h * TILE : (h + 1) * TILE, :] = jnp.where(lanes, q, jnp.zeros_like(q))
        dom[h * TILE : (h + 1) * TILE, :] = jnp.where(lanes, do_ref[:, pair], jnp.zeros_like(q))
    inner = do_ref[...].astype(F32) * o_ref[...].astype(F32)
    pick = (
        lax.broadcasted_iota(jnp.int32, (8, width), 1) // HEAD == lax.broadcasted_iota(jnp.int32, (8, width), 0)
    ).astype(F32)
    delta[...] = lax.dot_general(
        pick, inner, (((1,), (1,)), ((), ())), precision=lax.Precision.HIGHEST, preferred_element_type=F32
    )
    dqt[...] = jnp.zeros_like(dqt)

    def body(kt, carry):
        keys = pl.ds(pl.multiple_of(kt * TILE, TILE), TILE)
        for h in range(heads):
            s_scr[h] = nt(kaug_ref[h, keys, :], qaug[h])
            dp_scr[h] = nt(v_ref[keys, (h // 2) * PAIR : (h // 2 + 1) * PAIR], dom[h * TILE : (h + 1) * TILE, :])
        for h in range(heads):
            at = slice((h % 2) * TILE, (h % 2 + 1) * TILE)
            p = jnp.exp(s_scr[h] - lse_ref[head + h : head + h + 1, :])
            p_scr[h // 2, :, at] = p.astype(BF16)
            ds_scr[h // 2, :, at] = (p * (dp_scr[h] - delta[h : h + 1, :])).astype(BF16)
        for pr in range(pairs):
            pair = slice(pr * PAIR, (pr + 1) * PAIR)
            both = slice(2 * pr * TILE, 2 * (pr + 1) * TILE)
            dv[keys, pair] += nn(p_scr[pr], dom[both, :])
            dk[keys, pair] += nn(ds_scr[pr], qm[both, :])
            for e in (0, 1):
                own = slice((2 * pr + e) * HEAD, (2 * pr + e + 1) * HEAD)
                dqt[own, :] += nn(kt_ref[own, keys], ds_scr[pr, :, e * TILE : (e + 1) * TILE])
        return carry

    lo, hi = tile_bounds(info_ref, tile, total)
    lax.fori_loop(lo, hi, body, 0)

    def unrotate(u, c, s):
        return (u * c - swap_halves(u) * s).astype(BF16)

    def freq_sum(u, rot, pos):
        w = u * swap_halves(rot)
        sums_ref[3:4, :] += jnp.sum(w * pos[:, 0:1], axis=0, keepdims=True)
        sums_ref[4:5, :] += jnp.sum(w * pos[:, 1:2], axis=0, keepdims=True)

    dq = dqt[...].T * 0.125
    freq_sum(dq, q_ref[...].astype(F32) * 8.0, pos_ref[...])
    gq = unrotate(dq, cos_ref[...], sin_ref[...])
    gq_ref[...] = gq
    sums_ref[0:1, :] += jnp.sum(gq.astype(F32), axis=0, keepdims=True)

    if final:

        @pl.when(step == pl.num_programs(0) - 1)
        def _():
            for t in range(total // TILE):
                at = pl.ds(t * TILE, TILE)
                u = dk[at, :]
                freq_sum(u, k_ref[at, :].astype(F32), pos_all[at, :])
                gk = unrotate(u, cos_all[at, :], sin_all[at, :])
                gv = dv[at, :].astype(BF16)
                gk_ref[at, :] = gk
                gv_ref[at, :] = gv
                sums_ref[1:2, :] += jnp.sum(gk.astype(F32), axis=0, keepdims=True)
                sums_ref[2:3, :] += jnp.sum(gv.astype(F32), axis=0, keepdims=True)


def attend_back_call(base, info, do, o, lse, q, k, kaug, kt, v, mq, cos, sin, pos, first, pairs, held=None):
    total = q.shape[0]
    width = pairs * PAIR
    heads = 2 * pairs
    spot = first // pairs
    rows = total // 2
    final = held is not None
    here = lambda c: pl.BlockSpec((TILE, c), lambda i, b, s: (i, spot))
    there = lambda c: pl.BlockSpec((TILE, c), lambda i, b, s: (b[0] + i, spot))
    flat = lambda c: pl.BlockSpec((TILE, c), lambda i, b, s: (b[0] + i, 0))
    tall = pl.BlockSpec((total, width), lambda i, b, s: (0, spot))
    held_in = pl.BlockSpec(memory_space=pltpu.VMEM)
    whole = lambda a: pl.BlockSpec(a.shape, lambda i, b, s: (0,) * len(a.shape))
    args = [do, o, lse, q, kaug, kt, v, mq, cos, sin, pos]
    in_specs = [
        here(width), here(width), pl.BlockSpec((8, TILE), lambda i, b, s: (0, i)), there(width),
        pl.BlockSpec((heads, total, PAIR), lambda i, b, s: (spot, 0, 0)),
        pl.BlockSpec((width, total), lambda i, b, s: (spot, 0)),
        tall, flat(PAIR), there(width), there(width), flat(PAIR),
    ]
    big = jax.ShapeDtypeStruct((total, width), F32)
    low = jax.ShapeDtypeStruct((total, width), BF16)
    sums = jax.ShapeDtypeStruct((8, width), F32)
    scratch = [
        pltpu.VMEM((heads, TILE, PAIR), BF16),
        pltpu.VMEM((heads * TILE, PAIR), BF16),
        pltpu.VMEM((heads * TILE, PAIR), BF16),
        pltpu.VMEM((width, TILE), F32),
        pltpu.VMEM((8, TILE), F32),
        pltpu.VMEM((heads, TILE, TILE), F32),
        pltpu.VMEM((heads, TILE, TILE), F32),
        pltpu.VMEM((pairs, TILE, 2 * TILE), BF16),
        pltpu.VMEM((pairs, TILE, 2 * TILE), BF16),
    ]
    if final:
        args += [k, cos, sin, pos, *held]
        in_specs += [tall, tall, tall, whole(pos), held_in, held_in]
        grads = [low, low]
        scratch += [pltpu.VMEM((total, width), F32), pltpu.VMEM((total, width), F32)]
    else:
        grads = [big, big]
    return pl.pallas_call(
        lambda *refs: attend_back_kernel(*refs, final=final, head=2 * first),
        grid_spec=pltpu.PrefetchScalarGridSpec(
            num_scalar_prefetch=2,
            grid=(rows // TILE,),
            in_specs=in_specs,
            out_specs=[pl.BlockSpec((TILE, width), lambda i, b, s: (i, 0)), held_in, held_in, whole(sums)],
            scratch_shapes=scratch,
        ),
        out_shape=[jax.ShapeDtypeStruct((rows, width), BF16), *grads, sums],
        compiler_params=params(50),
        cost_estimate=cost(10 * pairs),
    )(base, info, *args)


def part_kernel(base_ref, *refs, lanes):
    w_ref, out_ref = refs[-2:]
    total = jnp.zeros(out_ref.shape, F32)
    for ref, at in zip(refs, lanes):
        total += nn(ref[...], w_ref[at : at + ref.shape[1], :])
    out_ref[...] = total.astype(out_ref.dtype)


def part_call(base, queries, keys, w, kind):
    rows = queries[0][0].shape[0]
    here = lambda c: pl.BlockSpec((TILE, c), lambda i, b: (i, 0))
    there = lambda c: pl.BlockSpec((TILE, c), lambda i, b: (b[0] + i, 0))
    arrays = [a for a, _ in queries + keys]
    lanes = [at for _, at in queries + keys]
    return pl.pallas_call(
        lambda *refs: part_kernel(*refs, lanes=lanes),
        grid_spec=pltpu.PrefetchScalarGridSpec(
            num_scalar_prefetch=1,
            grid=(rows // TILE,),
            in_specs=[here(a.shape[1]) for a, _ in queries]
            + [there(a.shape[1]) for a, _ in keys]
            + [pl.BlockSpec(w.shape, lambda i, b: (0, 0))],
            out_specs=pl.BlockSpec((TILE, w.shape[1]), lambda i, b: (i, 0)),
        ),
        out_shape=jax.ShapeDtypeStruct((rows, w.shape[1]), kind),
        compiler_params=params(10),
        cost_estimate=cost(5.6),
    )(base, *arrays, w)


def weight_kernel(place_ref, xh_ref, own_ref, *rest, depth, lanes):
    keys = 3 * len(lanes)
    grads = rest[:keys]
    w_ref, col_ref, vec_ref = rest[keys : keys + 3]
    *outs, spare = rest[keys + 3 :]
    sums_ref = outs[-1]
    third = w_ref.shape[1] // 3
    rows = own_ref.shape[0]
    block = w_ref.shape[0]
    flat = vec_ref[:, pl.ds(pl.multiple_of(pl.program_id(0) * block, PAIR), block)].T
    gain = flat[:, GAIN_ONE]
    shift = flat[:, SHIFT_ONE]
    total = jnp.zeros(gain.shape, F32)
    bias = jnp.zeros(gain.shape, F32)
    half = lambda at: pl.ds(pl.multiple_of(at * rows, TILE), rows)
    for g, (lane, width) in enumerate(lanes):
        for i in range(3):
            ref = grads[3 * g + i]
            at = slice(i * third + lane, i * third + lane + width)
            if i:
                x = nn(xh_ref[...], ref[...])
            else:
                own = own_ref[:, lane : lane + width]
                x = nn(xh_ref[:, half(place_ref[0])], own) + nn(xh_ref[:, half(1 - place_ref[0])], ref[...])
            w = w_ref[:, at].astype(F32)
            col = col_ref[:, at]
            total += jnp.sum(x * w, axis=1, keepdims=True)
            bias += jnp.sum(w * col, axis=1, keepdims=True)
            spare[:, at] = (x * gain + shift * col).astype(BF16)
    lane = lax.broadcasted_iota(jnp.int32, (block, PAIR), 1)
    both = jnp.where(lane == 0, total, jnp.where(lane == 1, bias, 0.0))
    sums_ref[...] = both.T[:8, :]
    if depth is None:
        outs[0][...] = spare[...]
        return
    core = place_ref[1]
    for t in range(spare.shape[0] // (2 * depth)):
        at = 2 * t * depth
        rows = slice(t * depth, (t + 1) * depth)
        outs[0][rows, :] = spare[pl.ds(pl.multiple_of(at + (1 - core) * depth, 16), depth), :]
        outs[1][rows, :] = spare[pl.ds(pl.multiple_of(at + core * depth, 16), depth), :]


def weight_call(place, xh, own, grads, w, col, vec, depth, lanes):
    model, total = xh.shape
    cols = w.shape[1]
    block = model // 2
    whole = lambda a: pl.BlockSpec(a.shape, lambda i, s: (0, 0))
    if depth is None:
        out_shape = [jax.ShapeDtypeStruct((model, cols), BF16)]
        out_specs = [pl.BlockSpec((block, cols), lambda i, s: (i, 0))]
    else:
        out_shape = [jax.ShapeDtypeStruct((model // 2, cols), BF16)] * 2
        out_specs = [pl.BlockSpec((block // 2, cols), lambda i, s: (i, 0))] * 2
    return pl.pallas_call(
        lambda *refs: weight_kernel(*refs, depth=depth, lanes=lanes),
        grid_spec=pltpu.PrefetchScalarGridSpec(
            num_scalar_prefetch=1,
            grid=(model // block,),
            in_specs=[
                pl.BlockSpec((block, total), lambda i, s: (i, 0)),
                whole(own),
                *[whole(g) for g in grads],
                pl.BlockSpec((block, cols), lambda i, s: (i, 0)),
                whole(col),
                whole(vec),
            ],
            out_specs=out_specs + [pl.BlockSpec((8, block), lambda i, s: (0, i))],
            scratch_shapes=[pltpu.VMEM((block, cols), BF16)],
        ),
        out_shape=out_shape + [jax.ShapeDtypeStruct((8, model), F32)],
        compiler_params=params(16),
        cost_estimate=cost(9),
    )(place, xh, own, *grads, w, col, vec)


def norm_back_kernel(x_ref, own_ref, got_ref, gres_ref, vec_ref, out_ref):
    x = x_ref[...].astype(F32)
    cen = x - jnp.mean(x, axis=1, keepdims=True)
    rs = lax.rsqrt(jnp.mean(cen * cen, axis=1, keepdims=True) + EPS)
    xh = cen * rs
    eg = (own_ref[...] + got_ref[...].astype(F32)) * vec_ref[GAIN_ONE]
    out_ref[...] = gres_ref[...] + rs * (
        eg - jnp.mean(eg, axis=1, keepdims=True) - xh * jnp.mean(eg * xh, axis=1, keepdims=True)
    )


def norm_back_call(x, own, got, gres, vec):
    rows, width = x.shape
    tile = pl.BlockSpec((TILE, width), lambda i: (i, 0))
    return pl.pallas_call(
        norm_back_kernel,
        grid=(rows // TILE,),
        in_specs=[tile, tile, tile, tile, pl.BlockSpec(vec.shape, lambda i: (0, 0))],
        out_specs=tile,
        out_shape=jax.ShapeDtypeStruct((rows, width), F32),
        compiler_params=params(56),
        cost_estimate=cost(6),
    )(x, own, got, gres, vec)


def collect_kernel(place_ref, own_ref, far_ref, up_ref, two_ref, one_ref, qkv_ref, down_ref, rest_ref, out_ref):
    width = out_ref.shape[1]
    half = own_ref.shape[1]
    lanes = pl.ds(pl.multiple_of(place_ref[0] * half, PAIR), half)
    sums = own_ref[...] + far_ref[...]
    out_ref[...] = jnp.zeros_like(out_ref)
    for row in range(3):
        out_ref[row : row + 1, lanes] = sums[row : row + 1, :]
    for row in range(up_ref.shape[1] // width):
        out_ref[3 + row : 4 + row, :] = up_ref[:, row * width : (row + 1) * width]
    for row in range(4):
        out_ref[7 + row : 8 + row, :] = two_ref[row : row + 1, :]
    for row in range(2):
        out_ref[11 + row : 12 + row, :] = one_ref[row : row + 1, :]
        out_ref[13 + row : 14 + row, lanes] = sums[3 + row : 4 + row, :]
    total = jnp.zeros((1, 1), F32)
    for ref, scale in ((qkv_ref, 1.0), (down_ref, 1.0), (rest_ref, 0.5)):
        v = ref[...].astype(F32)
        total += scale * jnp.sum(jnp.sum(v * v, axis=0, keepdims=True), axis=1, keepdims=True)
    lane = lax.broadcasted_iota(jnp.int32, (1, width), 1)
    out_ref[15:16, :] = jnp.where(lane == 0, total, 0.0)


def collect_call(place, *arrays):
    width = arrays[3].shape[1]
    whole = lambda a: pl.BlockSpec(a.shape, lambda i, s: (0, 0))
    return pl.pallas_call(
        collect_kernel,
        grid_spec=pltpu.PrefetchScalarGridSpec(
            num_scalar_prefetch=1,
            grid=(1,),
            in_specs=[whole(a) for a in arrays],
            out_specs=pl.BlockSpec((16, width), lambda i, s: (0, 0)),
        ),
        out_shape=jax.ShapeDtypeStruct((16, width), F32),
        compiler_params=params(6),
        cost_estimate=cost(3),
    )(place, *arrays)


def finish_kernel(in_ref, qkv_ref, up_ref, *rest):
    vectors, freq_ref, norm_ref = rest[:-2], rest[-2], rest[-1]
    width = in_ref.shape[1]
    value = in_ref[...]
    for row in range(3):
        qkv_ref[pl.ds(row * width, width)] = value[row]
    for row in range(4):
        up_ref[pl.ds(row * width, width)] = value[3 + row]
    for row in range(6):
        vectors[row][...] = value[7 + row]
    turned = value[13:15]
    turned = jnp.concatenate([turned] * 4, axis=0)
    turned = pltpu.roll(turned, width - HEAD // 2, 1) - turned
    freq_ref[...] = turned
    lane = lax.broadcasted_iota(jnp.int32, (2, width), 1) % HEAD
    square = lambda u: jnp.sum(jnp.sum(u * u, axis=0, keepdims=True), axis=1, keepdims=True)
    freqs = square(jnp.where(lane < HEAD // 2, turned[:2], 0.0))
    main = square(value[:13]) + value[15:16, 0:1]
    at = lax.broadcasted_iota(jnp.int32, (8, PAIR), 1)
    norm_ref[...] = jnp.sqrt(jnp.where(at == 0, main, freqs))


def finish_call(value, hidden):
    width = value.shape[1]
    shapes = [(3 * width,), (hidden,)] + [(width,)] * 6 + [(8, width), (8, PAIR)]
    whole = lambda shape: pl.BlockSpec(shape, lambda: (0,) * len(shape))
    return pl.pallas_call(
        finish_kernel,
        in_specs=[whole(value.shape)],
        out_specs=[whole(shape) for shape in shapes],
        out_shape=[jax.ShapeDtypeStruct(shape, F32) for shape in shapes],
        compiler_params=params(2),
        cost_estimate=cost(2),
    )(value)


def partners(count, mask):
    return [(i, i ^ mask) for i in range(count)]


def chip_groups(count):
    bits = count.bit_length() - 1
    groups = []
    at = 1
    while at < bits:
        size = 1 if at == 1 else min(2, bits - at)
        groups.append((at, size))
        at += size
    return groups


def spot(mask, count):
    at = 0
    scale = 1
    for low, size in chip_groups(count)[::-1]:
        at = at + ((mask >> (low - 1)) & ((1 << size) - 1)) * scale
        scale <<= size
    return at


def gather_parts(held, axis, count, group):
    low, size = group
    return [held] + [lax.ppermute(held, axis, partners(count, m << low)) for m in range(1, 1 << size)]


def gather_stage(held, axis, count, group):
    return jnp.concatenate(gather_parts(held, axis, count, group), axis=0)


def scatter_chips(held, axis, count, groups):
    index = lax.axis_index(axis)
    chips, rows, cols = held.shape
    for low, size in groups:
        span = 1 << size
        blocks = held.reshape((chips // span, span, rows, cols))
        me = (index >> low) & (span - 1)
        sums = lax.dynamic_index_in_dim(blocks, me, 1, False).astype(F32)
        for m in range(1, span):
            send = lax.dynamic_index_in_dim(blocks, me ^ m, 1, False)
            sums = sums + lax.ppermute(send, axis, partners(count, m << low)).astype(F32)
        chips //= span
        held = sums if chips == 1 else sums.astype(BF16)
    return held.reshape(rows, cols) if chips == 1 else held


def sum_over(value, count, held):
    axes = ("seq", "rows")
    bits = count.bit_length()
    at = 0
    while at < bits:
        size = min(2, bits - at)
        if at:
            kept = held[: len(held) if at + size == bits else -1]
            value, *kept = lax.optimization_barrier((value, *kept))
            held = (*kept, *held[len(kept) :])
        got = [lax.ppermute(value, axes, partners(2 * count, m << at)) for m in range(1, 1 << size)]
        value = value + got[0]
        if size == 2:
            value = value + (got[1] + got[2])
        at += size
    return value, held


def after(value, *others):
    return lax.optimization_barrier((value,) + others)[0]


def body(
    patches, lengths, w_qkv, qkv_bias, w_out, out_bias, w_up, up_bias, w_down, down_bias,
    gain_one, shift_one, gain_two, shift_two, rope_freqs, cotangent,
):
    _, rows, width = patches.shape
    count = lax.axis_size("seq")
    index = lax.axis_index("seq")
    side = lax.axis_index("rows")
    flip = [(0, 1), (1, 0)]
    total = 2 * rows
    heads = rope_freqs.shape[1]
    half = width // 2
    hidden = up_bias.shape[0]
    depth = w_out.shape[0]
    deep = w_down.shape[0]
    direct = count == 16
    share = deep // 2
    blocks = hidden // width
    per = rows // TILE
    info = jnp.concatenate([jnp.stack([side, index % 2, index // 2]).astype(jnp.int32), lengths[0]])
    base_own = (side * per)[None].astype(jnp.int32)
    base_far = ((1 - side) * per)[None].astype(jnp.int32)
    vec = jnp.concatenate(
        [qkv_bias, out_bias, down_bias, gain_one, shift_one, gain_two, shift_two, jnp.zeros((7 * width,), BF16)]
    )
    vec = vec.astype(F32).reshape(16, width)
    up_row = up_bias.astype(F32)[None, :]

    x = patches[0]
    cot = cotangent[0]
    if direct:
        packed, own_cols = pack_call(info, w_down, w_out, w_up, w_qkv, share)
    else:
        packed = jnp.concatenate([w_out] + [w_up[:, c : c + width] for c in range(0, hidden, width)], axis=0)
        own_cols = lax.dynamic_index_in_dim(w_qkv.reshape(depth, 3, 2, half), side, 2, False).reshape(depth, 3 * half)
    own_freqs = lax.dynamic_slice_in_dim(rope_freqs, side * (heads // 2), heads // 2, 1)
    lane_freqs = jnp.concatenate([own_freqs, own_freqs], axis=-1).reshape(2, half)
    cos, sin, mq, mk, pos = table_call(info, lane_freqs, total)
    x_other = lax.ppermute(x, "rows", flip)
    core_pairs = partners(count, 1)
    if direct:
        near, far = chip_groups(count)
        down_got = lax.ppermute(
            lax.dynamic_slice_in_dim(w_down[share:], (1 - index % 2) * half, half, 1), "seq", core_pairs
        )
        down = lax.dynamic_slice_in_dim(w_down[share:], index % 2 * half, half, 1)
        down = jnp.where(index % 2 == side, down, down_got)
        qkv_a = gather_stage(own_cols[None], "seq", count, far)
        qkv_a, down, cos, sin, mq, mk, pos, vec, up_row = lax.optimization_barrier(
            (qkv_a, down, cos, sin, mq, mk, pos, vec, up_row)
        )
        down_parts = gather_parts(down[None], "seq", count, far)
        qkv_a = gather_stage(qkv_a, "seq", count, near)
        qkv_b = lax.ppermute(after(qkv_a, x_other), "seq", core_pairs)
        packed = lax.all_gather(packed, "seq", axis=0, tiled=False)
        qkv_a, qkv_b = qkv_a.reshape(-1, 3 * half), qkv_b.reshape(-1, 3 * half)
    else:
        packed = lax.all_gather(packed, "seq", axis=0, tiled=False)
        packed = packed.reshape(count, blocks + 1, depth, width).transpose(1, 0, 2, 3).reshape(blocks + 1, width, width)
        qkv_a = lax.all_gather(own_cols, "seq", axis=0, tiled=True)
        qkv_b = jnp.zeros((8, 3 * half), BF16)

    xh, q, k, v, kaug, kt, vt, w_own, w_turn = qkv_call(
        info, x, x_other, qkv_a, qkv_b, depth if direct else None, vec, cos, sin, mk
    )
    if direct:
        *down_parts, q = lax.optimization_barrier((*down_parts, q))
        down = jnp.concatenate(down_parts, axis=0)
        down_got = lax.ppermute(down, "rows", flip)
    att_far, lse_far = attend_call(base_far, info, q, kaug, vt, mq)
    att_got = lax.ppermute(att_far, "rows", flip)
    if direct:
        down, down_got, att_far = lax.optimization_barrier((down, down_got, att_far))
        down = jnp.stack([down, down_got], axis=0)[None]
        down = gather_stage(down, "seq", count, near)
    att_own, lse_own = attend_call(base_own, info, after(q, att_far), kaug, vt, mq)

    if direct:
        down_a = after(down, att_own)
        down_b = lax.ppermute(down_a, "seq", core_pairs)
    else:
        down_a, down_b = lax.all_gather(w_down, "seq", axis=0, tiled=True), None
    att, res, normed = pre_call(info, att_own, att_got, x, packed, depth, vec)
    hid, gres, do_own, do_send, gwp, gwd_send, gwd_keep, gub, sums_two = ffn_call(
        info, att, res, normed, cot, packed, depth, down_a, down_b, vec, up_row
    )
    do_far = lax.ppermute(do_send, "rows", flip)

    if not direct:
        gwp = gwp.reshape(blocks + 1, count, depth, width).transpose(1, 0, 2, 3)
    shard_p = lax.psum_scatter(gwp.reshape(-1, width), "seq", scatter_dimension=0, tiled=True)

    gwd_got = lax.ppermute(gwd_send, "seq", core_pairs)

    back = (q, k, kaug, kt, v, mq, cos, sin, pos)
    all_pairs = half // PAIR
    gq_own, dk, dv, sums_own = attend_back_call(base_own, info, do_own, att_own, lse_own, *back, 0, all_pairs)
    gwd_got, gq_own, do_far = lax.optimization_barrier((gwd_got, gq_own, do_far))
    gwd = (gwd_keep.astype(F32) + gwd_got.astype(F32)).astype(BF16).reshape(count // 2, 2, deep, half)
    gwd_keep = lax.dynamic_index_in_dim(gwd, side, 1, False)
    gwd_got = lax.ppermute(lax.dynamic_index_in_dim(gwd, 1 - side, 1, False), "rows", flip)

    queries, keys, sums_far, grads, lanes = [], [], [], [], []
    for step, (first, pairs) in enumerate(((0, 3),)):
        lane = first * PAIR
        gq, gk, gv, sums = attend_back_call(
            base_far, info, do_far, att_far, lse_far, *back, first, pairs, held=(dk, dv)
        )
        queries.append((gq, lane))
        keys += [(gk, half + lane), (gv, 2 * half + lane)]
        sums_far.append(sums)
        grads += [gq, gk, gv]
        lanes.append((lane, pairs * PAIR))
    col = (sums_own[:3] + jnp.concatenate(sums_far, axis=1)[:3]).reshape(1, 3 * half)
    part_far = part_call(base_far, queries, keys, w_turn, BF16)
    part_got = lax.ppermute(part_far, "rows", flip)
    shard_got = lax.ppermute(shard_p, "rows", flip)
    gwd_got, xh, part_far = lax.optimization_barrier((gwd_got, xh, part_far))
    gwd = (gwd_keep.astype(F32) + gwd_got.astype(F32)).astype(BF16)
    gwd = scatter_chips(gwd, "seq", count, chip_groups(count)).astype(BF16)
    *gw, sums_one = weight_call(info, xh, gq_own, grads, w_own, col, vec, depth if direct else None, lanes)
    if not direct:
        gw = gw[0].reshape(count // 2, 2, depth, 3 * half)
        gw = [lax.dynamic_index_in_dim(gw, c, 1, False).reshape(-1, 3 * half) for c in (1 - index % 2, index % 2)]
    gw_got = lax.ppermute(gw[0], "seq", core_pairs)
    gw = (gw[1].astype(F32) + gw_got.astype(F32)).astype(BF16).reshape(count // 2, depth, 3 * half)
    gw = after(gw, shard_p)
    shard_own = scatter_chips(gw, "seq", count, chip_groups(count)).astype(BF16)
    shard_far = lax.ppermute(shard_own, "rows", flip)
    own_keys = [(gq_own, 0)]
    part_own = part_call(base_own, own_keys, keys, after(w_turn, sums_one), F32)
    patch_grad = norm_back_call(x, part_own, part_got, gres, vec)

    swaps = []
    for mask in (0, 1):
        swaps.append([(2 * i + r, 2 * (i - i % 2 + r) + ((i % 2) ^ mask)) for i in range(count) for r in range(2)])
    same_half, other_half = (lax.ppermute(after(gwd, shard_got), ("seq", "rows"), p) for p in swaps)
    shard_p = shard_p.astype(F32) + shard_got.astype(F32)
    shard_out = shard_p[:depth]
    shard_up = jnp.concatenate([shard_p[(1 + c) * depth : (2 + c) * depth] for c in range(blocks)], axis=1)
    small = collect_call(info, sums_own, *sums_far, gub, sums_two, sums_one, after(shard_own, patch_grad), gwd, shard_p)
    small, (same_half, other_half, shard_far) = sum_over(small, count, (same_half, other_half, shard_far))
    first = jnp.where(side == 0, shard_own, shard_far).reshape(depth, 3, 1, half)
    second = jnp.where(side == 0, shard_far, shard_own).reshape(depth, 3, 1, half)
    shard_qkv = jnp.concatenate([first, second], axis=2).reshape(depth, 6 * half).astype(F32)

    low = side == 0
    shard_down = jnp.concatenate(
        [jnp.where(low, same_half, other_half), jnp.where(low, other_half, same_half)], axis=1
    ).astype(F32)

    s_qkv, s_up, s_out, s_down, s_gain2, s_shift2, s_gain1, s_shift1, freqs, norms = finish_call(small, hidden)
    freqs = freqs[:2].reshape(2, heads, HEAD)[:, :, : HEAD // 2]
    return (
        hid[None],
        patch_grad[None],
        shard_qkv,
        s_qkv,
        shard_out,
        s_out,
        shard_up,
        s_up,
        shard_down,
        s_down,
        s_gain1,
        s_shift1,
        s_gain2,
        s_shift2,
        freqs,
        norms[0, 0],
        norms[0, 1],
    )


def solution(mesh):
    in_specs = (
        P("seq", "rows", None),
        P("seq", None),
        P("seq", None),
        P(),
        P("seq", None),
        P(),
        P("seq", None),
        P(),
        P("seq", None),
        P(),
        P(),
        P(),
        P(),
        P(),
        P(),
        P("seq", "rows", None),
    )
    out_specs = (
        P("seq", "rows", None),
        P("seq", "rows", None),
        P("seq", None),
        P(),
        P("seq", None),
        P(),
        P("seq", None),
        P(),
        P("seq", None),
        P(),
        P(),
        P(),
        P(),
        P(),
        P(),
        P(),
        P(),
    )
    return jax.shard_map(body, mesh=mesh, in_specs=in_specs, out_specs=out_specs, check_vma=False)
```

```python
import jax
import jax.numpy as jnp
from jax import lax
from jax.experimental import pallas as pl
from jax.experimental.pallas import tpu as pltpu
from jax.sharding import PartitionSpec as P

SIDE_S = 14
SIDE_M = 20
SIDE_L = 24
EPS = 1e-06
NEG = -1e30
HEAD = 64
PAIR = 128
TILE = 256
F32 = jnp.float32
BF16 = jnp.bfloat16
OUT_BIAS, DOWN_BIAS, GAIN_ONE, SHIFT_ONE, GAIN_TWO, SHIFT_TWO = (slice(r, r + 1) for r in range(3, 9))


def cost(us):
    return pl.CostEstimate(flops=int(us * 1150000000), bytes_accessed=10**5, transcendentals=0)


def params(mib):
    return pltpu.CompilerParams(vmem_limit_bytes=mib * 1024 * 1024)


def nn(a, b):
    return lax.dot_general(a, b, (((1,), (0,)), ((), ())), preferred_element_type=F32)


def nt(a, b):
    return lax.dot_general(a, b, (((1,), (1,)), ((), ())), preferred_element_type=F32)


def tn(a, b):
    return lax.dot_general(a, b, (((0,), (0,)), ((), ())), preferred_element_type=F32)


def swap_halves(u):
    width = u.shape[-1]
    lane = lax.broadcasted_iota(jnp.int32, u.shape, 1) % HEAD
    return jnp.where(
        lane < HEAD // 2,
        pltpu.roll(u, width - HEAD // 2, 1),
        pltpu.roll(u, HEAD // 2, 1),
    )


def head_lanes(shape, odd):
    lane = lax.broadcasted_iota(jnp.int32, shape, 1)
    return (lane >= HEAD) if odd else (lane < HEAD)


def tile_bounds(info_ref, tile, total):
    first = tile * TILE
    last = first + TILE - 1
    run = jnp.int32(0)
    low = jnp.int32(-1)
    high = jnp.int32(total)
    for s in range(3, info_ref.shape[0]):
        end = run + info_ref[s]
        low = jnp.where((first >= run) & (first < end), run, low)
        high = jnp.where((last >= run) & (last < end), end, high)
        run = end
    low = jnp.where(low < 0, run, low)
    return lax.div(low, TILE), lax.div(high + (TILE - 1), TILE)


def pack_kernel(info_ref, down_ref, out_ref, up_ref, qkv_ref, packed_ref, cols_ref):
    depth, width = out_ref.shape
    half = width // 2
    share = packed_ref.shape[0] - depth * (1 + up_ref.shape[1] // width)
    packed_ref[:share, :] = down_ref[:share, :]
    packed_ref[share : share + depth, :] = out_ref[...]
    for c in range(up_ref.shape[1] // width):
        at = share + (c + 1) * depth
        packed_ref[at : at + depth, :] = up_ref[:, c * width : (c + 1) * width]
    for i in range(3):
        at = pl.multiple_of(i * width + info_ref[0] * half, PAIR)
        cols_ref[:, i * half : (i + 1) * half] = qkv_ref[:, pl.ds(at, half)]


def pack_call(info, w_down, w_out, w_up, w_qkv, share):
    depth, width = w_out.shape
    whole = lambda r, c: pl.BlockSpec((r, c), lambda i, s: (0, 0))
    length = share + depth * (w_up.shape[1] // width + 1)
    arrays = (w_down, w_out, w_up, w_qkv)
    return pl.pallas_call(
        pack_kernel,
        grid_spec=pltpu.PrefetchScalarGridSpec(
            num_scalar_prefetch=1,
            grid=(1,),
            in_specs=[whole(*a.shape) for a in arrays],
            out_specs=[whole(length, width), whole(depth, 3 * width // 2)],
        ),
        out_shape=[
            jax.ShapeDtypeStruct((length, width), BF16),
            jax.ShapeDtypeStruct((depth, 3 * width // 2), BF16),
        ],
        compiler_params=params(60),
        cost_estimate=cost(2.5),
    )(info, *arrays)


def table_kernel(info_ref, freq_ref, cos_ref, sin_ref, mq_ref, mk_ref, pos_ref):
    step = pl.program_id(0)
    slots = info_ref.shape[0] - 3

    def place(shape):
        at = lax.broadcasted_iota(jnp.int32, shape, 0) + step * TILE
        block = jnp.full(shape, slots, jnp.int32)
        offset = jnp.zeros(shape, jnp.int32)
        side = jnp.ones(shape, F32)
        run = jnp.int32(0)
        for s in range(slots):
            count = info_ref[3 + s]
            inside = (at >= run) & (at < run + count)
            width = jnp.where(count == SIDE_S * SIDE_S, SIDE_S, jnp.where(count == SIDE_M * SIDE_M, SIDE_M, SIDE_L))
            block = jnp.where(inside, s, block)
            offset = jnp.where(inside, at - run, offset)
            side = jnp.where(inside, width.astype(F32), side)
            run = run + count
        offset = offset.astype(F32)
        row = jnp.floor((offset + 0.5) / side)
        return block, row, offset - row * side

    block, row, col = place((TILE, PAIR))
    lane = lax.broadcasted_iota(jnp.int32, (TILE, PAIR), 1)
    slot = lane % HEAD
    same = slot == block
    mk_ref[...] = same.astype(F32).astype(BF16)
    mq_ref[...] = jnp.where(same | (slot > slots), 0.0, NEG).astype(BF16)
    pos_ref[...] = jnp.where(lane == 0, row, jnp.where(lane == 1, col, 0.0))
    half = TILE // 2
    width = cos_ref.shape[1]
    front = lax.broadcasted_iota(jnp.int32, (half, width), 1) % HEAD < HEAD // 2
    both = lambda u: (u[:half, 0:1], u[half:, 0:1])
    row_a, row_b = both(row)
    col_a, col_b = both(col)
    angle = jnp.where(front, row_a, row_b) * freq_ref[0:1, :] + jnp.where(front, col_a, col_b) * freq_ref[1:2, :]
    for ref, value in ((cos_ref, jnp.cos(angle)), (sin_ref, jnp.sin(angle))):
        up = pltpu.roll(value, HEAD // 2, 1)
        down = pltpu.roll(value, width - HEAD // 2, 1)
        sign = -1.0 if ref is sin_ref else 1.0
        ref[:half, :] = jnp.where(front, sign * value, up)
        ref[half:, :] = jnp.where(front, sign * down, value)


def table_call(info, freqs, total):
    width = freqs.shape[1]
    tile = lambda c: pl.BlockSpec((TILE, c), lambda i, s: (i, 0))
    return pl.pallas_call(
        table_kernel,
        grid_spec=pltpu.PrefetchScalarGridSpec(
            num_scalar_prefetch=1,
            grid=(total // TILE,),
            in_specs=[pl.BlockSpec(freqs.shape, lambda i, s: (0, 0))],
            out_specs=[tile(width), tile(width), tile(PAIR), tile(PAIR), tile(PAIR)],
        ),
        out_shape=[
            jax.ShapeDtypeStruct((total, width), F32),
            jax.ShapeDtypeStruct((total, width), F32),
            jax.ShapeDtypeStruct((total, PAIR), BF16),
            jax.ShapeDtypeStruct((total, PAIR), BF16),
            jax.ShapeDtypeStruct((total, PAIR), F32),
        ],
        compiler_params=params(60),
        cost_estimate=cost(9),
    )(info, freqs)


def qkv_kernel(
    place_ref, own_ref, other_ref, wa_ref, wb_ref, vec_ref, cos_ref, sin_ref, mk_ref,
    xh_ref, q_ref, k_ref, v_ref, kaug_ref, kt_ref, vt_ref, w_ref, wt_ref, *, depth,
):
    step = pl.program_id(0)
    half = pl.num_programs(0) // 2
    width = cos_ref.shape[1]

    @pl.when(step == 0)
    def _():
        if depth is None:
            w_ref[...] = wa_ref[...]
        else:
            core = place_ref[1]
            pieces = wa_ref.shape[0] // depth
            for m in range(pieces):
                at = (place_ref[2] ^ m) * (2 * depth)
                held = spot(m, 2 * pieces)
                rows = slice(held * depth, (held + 1) * depth)
                w_ref[pl.ds(pl.multiple_of(at + core * depth, 16), depth), :] = wa_ref[rows, :]
                w_ref[pl.ds(pl.multiple_of(at + (1 - core) * depth, 16), depth), :] = wb_ref[rows, :]
        wt_ref[...] = w_ref[...].T

    mine = (step // half) == place_ref[0]
    x = jnp.where(mine, own_ref[...].astype(F32), other_ref[...].astype(F32))
    mean = jnp.mean(x, axis=1, keepdims=True)
    cen = x - mean
    var = jnp.mean(cen * cen, axis=1, keepdims=True)
    xh = cen * lax.rsqrt(var + EPS)
    xh_ref[...] = xh.astype(BF16).T
    normed = (xh * vec_ref[GAIN_ONE] + vec_ref[SHIFT_ONE]).astype(BF16)
    mid = pl.ds(pl.multiple_of(place_ref[0] * width, PAIR), width)
    bias = jnp.concatenate([vec_ref[i : i + 1, mid] for i in range(3)], axis=1)
    proj = nn(normed, w_ref[...]) + bias
    c = cos_ref[...]
    s = sin_ref[...]
    q = proj[:, :width]
    k = proj[:, width : 2 * width]
    q = (q * c + swap_halves(q) * s).astype(BF16)
    k = (k * c + swap_halves(k) * s).astype(BF16)
    v = proj[:, 2 * width :].astype(BF16)
    q_ref[...] = (q.astype(F32) * 0.125).astype(BF16)
    k_ref[...] = k
    v_ref[...] = v
    kt_ref[...] = k.T
    vt_ref[...] = v.T
    mk = mk_ref[...]
    for h in range(width // HEAD):
        pair = h // 2
        kp = k[:, pair * PAIR : (pair + 1) * PAIR]
        kaug_ref[h] = jnp.where(head_lanes(kp.shape, h % 2), kp, mk)


def qkv_call(place, own, other, wa, wb, depth, vec, cos, sin, mk):
    rows, width = own.shape
    total = 2 * rows
    cols = wa.shape[1]
    third = cols // 3
    heads = third // HEAD
    per = rows // TILE
    last = per - 1
    whole = lambda i, s: (0, 0)
    tile = lambda c: pl.BlockSpec((TILE, c), lambda i, s: (i, 0))
    return pl.pallas_call(
        lambda *refs: qkv_kernel(*refs, depth=depth),
        grid_spec=pltpu.PrefetchScalarGridSpec(
            num_scalar_prefetch=1,
            grid=(total // TILE,),
            in_specs=[
                pl.BlockSpec((TILE, width), lambda i, s: (jnp.clip(i - per * s[0], 0, last), 0)),
                pl.BlockSpec((TILE, width), lambda i, s: (jnp.clip(i - per * (1 - s[0]), 0, last), 0)),
                pl.BlockSpec(wa.shape, whole),
                pl.BlockSpec(wb.shape, whole),
                pl.BlockSpec(vec.shape, whole),
                tile(third),
                tile(third),
                tile(PAIR),
            ],
            out_specs=[
                pl.BlockSpec((width, TILE), lambda i, s: (0, i)),
                tile(third),
                tile(third),
                tile(third),
                pl.BlockSpec((heads, TILE, PAIR), lambda i, s: (0, i, 0)),
                pl.BlockSpec((third, TILE), lambda i, s: (0, i)),
                pl.BlockSpec((third, TILE), lambda i, s: (0, i)),
                pl.BlockSpec((width, cols), whole),
                pl.BlockSpec((cols, width), whole),
            ],
        ),
        out_shape=[
            jax.ShapeDtypeStruct((width, total), BF16),
            jax.ShapeDtypeStruct((total, third), BF16),
            jax.ShapeDtypeStruct((total, third), BF16),
            jax.ShapeDtypeStruct((total, third), BF16),
            jax.ShapeDtypeStruct((heads, total, PAIR), BF16),
            jax.ShapeDtypeStruct((third, total), BF16),
            jax.ShapeDtypeStruct((third, total), BF16),
            jax.ShapeDtypeStruct((width, cols), BF16),
            jax.ShapeDtypeStruct((cols, width), BF16),
        ],
        compiler_params=params(60),
        cost_estimate=cost(1),
    )(place, own, other, wa, wb, vec, cos, sin, mk)


def attend_kernel(base_ref, info_ref, q_ref, kaug_ref, vt_ref, mq_ref, out_ref, lse_ref, qaug, scores, acc):
    step = pl.program_id(0) + base_ref[0]
    width = out_ref.shape[1]
    heads = width // HEAD
    mq = mq_ref[...]
    for h in range(heads):
        pair = h // 2
        q = q_ref[:, pair * PAIR : (pair + 1) * PAIR]
        qaug[h] = jnp.where(head_lanes(q.shape, h % 2), q, mq)
    lo, hi = tile_bounds(info_ref, step, kaug_ref.shape[1])

    def first(kt, best):
        keys = pl.ds(pl.multiple_of(kt * TILE, TILE), TILE)
        out = []
        for h in range(heads):
            s = nt(kaug_ref[h, keys, :], qaug[h])
            scores[h, keys, :] = s
            out.append(jnp.maximum(best[h], jnp.max(s.reshape(TILE // 8, 8, TILE), axis=0)))
        return tuple(out)

    best = lax.fori_loop(lo, hi, first, tuple(jnp.full((8, TILE), -jnp.inf, F32) for _ in range(heads)))
    best = [jnp.max(b, axis=0, keepdims=True) for b in best]
    acc[...] = jnp.zeros_like(acc)

    def second(kt, sums):
        keys = pl.ds(pl.multiple_of(kt * TILE, TILE), TILE)
        out = []
        for h in range(heads):
            p = jnp.exp(scores[h, keys, :] - best[h])
            out.append(sums[h] + jnp.sum(p.reshape(TILE // 8, 8, TILE), axis=0))
            own = slice(h * HEAD, (h + 1) * HEAD)
            acc[own, :] += nn(vt_ref[own, keys], p.astype(BF16))
        return tuple(out)

    sums = lax.fori_loop(lo, hi, second, tuple(jnp.zeros((8, TILE), F32) for _ in range(heads)))
    lses = []
    outs = []
    for h in range(heads):
        tot = jnp.sum(sums[h], axis=0, keepdims=True)
        outs.append(acc[h * HEAD : (h + 1) * HEAD, :] / tot)
        lses.append(best[h] + jnp.log(tot))
    lses += [jnp.zeros_like(lses[0])] * (8 - heads)
    lse_ref[...] = jnp.concatenate(lses, axis=0)
    out_ref[...] = jnp.concatenate(outs, axis=0).T.astype(BF16)


def attend_call(base, info, q, kaug, vt, mq):
    total, width = q.shape
    heads = width // HEAD
    rows = total // 2
    whole = lambda i, b, s: (0, 0)
    return pl.pallas_call(
        attend_kernel,
        grid_spec=pltpu.PrefetchScalarGridSpec(
            num_scalar_prefetch=2,
            grid=(rows // TILE,),
            in_specs=[
                pl.BlockSpec((TILE, width), lambda i, b, s: (b[0] + i, 0)),
                pl.BlockSpec(kaug.shape, lambda i, b, s: (0, 0, 0)),
                pl.BlockSpec(vt.shape, whole),
                pl.BlockSpec((TILE, PAIR), lambda i, b, s: (b[0] + i, 0)),
            ],
            out_specs=[
                pl.BlockSpec((TILE, width), lambda i, b, s: (i, 0)),
                pl.BlockSpec((8, TILE), lambda i, b, s: (0, i)),
            ],
            scratch_shapes=[
                pltpu.VMEM((heads, TILE, PAIR), BF16),
                pltpu.VMEM((heads, total, TILE), F32),
                pltpu.VMEM((width, TILE), F32),
            ],
        ),
        out_shape=[
            jax.ShapeDtypeStruct((rows, width), BF16),
            jax.ShapeDtypeStruct((8, rows), F32),
        ],
        compiler_params=params(60),
        cost_estimate=cost(4),
    )(base, info, q, kaug, vt, mq)


def phi_parts(x):
    cdf = 0.5 * (1.0 + lax.erf(x * 0.7071067811865476))
    pdf = jnp.exp(-0.5 * x * x) * 0.3989422804014327
    return cdf, pdf


def pre_kernel(place_ref, mine_ref, got_ref, x_ref, wo_ref, vec_ref, att_ref, res_ref, normed_ref):
    width = x_ref.shape[1]
    half = width // 2
    lanes = lambda at: pl.ds(pl.multiple_of(at * half, PAIR), half)
    att_ref[:, lanes(place_ref[0])] = mine_ref[...]
    att_ref[:, lanes(1 - place_ref[0])] = got_ref[...]
    wo = wo_ref[...].reshape(width, width)
    r = x_ref[...].astype(F32) + (nn(att_ref[...], wo) + vec_ref[OUT_BIAS])
    res_ref[...] = r
    cen = r - jnp.mean(r, axis=1, keepdims=True)
    var = jnp.mean(cen * cen, axis=1, keepdims=True)
    normed_ref[...] = (cen * lax.rsqrt(var + EPS) * vec_ref[GAIN_TWO] + vec_ref[SHIFT_TWO]).astype(BF16)


def pack_spec(packed, depth, width, at):
    if packed.shape[1] == width:
        return pl.BlockSpec((1, width, width), lambda j, s: (at(j), 0, 0))
    skip = packed.shape[1] % (5 * depth) // depth
    return pl.BlockSpec((packed.shape[0], depth, width), lambda j, s: (0, skip + at(j), 0))


def pre_call(place, mine, got, x, packed, depth, vec):
    rows, width = x.shape
    tile = lambda c: pl.BlockSpec((TILE, c), lambda j, s: (j, 0))
    return pl.pallas_call(
        pre_kernel,
        grid_spec=pltpu.PrefetchScalarGridSpec(
            num_scalar_prefetch=1,
            grid=(rows // TILE,),
            in_specs=[
                tile(width // 2),
                tile(width // 2),
                tile(width),
                pack_spec(packed, depth, width, lambda j: 0),
                pl.BlockSpec(vec.shape, lambda j, s: (0, 0)),
            ],
            out_specs=[tile(width), tile(width), tile(width)],
        ),
        out_shape=[
            jax.ShapeDtypeStruct((rows, width), BF16),
            jax.ShapeDtypeStruct((rows, width), F32),
            jax.ShapeDtypeStruct((rows, width), BF16),
        ],
        compiler_params=params(60),
        cost_estimate=cost(30),
    )(place, mine, got, x, packed, vec)


def ffn_kernel(
    place_ref, att_ref, res_ref, normed_ref, cot_ref, wo_ref, wu_ref, *rest, chips,
):
    many = 2 * chips + 1
    down = rest[:many]
    (
        vec_ref, ub_ref,
        hid_ref, gres_ref, gown_ref, gfar_ref, gwp_ref, send_ref, keep_ref, gub_ref, sums_ref,
        acc, gacc, act, gup, wd_s,
    ) = rest[many:]
    step = pl.program_id(0)
    steps = pl.num_programs(0) - 1
    rows, width = res_ref.shape
    half = width // 2
    core = place_ref[1]
    chunks = [pl.ds(r, TILE) for r in range(0, rows, TILE)]
    lanes = lambda at: pl.ds(pl.multiple_of(at * half, PAIR), half)

    @pl.when(step == 0)
    def _():
        acc[...] = jnp.zeros_like(acc)
        gacc[...] = jnp.zeros_like(gacc)

    @pl.when(step < steps)
    def _():
        if chips:
            deep = width // (2 * chips)
            share = down[-1].shape[1]
            for t in range(2 * chips):
                wd_s[t * deep : t * deep + share, :] = down[-1][t]
            for t in range(chips):
                for r in (0, 1):
                    at = 2 * t * deep + (place_ref[0] ^ r) * deep + share
                    spot_rows = pl.ds(pl.multiple_of(at, 16), deep - share)
                    wd_s[spot_rows, lanes(core)] = down[t][r]
                    wd_s[spot_rows, lanes(1 - core)] = down[chips + t][r]
            wd_ref = wd_s
        else:
            wd_ref = down[0]
        bias_sum = jnp.zeros((1, ub_ref.shape[1]), F32)
        wu = wu_ref[...].reshape(width, width)
        for ch in chunks:
            up = nn(normed_ref[ch, :], wu) + ub_ref[...]
            cdf, pdf = phi_parts(up)
            a = (up * cdf).astype(BF16)
            act[ch, :] = a
            g = (nt(cot_ref[ch, :], wd_ref[...]) * (cdf + up * pdf)).astype(BF16)
            gup[ch, :] = g
            bias_sum += jnp.sum(g.astype(F32), axis=0, keepdims=True)
            acc[ch, :] += nn(a, wd_ref[...])
            gacc[ch, :] += nt(g, wu)
        gub_ref[...] = bias_sum
        send_ref[...] = tn(act[...], cot_ref[:, lanes(1 - core)]).astype(BF16)
        keep_ref[...] = tn(act[...], cot_ref[:, lanes(core)]).astype(BF16)
        gwp_ref[...] = tn(normed_ref[...], gup[...]).astype(BF16).reshape(gwp_ref.shape)

    @pl.when(step == steps)
    def _():
        zero = jnp.zeros((1, width), F32)
        s_out, s_down, s_gain, s_shift = zero, zero, zero, zero
        gain = vec_ref[GAIN_TWO]
        wo = wo_ref[...].reshape(width, width)
        for ch in chunks:
            r = res_ref[ch, :]
            hid_ref[ch, :] = (r + acc[ch, :] + vec_ref[DOWN_BIAS]).astype(BF16)
            cen = r - jnp.mean(r, axis=1, keepdims=True)
            rs = lax.rsqrt(jnp.mean(cen * cen, axis=1, keepdims=True) + EPS)
            xh = cen * rs
            e = gacc[ch, :]
            eg = e * gain
            cot = cot_ref[ch, :].astype(F32)
            g = cot + rs * (
                eg - jnp.mean(eg, axis=1, keepdims=True) - xh * jnp.mean(eg * xh, axis=1, keepdims=True)
            )
            gres_ref[ch, :] = g
            gb = g.astype(BF16)
            act[ch, :] = gb
            gup[ch, :] = nt(gb, wo).astype(BF16)
            gown_ref[ch, :] = gup[ch, lanes(place_ref[0])]
            gfar_ref[ch, :] = gup[ch, lanes(1 - place_ref[0])]
            s_out += jnp.sum(gb.astype(F32), axis=0, keepdims=True)
            s_down += jnp.sum(cot, axis=0, keepdims=True)
            s_gain += jnp.sum(e * xh, axis=0, keepdims=True)
            s_shift += jnp.sum(e, axis=0, keepdims=True)
        gwp_ref[...] = tn(att_ref[...], act[...]).astype(BF16).reshape(gwp_ref.shape)
        sums_ref[...] = jnp.concatenate([s_out, s_down, s_gain, s_shift] + [zero] * 4, axis=0)


def ffn_call(place, att, res, normed, cot, packed, depth, down_a, down_b, vec, ub):
    rows, width = res.shape
    half = width // 2
    hidden = ub.shape[1]
    steps = hidden // width
    last = steps - 1
    whole = lambda j, s: (0, 0)
    held = pl.BlockSpec(memory_space=pltpu.VMEM)
    one = lambda r, c: pl.BlockSpec((r, c), whole)
    pack = lambda at: pack_spec(packed, depth, width, at)
    clip = lambda j: jnp.minimum(j, last)
    if down_b is None:
        chips = 0
        down = (down_a,)
        down_specs = [pl.BlockSpec((width, width), lambda j, s: (clip(j), 0))]
        grads = jax.ShapeDtypeStruct(packed.shape, BF16)
    else:
        count = packed.shape[0]
        share = packed.shape[1] - (steps + 1) * depth
        piece_rows = down_a.shape[3]
        chips = width * count // (2 * hidden)
        grads = jax.ShapeDtypeStruct((count, (steps + 1) * depth, width), BF16)

        def piece(t):
            def at(j, s):
                chip = (clip(j) * chips + t) ^ s[2]
                return (chip & 1, 0, chip >> 1, 0, 0)

            return pl.BlockSpec((pl.squeezed, 2, pl.squeezed, piece_rows, half), at)

        down_specs = [piece(t) for t in range(chips)] * 2
        down_specs.append(pl.BlockSpec((2 * chips, share, width), lambda j, s: (clip(j), 0, 0)))
        down = (down_a,) * chips + (down_b,) * chips + (packed,)
    return pl.pallas_call(
        lambda *refs: ffn_kernel(*refs, chips=chips),
        grid_spec=pltpu.PrefetchScalarGridSpec(
            num_scalar_prefetch=1,
            grid=(steps + 1,),
            in_specs=[
                one(rows, width),
                one(rows, width),
                one(rows, width),
                one(rows, width),
                pack(lambda j: 0),
                pack(lambda j: 1 + clip(j)),
                *down_specs,
                one(*vec.shape),
                pl.BlockSpec((1, width), lambda j, s: (0, clip(j))),
            ],
            out_specs=[
                one(rows, width),
                one(rows, width),
                one(rows, half),
                one(rows, half),
                pack_spec(grads, depth, width, lambda j: jnp.where(j < steps, 1 + j, 0)),
                pl.BlockSpec((width, half), lambda j, s: (clip(j), 0)),
                pl.BlockSpec((width, half), lambda j, s: (clip(j), 0)),
                pl.BlockSpec((1, width), lambda j, s: (0, clip(j))),
                one(8, width),
            ],
            scratch_shapes=[
                pltpu.VMEM((rows, width), F32),
                pltpu.VMEM((rows, width), F32),
                pltpu.VMEM((rows, width), BF16),
                pltpu.VMEM((rows, width), BF16),
                pltpu.VMEM((width, width), BF16),
            ],
        ),
        out_shape=[
            jax.ShapeDtypeStruct((rows, width), BF16),
            jax.ShapeDtypeStruct((rows, width), F32),
            jax.ShapeDtypeStruct((rows, half), BF16),
            jax.ShapeDtypeStruct((rows, half), BF16),
            grads,
            jax.ShapeDtypeStruct((hidden, half), BF16),
            jax.ShapeDtypeStruct((hidden, half), BF16),
            jax.ShapeDtypeStruct((1, hidden), F32),
            jax.ShapeDtypeStruct((8, width), F32),
        ],
        compiler_params=params(60),
        cost_estimate=cost(38),
    )(place, att, res, normed, cot, packed, packed, *down, vec, ub)


def attend_back_kernel(base_ref, info_ref, do_ref, o_ref, lse_ref, q_ref, kaug_ref, kt_ref, v_ref, mq_ref, cos_ref, sin_ref, pos_ref, *rest, final, head):
    if final:
        late, dk_in, dv_in, gq_ref, gk_ref, gv_ref, sums_ref = rest[:4], *rest[4:10]
        qaug, qm, dom, dqt, delta, s_scr, dp_scr, p_scr, ds_scr, dk, dv, *kept, sems = rest[10:]
        k_ref, cos_all, sin_all, pos_all = kept
        copies = [pltpu.make_async_copy(a, b, sems.at[i]) for i, (a, b) in enumerate(zip(late, kept))]
    else:
        gq_ref, dk, dv, sums_ref = rest[:4]
        qaug, qm, dom, dqt, delta, s_scr, dp_scr, p_scr, ds_scr = rest[4:]
    step = pl.program_id(0)
    tile = step + base_ref[0]
    width = do_ref.shape[1]
    heads = width // HEAD
    pairs = heads // 2
    total = v_ref.shape[0]

    @pl.when(step == 0)
    def _():
        if final:
            for copy in copies:
                copy.start()
            dk[...] = dk_in[...]
            dv[...] = dv_in[...]
        else:
            dk[...] = jnp.zeros_like(dk)
            dv[...] = jnp.zeros_like(dv)
        sums_ref[...] = jnp.zeros_like(sums_ref)

    mq = mq_ref[...]
    for h in range(heads):
        pair = slice((h // 2) * PAIR, (h // 2 + 1) * PAIR)
        q = q_ref[:, pair]
        lanes = head_lanes(q.shape, h % 2)
        qaug[h] = jnp.where(lanes, q, mq)
        qm[h * TILE : (h + 1) * TILE, :] = jnp.where(lanes, q, jnp.zeros_like(q))
        dom[h * TILE : (h + 1) * TILE, :] = jnp.where(lanes, do_ref[:, pair], jnp.zeros_like(q))
    inner = do_ref[...].astype(F32) * o_ref[...].astype(F32)
    pick = (
        lax.broadcasted_iota(jnp.int32, (8, width), 1) // HEAD == lax.broadcasted_iota(jnp.int32, (8, width), 0)
    ).astype(F32)
    delta[...] = lax.dot_general(
        pick, inner, (((1,), (1,)), ((), ())), precision=lax.Precision.HIGHEST, preferred_element_type=F32
    )
    dqt[...] = jnp.zeros_like(dqt)

    def body(kt, carry):
        keys = pl.ds(pl.multiple_of(kt * TILE, TILE), TILE)
        for h in range(heads):
            s_scr[h] = nt(kaug_ref[h, keys, :], qaug[h])
            dp_scr[h] = nt(v_ref[keys, (h // 2) * PAIR : (h // 2 + 1) * PAIR], dom[h * TILE : (h + 1) * TILE, :])
        for h in range(heads):
            at = slice((h % 2) * TILE, (h % 2 + 1) * TILE)
            p = jnp.exp(s_scr[h] - lse_ref[head + h : head + h + 1, :])
            p_scr[h // 2, :, at] = p.astype(BF16)
            ds_scr[h // 2, :, at] = (p * (dp_scr[h] - delta[h : h + 1, :])).astype(BF16)
        for pr in range(pairs):
            pair = slice(pr * PAIR, (pr + 1) * PAIR)
            both = slice(2 * pr * TILE, 2 * (pr + 1) * TILE)
            dv[keys, pair] += nn(p_scr[pr], dom[both, :])
            dk[keys, pair] += nn(ds_scr[pr], qm[both, :])
            for e in (0, 1):
                own = slice((2 * pr + e) * HEAD, (2 * pr + e + 1) * HEAD)
                dqt[own, :] += nn(kt_ref[own, keys], ds_scr[pr, :, e * TILE : (e + 1) * TILE])
        return carry

    lo, hi = tile_bounds(info_ref, tile, total)
    lax.fori_loop(lo, hi, body, 0)

    def unrotate(u, c, s):
        return (u * c - swap_halves(u) * s).astype(BF16)

    def freq_sum(u, rot, pos):
        w = u * swap_halves(rot)
        sums_ref[3:4, :] += jnp.sum(w * pos[:, 0:1], axis=0, keepdims=True)
        sums_ref[4:5, :] += jnp.sum(w * pos[:, 1:2], axis=0, keepdims=True)

    dq = dqt[...].T * 0.125
    freq_sum(dq, q_ref[...].astype(F32) * 8.0, pos_ref[...])
    gq = unrotate(dq, cos_ref[...], sin_ref[...])
    gq_ref[...] = gq
    sums_ref[0:1, :] += jnp.sum(gq.astype(F32), axis=0, keepdims=True)

    if final:

        @pl.when(step == pl.num_programs(0) - 1)
        def _():
            for copy in copies:
                copy.wait()
            for t in range(total // TILE):
                at = pl.ds(t * TILE, TILE)
                u = dk[at, :]
                freq_sum(u, k_ref[at, :].astype(F32), pos_all[at, :])
                gk = unrotate(u, cos_all[at, :], sin_all[at, :])
                gv = dv[at, :].astype(BF16)
                gk_ref[at, :] = gk
                gv_ref[at, :] = gv
                sums_ref[1:2, :] += jnp.sum(gk.astype(F32), axis=0, keepdims=True)
                sums_ref[2:3, :] += jnp.sum(gv.astype(F32), axis=0, keepdims=True)


def attend_back_call(base, info, do, o, lse, q, k, kaug, kt, v, mq, cos, sin, pos, first, pairs, held=None):
    total = q.shape[0]
    width = pairs * PAIR
    heads = 2 * pairs
    spot = first // pairs
    rows = total // 2
    final = held is not None
    here = lambda c: pl.BlockSpec((TILE, c), lambda i, b, s: (i, spot))
    there = lambda c: pl.BlockSpec((TILE, c), lambda i, b, s: (b[0] + i, spot))
    flat = lambda c: pl.BlockSpec((TILE, c), lambda i, b, s: (b[0] + i, 0))
    tall = pl.BlockSpec((total, width), lambda i, b, s: (0, spot))
    held_in = pl.BlockSpec(memory_space=pltpu.VMEM)
    whole = lambda a: pl.BlockSpec(a.shape, lambda i, b, s: (0,) * len(a.shape))
    args = [do, o, lse, q, kaug, kt, v, mq, cos, sin, pos]
    in_specs = [
        here(width), here(width), pl.BlockSpec((8, TILE), lambda i, b, s: (0, i)), there(width),
        pl.BlockSpec((heads, total, PAIR), lambda i, b, s: (spot, 0, 0)),
        pl.BlockSpec((width, total), lambda i, b, s: (spot, 0)),
        tall, flat(PAIR), there(width), there(width), flat(PAIR),
    ]
    big = jax.ShapeDtypeStruct((total, width), F32)
    low = jax.ShapeDtypeStruct((total, width), BF16)
    sums = jax.ShapeDtypeStruct((8, width), F32)
    scratch = [
        pltpu.VMEM((heads, TILE, PAIR), BF16),
        pltpu.VMEM((heads * TILE, PAIR), BF16),
        pltpu.VMEM((heads * TILE, PAIR), BF16),
        pltpu.VMEM((width, TILE), F32),
        pltpu.VMEM((8, TILE), F32),
        pltpu.VMEM((heads, TILE, TILE), F32),
        pltpu.VMEM((heads, TILE, TILE), F32),
        pltpu.VMEM((pairs, TILE, 2 * TILE), BF16),
        pltpu.VMEM((pairs, TILE, 2 * TILE), BF16),
    ]
    if final:
        args += [k, cos, sin, pos, *held]
        in_specs += [pl.BlockSpec(memory_space=pl.ANY)] * 4 + [held_in, held_in]
        grads = [low, low]
        scratch += [pltpu.VMEM((total, width), F32), pltpu.VMEM((total, width), F32)]
        scratch += [pltpu.VMEM(a.shape, a.dtype) for a in (k, cos, sin, pos)]
        scratch.append(pltpu.SemaphoreType.DMA((4,)))
    else:
        grads = [big, big]
    return pl.pallas_call(
        lambda *refs: attend_back_kernel(*refs, final=final, head=2 * first),
        grid_spec=pltpu.PrefetchScalarGridSpec(
            num_scalar_prefetch=2,
            grid=(rows // TILE,),
            in_specs=in_specs,
            out_specs=[pl.BlockSpec((TILE, width), lambda i, b, s: (i, 0)), held_in, held_in, whole(sums)],
            scratch_shapes=scratch,
        ),
        out_shape=[jax.ShapeDtypeStruct((rows, width), BF16), *grads, sums],
        compiler_params=params(50),
        cost_estimate=cost(10 * pairs),
    )(base, info, *args)


def part_kernel(base_ref, *refs, lanes):
    w_ref, out_ref = refs[-2:]
    total = jnp.zeros(out_ref.shape, F32)
    for ref, at in zip(refs, lanes):
        total += nn(ref[...], w_ref[at : at + ref.shape[1], :])
    out_ref[...] = total.astype(out_ref.dtype)


def part_call(base, queries, keys, w, kind):
    rows = queries[0][0].shape[0]
    here = lambda c: pl.BlockSpec((TILE, c), lambda i, b: (i, 0))
    there = lambda c: pl.BlockSpec((TILE, c), lambda i, b: (b[0] + i, 0))
    arrays = [a for a, _ in queries + keys]
    lanes = [at for _, at in queries + keys]
    return pl.pallas_call(
        lambda *refs: part_kernel(*refs, lanes=lanes),
        grid_spec=pltpu.PrefetchScalarGridSpec(
            num_scalar_prefetch=1,
            grid=(rows // TILE,),
            in_specs=[here(a.shape[1]) for a, _ in queries]
            + [there(a.shape[1]) for a, _ in keys]
            + [pl.BlockSpec(w.shape, lambda i, b: (0, 0))],
            out_specs=pl.BlockSpec((TILE, w.shape[1]), lambda i, b: (i, 0)),
        ),
        out_shape=jax.ShapeDtypeStruct((rows, w.shape[1]), kind),
        compiler_params=params(10),
        cost_estimate=cost(5.6),
    )(base, *arrays, w)


def weight_kernel(place_ref, xh_ref, own_ref, *rest, depth, lanes):
    keys = 3 * len(lanes)
    grads = rest[:keys]
    w_ref, col_ref, vec_ref = rest[keys : keys + 3]
    *outs, spare = rest[keys + 3 :]
    sums_ref = outs[-1]
    third = w_ref.shape[1] // 3
    rows = own_ref.shape[0]
    block = w_ref.shape[0]
    flat = vec_ref[:, pl.ds(pl.multiple_of(pl.program_id(0) * block, PAIR), block)].T
    gain = flat[:, GAIN_ONE]
    shift = flat[:, SHIFT_ONE]
    total = jnp.zeros(gain.shape, F32)
    bias = jnp.zeros(gain.shape, F32)
    half = lambda at: pl.ds(pl.multiple_of(at * rows, TILE), rows)
    for g, (lane, width) in enumerate(lanes):
        for i in range(3):
            ref = grads[3 * g + i]
            at = slice(i * third + lane, i * third + lane + width)
            if i:
                x = nn(xh_ref[...], ref[...])
            else:
                own = own_ref[:, lane : lane + width]
                x = nn(xh_ref[:, half(place_ref[0])], own) + nn(xh_ref[:, half(1 - place_ref[0])], ref[...])
            w = w_ref[:, at].astype(F32)
            col = col_ref[:, at]
            total += jnp.sum(x * w, axis=1, keepdims=True)
            bias += jnp.sum(w * col, axis=1, keepdims=True)
            spare[:, at] = (x * gain + shift * col).astype(BF16)
    lane = lax.broadcasted_iota(jnp.int32, (block, PAIR), 1)
    both = jnp.where(lane == 0, total, jnp.where(lane == 1, bias, 0.0))
    sums_ref[...] = both.T[:8, :]
    if depth is None:
        outs[0][...] = spare[...]
        return
    core = place_ref[1]
    for t in range(spare.shape[0] // (2 * depth)):
        at = 2 * t * depth
        rows = slice(t * depth, (t + 1) * depth)
        outs[0][rows, :] = spare[pl.ds(pl.multiple_of(at + (1 - core) * depth, 16), depth), :]
        outs[1][rows, :] = spare[pl.ds(pl.multiple_of(at + core * depth, 16), depth), :]


def weight_call(place, xh, own, grads, w, col, vec, depth, lanes):
    model, total = xh.shape
    cols = w.shape[1]
    block = model // 2
    whole = lambda a: pl.BlockSpec(a.shape, lambda i, s: (0, 0))
    if depth is None:
        out_shape = [jax.ShapeDtypeStruct((model, cols), BF16)]
        out_specs = [pl.BlockSpec((block, cols), lambda i, s: (i, 0))]
    else:
        out_shape = [jax.ShapeDtypeStruct((model // 2, cols), BF16)] * 2
        out_specs = [pl.BlockSpec((block // 2, cols), lambda i, s: (i, 0))] * 2
    return pl.pallas_call(
        lambda *refs: weight_kernel(*refs, depth=depth, lanes=lanes),
        grid_spec=pltpu.PrefetchScalarGridSpec(
            num_scalar_prefetch=1,
            grid=(model // block,),
            in_specs=[
                pl.BlockSpec((block, total), lambda i, s: (i, 0)),
                whole(own),
                *[whole(g) for g in grads],
                pl.BlockSpec((block, cols), lambda i, s: (i, 0)),
                whole(col),
                whole(vec),
            ],
            out_specs=out_specs + [pl.BlockSpec((8, block), lambda i, s: (0, i))],
            scratch_shapes=[pltpu.VMEM((block, cols), BF16)],
        ),
        out_shape=out_shape + [jax.ShapeDtypeStruct((8, model), F32)],
        compiler_params=params(16),
        cost_estimate=cost(9),
    )(place, xh, own, *grads, w, col, vec)


def norm_back_kernel(x_ref, own_ref, got_ref, gres_ref, vec_ref, out_ref):
    x = x_ref[...].astype(F32)
    cen = x - jnp.mean(x, axis=1, keepdims=True)
    rs = lax.rsqrt(jnp.mean(cen * cen, axis=1, keepdims=True) + EPS)
    xh = cen * rs
    eg = (own_ref[...] + got_ref[...].astype(F32)) * vec_ref[GAIN_ONE]
    out_ref[...] = gres_ref[...] + rs * (
        eg - jnp.mean(eg, axis=1, keepdims=True) - xh * jnp.mean(eg * xh, axis=1, keepdims=True)
    )


def norm_back_call(x, own, got, gres, vec):
    rows, width = x.shape
    tile = pl.BlockSpec((TILE, width), lambda i: (i, 0))
    return pl.pallas_call(
        norm_back_kernel,
        grid=(rows // TILE,),
        in_specs=[tile, tile, tile, tile, pl.BlockSpec(vec.shape, lambda i: (0, 0))],
        out_specs=tile,
        out_shape=jax.ShapeDtypeStruct((rows, width), F32),
        compiler_params=params(56),
        cost_estimate=cost(6),
    )(x, own, got, gres, vec)


def collect_kernel(place_ref, own_ref, far_ref, up_ref, two_ref, one_ref, qkv_ref, down_ref, rest_ref, out_ref):
    width = out_ref.shape[1]
    half = own_ref.shape[1]
    lanes = pl.ds(pl.multiple_of(place_ref[0] * half, PAIR), half)
    sums = own_ref[...] + far_ref[...]
    out_ref[...] = jnp.zeros_like(out_ref)
    for row in range(3):
        out_ref[row : row + 1, lanes] = sums[row : row + 1, :]
    for row in range(up_ref.shape[1] // width):
        out_ref[3 + row : 4 + row, :] = up_ref[:, row * width : (row + 1) * width]
    for row in range(4):
        out_ref[7 + row : 8 + row, :] = two_ref[row : row + 1, :]
    for row in range(2):
        out_ref[11 + row : 12 + row, :] = one_ref[row : row + 1, :]
        out_ref[13 + row : 14 + row, lanes] = sums[3 + row : 4 + row, :]
    total = jnp.zeros((1, 1), F32)
    for ref, scale in ((qkv_ref, 1.0), (down_ref, 1.0), (rest_ref, 0.5)):
        v = ref[...].astype(F32)
        total += scale * jnp.sum(jnp.sum(v * v, axis=0, keepdims=True), axis=1, keepdims=True)
    lane = lax.broadcasted_iota(jnp.int32, (1, width), 1)
    out_ref[15:16, :] = jnp.where(lane == 0, total, 0.0)


def collect_call(place, *arrays):
    width = arrays[3].shape[1]
    whole = lambda a: pl.BlockSpec(a.shape, lambda i, s: (0, 0))
    return pl.pallas_call(
        collect_kernel,
        grid_spec=pltpu.PrefetchScalarGridSpec(
            num_scalar_prefetch=1,
            grid=(1,),
            in_specs=[whole(a) for a in arrays],
            out_specs=pl.BlockSpec((16, width), lambda i, s: (0, 0)),
        ),
        out_shape=jax.ShapeDtypeStruct((16, width), F32),
        compiler_params=params(6),
        cost_estimate=cost(3),
    )(place, *arrays)


def finish_kernel(in_ref, qkv_ref, up_ref, *rest):
    vectors, freq_ref, norm_ref = rest[:-2], rest[-2], rest[-1]
    width = in_ref.shape[1]
    value = in_ref[...]
    for row in range(3):
        qkv_ref[pl.ds(row * width, width)] = value[row]
    for row in range(4):
        up_ref[pl.ds(row * width, width)] = value[3 + row]
    for row in range(6):
        vectors[row][...] = value[7 + row]
    turned = value[13:15]
    turned = jnp.concatenate([turned] * 4, axis=0)
    turned = pltpu.roll(turned, width - HEAD // 2, 1) - turned
    freq_ref[...] = turned
    lane = lax.broadcasted_iota(jnp.int32, (2, width), 1) % HEAD
    square = lambda u: jnp.sum(jnp.sum(u * u, axis=0, keepdims=True), axis=1, keepdims=True)
    freqs = square(jnp.where(lane < HEAD // 2, turned[:2], 0.0))
    main = square(value[:13]) + value[15:16, 0:1]
    at = lax.broadcasted_iota(jnp.int32, (8, PAIR), 1)
    norm_ref[...] = jnp.sqrt(jnp.where(at == 0, main, freqs))


def finish_call(value, hidden):
    width = value.shape[1]
    shapes = [(3 * width,), (hidden,)] + [(width,)] * 6 + [(8, width), (8, PAIR)]
    whole = lambda shape: pl.BlockSpec(shape, lambda: (0,) * len(shape))
    return pl.pallas_call(
        finish_kernel,
        in_specs=[whole(value.shape)],
        out_specs=[whole(shape) for shape in shapes],
        out_shape=[jax.ShapeDtypeStruct(shape, F32) for shape in shapes],
        compiler_params=params(2),
        cost_estimate=cost(2),
    )(value)


def partners(count, mask):
    return [(i, i ^ mask) for i in range(count)]


def chip_groups(count):
    bits = count.bit_length() - 1
    groups = []
    at = 1
    while at < bits:
        size = 1 if at == 1 else min(2, bits - at)
        groups.append((at, size))
        at += size
    return groups


def spot(mask, count):
    at = 0
    scale = 1
    for low, size in chip_groups(count)[::-1]:
        at = at + ((mask >> (low - 1)) & ((1 << size) - 1)) * scale
        scale <<= size
    return at


def gather_parts(held, axis, count, group):
    low, size = group
    return [held] + [lax.ppermute(held, axis, partners(count, m << low)) for m in range(1, 1 << size)]


def gather_stage(held, axis, count, group):
    return jnp.concatenate(gather_parts(held, axis, count, group), axis=0)


def scatter_chips(held, axis, count, groups):
    index = lax.axis_index(axis)
    chips, rows, cols = held.shape
    for low, size in groups:
        span = 1 << size
        blocks = held.reshape((chips // span, span, rows, cols))
        me = (index >> low) & (span - 1)
        sums = lax.dynamic_index_in_dim(blocks, me, 1, False).astype(F32)
        for m in range(1, span):
            send = lax.dynamic_index_in_dim(blocks, me ^ m, 1, False)
            sums = sums + lax.ppermute(send, axis, partners(count, m << low)).astype(F32)
        chips //= span
        held = sums if chips == 1 else sums.astype(BF16)
    return held.reshape(rows, cols) if chips == 1 else held


def sum_over(value, count, held):
    axes = ("seq", "rows")
    bits = count.bit_length()
    at = 0
    while at < bits:
        size = min(2, bits - at)
        if at:
            kept = held[: len(held) if at + size == bits else -1]
            value, *kept = lax.optimization_barrier((value, *kept))
            held = (*kept, *held[len(kept) :])
        got = [lax.ppermute(value, axes, partners(2 * count, m << at)) for m in range(1, 1 << size)]
        value = value + got[0]
        if size == 2:
            value = value + (got[1] + got[2])
        at += size
    return value, held


def after(value, *others):
    return lax.optimization_barrier((value,) + others)[0]


def body(
    patches, lengths, w_qkv, qkv_bias, w_out, out_bias, w_up, up_bias, w_down, down_bias,
    gain_one, shift_one, gain_two, shift_two, rope_freqs, cotangent,
):
    _, rows, width = patches.shape
    count = lax.axis_size("seq")
    index = lax.axis_index("seq")
    side = lax.axis_index("rows")
    flip = [(0, 1), (1, 0)]
    total = 2 * rows
    heads = rope_freqs.shape[1]
    half = width // 2
    hidden = up_bias.shape[0]
    depth = w_out.shape[0]
    deep = w_down.shape[0]
    direct = count == 16
    share = deep // 2
    blocks = hidden // width
    per = rows // TILE
    info = jnp.concatenate([jnp.stack([side, index % 2, index // 2]).astype(jnp.int32), lengths[0]])
    base_own = (side * per)[None].astype(jnp.int32)
    base_far = ((1 - side) * per)[None].astype(jnp.int32)
    vec = jnp.concatenate(
        [qkv_bias, out_bias, down_bias, gain_one, shift_one, gain_two, shift_two, jnp.zeros((7 * width,), BF16)]
    )
    vec = vec.astype(F32).reshape(16, width)
    up_row = up_bias.astype(F32)[None, :]

    x = patches[0]
    cot = cotangent[0]
    if direct:
        packed, own_cols = pack_call(info, w_down, w_out, w_up, w_qkv, share)
    else:
        packed = jnp.concatenate([w_out] + [w_up[:, c : c + width] for c in range(0, hidden, width)], axis=0)
        own_cols = lax.dynamic_index_in_dim(w_qkv.reshape(depth, 3, 2, half), side, 2, False).reshape(depth, 3 * half)
    own_freqs = lax.dynamic_slice_in_dim(rope_freqs, side * (heads // 2), heads // 2, 1)
    lane_freqs = jnp.concatenate([own_freqs, own_freqs], axis=-1).reshape(2, half)
    cos, sin, mq, mk, pos = table_call(info, lane_freqs, total)
    x_other = lax.ppermute(x, "rows", flip)
    core_pairs = partners(count, 1)
    if direct:
        near, far = chip_groups(count)
        down_got = lax.ppermute(
            lax.dynamic_slice_in_dim(w_down[share:], (1 - index % 2) * half, half, 1), "seq", core_pairs
        )
        down = lax.dynamic_slice_in_dim(w_down[share:], index % 2 * half, half, 1)
        down = jnp.where(index % 2 == side, down, down_got)
        qkv_a = gather_stage(own_cols[None], "seq", count, far)
        qkv_a, down, cos, sin, mq, mk, pos, vec, up_row = lax.optimization_barrier(
            (qkv_a, down, cos, sin, mq, mk, pos, vec, up_row)
        )
        down_parts = gather_parts(down[None], "seq", count, far)
        qkv_a = gather_stage(qkv_a, "seq", count, near)
        qkv_b = lax.ppermute(after(qkv_a, x_other), "seq", core_pairs)
        packed = lax.all_gather(packed, "seq", axis=0, tiled=False)
        qkv_a, qkv_b = qkv_a.reshape(-1, 3 * half), qkv_b.reshape(-1, 3 * half)
    else:
        packed = lax.all_gather(packed, "seq", axis=0, tiled=False)
        packed = packed.reshape(count, blocks + 1, depth, width).transpose(1, 0, 2, 3).reshape(blocks + 1, width, width)
        qkv_a = lax.all_gather(own_cols, "seq", axis=0, tiled=True)
        qkv_b = jnp.zeros((8, 3 * half), BF16)

    xh, q, k, v, kaug, kt, vt, w_own, w_turn = qkv_call(
        info, x, x_other, qkv_a, qkv_b, depth if direct else None, vec, cos, sin, mk
    )
    if direct:
        *down_parts, q = lax.optimization_barrier((*down_parts, q))
        down = jnp.concatenate(down_parts, axis=0)
        down_got = lax.ppermute(down, "rows", flip)
    att_far, lse_far = attend_call(base_far, info, q, kaug, vt, mq)
    att_got = lax.ppermute(att_far, "rows", flip)
    if direct:
        down, down_got, att_far = lax.optimization_barrier((down, down_got, att_far))
        down = jnp.stack([down, down_got], axis=0)[None]
        down = gather_stage(down, "seq", count, near)
    att_own, lse_own = attend_call(base_own, info, after(q, att_far), kaug, vt, mq)

    if direct:
        down_a = after(down, att_own)
        down_b = lax.ppermute(down_a, "seq", core_pairs)
    else:
        down_a, down_b = lax.all_gather(w_down, "seq", axis=0, tiled=True), None
    att, res, normed = pre_call(info, att_own, att_got, x, packed, depth, vec)
    hid, gres, do_own, do_send, gwp, gwd_send, gwd_keep, gub, sums_two = ffn_call(
        info, att, res, normed, cot, packed, depth, down_a, down_b, vec, up_row
    )
    do_far = lax.ppermute(do_send, "rows", flip)

    if not direct:
        gwp = gwp.reshape(blocks + 1, count, depth, width).transpose(1, 0, 2, 3)
    shard_p = lax.psum_scatter(gwp.reshape(-1, width), "seq", scatter_dimension=0, tiled=True)

    gwd_got = lax.ppermute(gwd_send, "seq", core_pairs)

    back = (q, k, kaug, kt, v, mq, cos, sin, pos)
    all_pairs = half // PAIR
    gq_own, dk, dv, sums_own = attend_back_call(base_own, info, do_own, att_own, lse_own, *back, 0, all_pairs)
    gwd_got, gq_own, do_far = lax.optimization_barrier((gwd_got, gq_own, do_far))
    gwd = (gwd_keep.astype(F32) + gwd_got.astype(F32)).astype(BF16).reshape(count // 2, 2, deep, half)
    gwd_keep = lax.dynamic_index_in_dim(gwd, side, 1, False)
    gwd_got = lax.ppermute(lax.dynamic_index_in_dim(gwd, 1 - side, 1, False), "rows", flip)

    queries, keys, sums_far, grads, lanes = [], [], [], [], []
    for step, (first, pairs) in enumerate(((0, 3),)):
        lane = first * PAIR
        gq, gk, gv, sums = attend_back_call(
            base_far, info, do_far, att_far, lse_far, *back, first, pairs, held=(dk, dv)
        )
        queries.append((gq, lane))
        keys += [(gk, half + lane), (gv, 2 * half + lane)]
        sums_far.append(sums)
        grads += [gq, gk, gv]
        lanes.append((lane, pairs * PAIR))
    col = (sums_own[:3] + jnp.concatenate(sums_far, axis=1)[:3]).reshape(1, 3 * half)
    part_far = part_call(base_far, queries, keys, w_turn, BF16)
    part_got = lax.ppermute(part_far, "rows", flip)
    shard_got = lax.ppermute(shard_p, "rows", flip)
    gwd_got, xh, part_far = lax.optimization_barrier((gwd_got, xh, part_far))
    gwd = (gwd_keep.astype(F32) + gwd_got.astype(F32)).astype(BF16)
    gwd = scatter_chips(gwd, "seq", count, chip_groups(count)).astype(BF16)
    *gw, sums_one = weight_call(info, xh, gq_own, grads, w_own, col, vec, depth if direct else None, lanes)
    if not direct:
        gw = gw[0].reshape(count // 2, 2, depth, 3 * half)
        gw = [lax.dynamic_index_in_dim(gw, c, 1, False).reshape(-1, 3 * half) for c in (1 - index % 2, index % 2)]
    gw_got = lax.ppermute(gw[0], "seq", core_pairs)
    gw = (gw[1].astype(F32) + gw_got.astype(F32)).astype(BF16).reshape(count // 2, depth, 3 * half)
    gw = after(gw, shard_p)
    shard_own = scatter_chips(gw, "seq", count, chip_groups(count)).astype(BF16)
    shard_far = lax.ppermute(shard_own, "rows", flip)
    own_keys = [(gq_own, 0)]
    part_own = part_call(base_own, own_keys, keys, after(w_turn, sums_one), F32)
    patch_grad = norm_back_call(x, part_own, part_got, gres, vec)

    swaps = []
    for mask in (0, 1):
        swaps.append([(2 * i + r, 2 * (i - i % 2 + r) + ((i % 2) ^ mask)) for i in range(count) for r in range(2)])
    same_half, other_half = (lax.ppermute(after(gwd, shard_got), ("seq", "rows"), p) for p in swaps)
    shard_p = shard_p.astype(F32) + shard_got.astype(F32)
    shard_out = shard_p[:depth]
    shard_up = jnp.concatenate([shard_p[(1 + c) * depth : (2 + c) * depth] for c in range(blocks)], axis=1)
    small = collect_call(info, sums_own, *sums_far, gub, sums_two, sums_one, after(shard_own, patch_grad), gwd, shard_p)
    small, (same_half, other_half, shard_far) = sum_over(small, count, (same_half, other_half, shard_far))
    first = jnp.where(side == 0, shard_own, shard_far).reshape(depth, 3, 1, half)
    second = jnp.where(side == 0, shard_far, shard_own).reshape(depth, 3, 1, half)
    shard_qkv = jnp.concatenate([first, second], axis=2).reshape(depth, 6 * half).astype(F32)

    low = side == 0
    shard_down = jnp.concatenate(
        [jnp.where(low, same_half, other_half), jnp.where(low, other_half, same_half)], axis=1
    ).astype(F32)

    s_qkv, s_up, s_out, s_down, s_gain2, s_shift2, s_gain1, s_shift1, freqs, norms = finish_call(small, hidden)
    freqs = freqs[:2].reshape(2, heads, HEAD)[:, :, : HEAD // 2]
    return (
        hid[None],
        patch_grad[None],
        shard_qkv,
        s_qkv,
        shard_out,
        s_out,
        shard_up,
        s_up,
        shard_down,
        s_down,
        s_gain1,
        s_shift1,
        s_gain2,
        s_shift2,
        freqs,
        norms[0, 0],
        norms[0, 1],
    )


def solution(mesh):
    in_specs = (
        P("seq", "rows", None),
        P("seq", None),
        P("seq", None),
        P(),
        P("seq", None),
        P(),
        P("seq", None),
        P(),
        P("seq", None),
        P(),
        P(),
        P(),
        P(),
        P(),
        P(),
        P("seq", "rows", None),
    )
    out_specs = (
        P("seq", "rows", None),
        P("seq", "rows", None),
        P("seq", None),
        P(),
        P("seq", None),
        P(),
        P("seq", None),
        P(),
        P("seq", None),
        P(),
        P(),
        P(),
        P(),
        P(),
        P(),
        P(),
        P(),
    )
    return jax.shard_map(body, mesh=mesh, in_specs=in_specs, out_specs=out_specs, check_vma=False)
```
